128 devices in a mesh: shard: 128 (over z, x, y, core).
Axes of the slice: x: 4, y: 4, z: 4, core: 2. Of those that a mesh axis runs over, the one named last changes fastest.
Arguments:
- embeddings: bfloat16 [2048, 128, 1280], P('shard'), may hold values from -6 to 6
- lengths: int32 [2048], P('shard'), may hold values from 16 to 128
- requests: int32 [128, 128], P('shard'), may hold values from -1 to 15, as said below
- query_local: int32 [128, 128], P('shard'), may hold values from 0 to 15
Outputs:
- local_best: float32 [2048, 128], P('shard')
- cross_best: float32 [2048, 128], P('shard')
The draws below stay inside these ranges and needn't reach their ends.
Inputs may be any that keep to these rules, and one draw needn't show every extreme that they name: requests[d, o] is -1 where cluster d lists no partner in cluster o, else a protein index within cluster o; requests[d, d] is -1; the number of listed partners differs from cluster to cluster.
All inputs are finite; a program needn't handle non-finite values.
Results may differ from the reference program's by a relative error of at most 0.0003.
Values may be sent and summed in bfloat16 or wider, within the bound.
No kernel may reach another device: no remote copies, remote signals or barrier semaphores. Data moves between devices by JAX's collectives and lax.ppermute only.
A program may use at most 256 MiB of HBM per device.

```python
import jax
import jax.numpy as jnp
from jax import lax

E = 1280
L = 128
P_DEV = 16
PEERS = 128
PROTEINS = 2048


def draw_requests(key, part):
    key = jax.random.fold_in(key, 11)
    key_rate, key_roll, key_pick = jax.random.split(key, 3)
    listing_rate = jax.random.randint(key_rate, (PEERS, 1), 0, 6)
    rotation_value = jax.random.randint(key_roll, (PEERS, PEERS), 0, 8)
    partner_pick = jax.random.randint(key_pick, (PEERS, PEERS), 0, P_DEV)
    diagonal = jnp.arange(PEERS)[:, None] == jnp.arange(PEERS)[None, :]
    chosen = (rotation_value < listing_rate) & jnp.logical_not(diagonal)
    return jnp.where(chosen, partner_pick, -1).astype(jnp.int32)


def plant(values, stream_key, least, top_value):
    longest = values.shape.index(max(values.shape))
    spots = []
    for shift in (0, 1):
        where = [jax.random.randint(jax.random.fold_in(stream_key, axis), (), 0, length) for axis, length in enumerate(values.shape)]
        where[longest] = (where[longest] + shift) % values.shape[longest]
        spots.append(tuple(where))
    return values.at[spots[0]].set(least).at[spots[1]].set(top_value)


def block_scale(stream_key, dims, cuts, smallest, largest):
    factor_of = 1.0
    for position, blocks in cuts:
        steps = jax.random.uniform(jax.random.fold_in(jax.random.fold_in(stream_key, 6), position), (blocks,), jnp.float32, smallest / len(cuts), largest / len(cuts))
        factor_of = factor_of * jnp.repeat(jnp.exp(steps), dims[position] // blocks).reshape((-1,) + (1,) * (len(dims) - 1 - position))
    return factor_of


def noise(rng, shape, deviation, bound, pieces=(), kind=jnp.bfloat16):
    loudness = block_scale(rng, shape, pieces, -0.22, 0.18) if pieces else 1.0
    values = jax.random.normal(rng, shape, jnp.float32) * deviation * loudness
    return jnp.minimum(jnp.maximum(values, -bound), bound).astype(kind)


def setup_inputs(seed: int = 0) -> dict:
    keys = jax.random.split(jax.random.key(seed), 5)
    embeddings = noise(keys[0], (PROTEINS, L, E), 1.0, 6.0, ((0, 128),))
    lengths = plant(jax.random.randint(keys[1], (PROTEINS,), L // 8, L + 1), jax.random.fold_in(keys[1], 1), L // 8, L).astype(jnp.int32)
    requests = draw_requests(jax.random.fold_in(keys[4], 71), 0)
    query_local = plant(jax.random.randint(keys[3], (PEERS, PEERS), 0, P_DEV), jax.random.fold_in(keys[3], 1), 0, P_DEV - 1).astype(jnp.int32)
    return {"embeddings": embeddings, "lengths": lengths, "requests": requests, "query_local": query_local}


lowest = -1e+30

def centred(score_matrix, row_validity_mask, col_mask):
    row_count = lax.optimization_barrier(jnp.sum(row_validity_mask, -1))
    col_count = lax.optimization_barrier(jnp.sum(col_mask, -1))
    row_mean = lax.optimization_barrier(jnp.sum(score_matrix * col_mask[..., None, :], -1)) / col_count[..., None]
    col_mean = lax.optimization_barrier(jnp.sum(score_matrix * row_validity_mask[..., :, None], -2)) / row_count[..., None]
    grand_mean = lax.optimization_barrier(jnp.sum(row_mean * row_validity_mask, -1)) / row_count
    return score_matrix - row_mean[..., :, None] - col_mean[..., None, :] + grand_mean[..., None, None]

def residue_mask(lengths, slots):
    return (jnp.arange(slots)[None, :] < lengths[:, None]).astype(jnp.float32)

def reference(embeddings, lengths, requests, query_local):
    slots = embeddings.shape[1]
    width = embeddings.shape[2]
    inverse_square_root = 1.0 / jnp.sqrt(jnp.float32(width))
    masks = residue_mask(lengths, slots)

    def one_cluster(cluster):
        start = (cluster * P_DEV).astype(jnp.int32)
        block_rows = lax.dynamic_slice_in_dim(embeddings, start, P_DEV, 0).astype(jnp.float32)
        block_mask = lax.dynamic_slice_in_dim(masks, start, P_DEV, 0)
        score_matrix = jnp.einsum('bie,qje->bqij', block_rows, block_rows) * inverse_square_root
        cent = centred(score_matrix, block_mask[:, None, :], block_mask[None, :, :])
        row_max = lax.optimization_barrier(jnp.max(jnp.where(block_mask[None, :, None, :] > 0, cent, lowest), -1))
        self_pair = jnp.arange(P_DEV)[:, None] == jnp.arange(P_DEV)[None, :]
        row_max = jnp.where(self_pair[:, :, None], lowest, row_max)
        best_match = lax.optimization_barrier(jnp.max(row_max, 1))
        return jnp.where(block_mask > 0, best_match, 0.0)
    local_best = lax.map(one_cluster, jnp.arange(PEERS)).reshape(PROTEINS, slots)
    owner_ids = jnp.arange(PEERS)

    def one_device(device):
        wanted = requests[device]
        query_pick = query_local[device]
        is_live = wanted >= 0
        query_ids = device * P_DEV + query_pick
        partner_ids = owner_ids * P_DEV + jnp.clip(wanted, 0)
        query_embedding = embeddings[query_ids].astype(jnp.float32)
        partner_embedding = embeddings[partner_ids].astype(jnp.float32)
        query_mask = masks[query_ids]
        partner_mask = masks[partner_ids]
        score_matrix = jnp.einsum('dzp,dwp->dzw', query_embedding, partner_embedding) * inverse_square_root
        cent = centred(score_matrix, query_mask, partner_mask)
        row_side = lax.optimization_barrier(jnp.max(jnp.where(partner_mask[:, None, :] > 0, cent, lowest), -1))
        col_side = lax.optimization_barrier(jnp.max(jnp.where(query_mask[:, :, None] > 0, cent, lowest), -2))
        row_side = jnp.where(is_live[:, None], row_side, lowest)
        col_side = jnp.where(is_live[:, None], col_side, lowest)
        return (row_side, col_side, query_ids.astype(jnp.int32), partner_ids.astype(jnp.int32))
    row_side, col_side, query_ids, partner_ids = lax.map(one_device, jnp.arange(PEERS))
    best = jnp.full((PROTEINS, slots), lowest, jnp.float32)
    best = best.at[query_ids.reshape(-1)].max(row_side.reshape(-1, slots))
    best = best.at[partner_ids.reshape(-1)].max(col_side.reshape(-1, slots))
    cross_best = jnp.where((masks > 0) & (best > -1e+29), best, 0.0)
    return (local_best, cross_best)
```

```python
import functools

import jax
import jax.numpy as jnp
from jax import lax
from jax.experimental import pallas as pl
from jax.experimental.pallas import tpu as pltpu
from jax.sharding import PartitionSpec as P

lowest = -1e30
N = 128
GR = 8
C1 = 2

R_F1ROW, R_F1COL, R_F2ROW, R_F2COL, R_SEND, R_SENDM, R_GIN, R_LIN, R_OWN, R_LEFT, R_GOUT = range(11)


def swap_rows(x, s):
    return jnp.where((s & 1) == 0, pltpu.roll(x, N - 1, 0), pltpu.roll(x, 1, 0))


def skew(x, by, axis, sign):
    for b in range(7):
        shift = (1 << b) if sign > 0 else N - (1 << b)
        x = jnp.where(((by >> b) & 1) == 1, pltpu.roll(x, shift, axis), x)
    return x


def route_kernel(c2, me_ref, req_ref, q_ref, lens_ref, lens_t_ref, tab_ref, tmp_ref):
    s = lax.broadcasted_iota(jnp.int32, (N, N), 0)
    r = lax.broadcasted_iota(jnp.int32, (N, N), 1)
    req = req_ref[...]
    q = q_ref[...]
    live = (req >= 0).astype(jnp.int32)
    req = jnp.maximum(req, 0)
    la = jnp.zeros((N, N), jnp.int32)
    lb = jnp.zeros((N, N), jnp.int32)
    for p in range(16):
        la = jnp.where(q == p, lens_ref[:, p : p + 1], la)
        lb = jnp.where(req == p, lens_t_ref[p : p + 1, :], lb)
    la = la * live
    lb = lb * live
    live_t = live.T
    both = live + live_t
    w_col = jnp.sum(both, axis=1, keepdims=True)
    w_row = jnp.sum(both, axis=0, keepdims=True)
    diff = ((lb + 15) >> 4) - ((la + 15) >> 4)
    score = (
        100 * (diff + diff.T)
        + (live - live_t) * (w_col - w_row)
        + jnp.where(((s + r) & 1) == 0, 25, -25)
    )
    lister_gets = score < 0
    lin = jnp.where(lister_gets, lb.T, la)
    psend = jnp.where(lister_gets, req.T, q)
    pown = jnp.where(lister_gets, q.T, req)
    m_tot = (lin + 15) >> 4

    diag = s == r
    m_sw = swap_rows(m_tot, s)
    free = jnp.where(diag, 0, C1)
    n_own = jnp.minimum(m_tot, free)
    rem = m_tot - n_own
    rem_sw = swap_rows(rem, s)
    n_mate = jnp.minimum(rem_sw, free - n_own)
    g_mate = m_sw - rem_sw
    w1 = free - n_own - n_mate
    for k in range(C1):
        own_code = (r << 3) | k
        mate_code = (1 << 10) | (r << 3) | (g_mate + k - n_own)
        code = jnp.where(k < n_own, own_code, jnp.where(k < n_own + n_mate, mate_code, 0))
        w1 = w1 | (code << (2 + 11 * k))
    rem = swap_rows(rem_sw - n_mate, s)
    free = jnp.where(diag, 0, c2)
    g_own = m_tot - rem
    n_own = jnp.minimum(rem, free)
    rem = rem - n_own
    rem_sw = swap_rows(rem, s)
    n_mate = jnp.minimum(rem_sw, free - n_own)
    g_mate = m_sw - rem_sw
    w2 = free - n_own - n_mate
    for k in range(c2):
        own_code = (g_own + k) << 2
        mate_code = 1 | ((g_mate + k - n_own) << 2)
        code = jnp.where(k < n_own, own_code, jnp.where(k < n_own + n_mate, mate_code, 0))
        w2 = w2 | (code << (2 + 14 * k))
    rem = swap_rows(rem_sw - n_mate, s)

    w1 = skew(w1, s, 1, -1)
    w2 = skew(w2, r, 0, -1)

    def sweep(flag, total, w1, w2, rem):
        def step(w1, w2, rem):
            f1 = w1 & 3
            f2 = w2 & 3
            ok = jnp.minimum(jnp.minimum(f1, f2), rem) > 0
            g = total - rem
            code1 = (flag << 10) | (r << 3) | g
            code2 = 2 | (g << 2) | ((C1 - f1) << 5) | (s << 6) | (flag << 13)
            new1 = (w1 - 1) | (code1 << jnp.where(f1 == C1, 2, 13))
            new2 = (w2 - 1) | (code2 << jnp.where(f2 == c2, 2, 16))
            w1 = jnp.where(ok, new1, w1)
            w2 = jnp.where(ok, new2, w2)
            rem = jnp.where(ok, rem - 1, rem)
            return pltpu.roll(w1, N - 1, 1), pltpu.roll(w2, N - 1, 0), rem

        def body(c):
            i, left, w1, w2, rem = c
            for _ in range(8):
                w1, w2, rem = step(w1, w2, rem)
            return i + 1, jnp.sum(rem), w1, w2, rem

        i, left, w1, w2, rem = lax.while_loop(
            lambda c: (c[0] < N // 8) & (c[1] > 0),
            body,
            (jnp.int32(0), jnp.sum(rem), w1, w2, rem),
        )
        return 8 * i, left, w1, w2, rem

    t_a, _, w1, w2, rem = sweep(0, m_tot, w1, w2, rem)
    t_b, left, w1, w2, rem = sweep(1, m_sw, w1, w2, swap_rows(rem, s))
    turn = (t_a + t_b) & (N - 1)
    w1 = skew(pltpu.roll(w1, turn, 1), s, 1, 1)
    w2 = skew(pltpu.roll(w2, turn, 0), r, 0, 1)

    me = me_ref[0]
    mate = me ^ 1

    def put(row, x, at):
        tmp_ref[...] = x
        tab_ref[row : row + 1, :] = tmp_ref[pl.ds(at, 1), :]

    put(R_F1ROW, w1, me)
    put(R_F1COL, w1.T, me)
    put(R_F2ROW, w2, me)
    put(R_F2COL, w2.T, me)
    put(R_SEND, psend, me)
    put(R_SENDM, psend, mate)
    put(R_GIN, m_tot.T, me)
    put(R_LIN, lin.T, me)
    put(R_OWN, pown.T, me)
    tab_ref[R_LEFT : R_LEFT + 1, :] = jnp.full((1, N), left, jnp.int32)
    put(R_GOUT, m_tot, me)
    tab_ref[R_GOUT + 1 :, :] = jnp.zeros((16 - R_GOUT - 1, N), jnp.int32)


def route(c2, me, req, q, lens):
    return pl.pallas_call(
        functools.partial(route_kernel, c2),
        out_shape=jax.ShapeDtypeStruct((16, N), jnp.int32),
        in_specs=[pl.BlockSpec(memory_space=pltpu.SMEM)] + [pl.BlockSpec(memory_space=pltpu.VMEM)] * 4,
        out_specs=pl.BlockSpec(memory_space=pltpu.VMEM),
        scratch_shapes=[pltpu.VMEM((N, N), jnp.int32)],
        compiler_params=pltpu.CompilerParams(vmem_limit_bytes=32 << 20),
        name=f"route{c2}",
    )(me, req, q, lens, lens.T)


def pack1_kernel(tab_ref, own_ref, mate_ref, out_ref, sem):
    def body(m, _):
        w = tab_ref[R_F1ROW, m]
        for k in range(C1):
            code = w >> (2 + 11 * k)
            g = code & 7
            to = (code >> 3) & (N - 1)
            from_mate = (code >> 10) & 1

            @pl.when(from_mate == 0)
            def _():
                at = tab_ref[R_SEND, to] * GR + g
                pltpu.make_async_copy(own_ref.at[at], out_ref.at[m * C1 + k], sem).start()

            @pl.when(from_mate == 1)
            def _():
                at = tab_ref[R_SENDM, to] * GR + g
                pltpu.make_async_copy(mate_ref.at[at], out_ref.at[m * C1 + k], sem).start()

        return 0

    lax.fori_loop(0, N, body, 0, unroll=4)
    pltpu.make_async_copy(out_ref, out_ref, sem).wait()


def pack2_kernel(c2, tab_ref, own_ref, mate_ref, got_ref, out_ref, sem):
    def body(to, _):
        w = tab_ref[R_F2ROW, to]
        for k in range(c2):
            code = w >> (2 + 14 * k)
            kind = code & 3
            g = (code >> 2) & 7
            slot = ((code >> 6) & (N - 1)) * C1 + ((code >> 5) & 1)
            dst = out_ref.at[to * c2 + k]

            @pl.when(kind == 0)
            def _():
                pltpu.make_async_copy(own_ref.at[tab_ref[R_SEND, to] * GR + g], dst, sem).start()

            @pl.when(kind == 1)
            def _():
                pltpu.make_async_copy(mate_ref.at[tab_ref[R_SENDM, to] * GR + g], dst, sem).start()

            @pl.when(kind >= 2)
            def _():
                pltpu.make_async_copy(got_ref.at[slot], dst, sem).start()

        return 0

    lax.fori_loop(0, N, body, 0, unroll=4)
    pltpu.make_async_copy(out_ref, out_ref, sem).wait()


def pack_whole_kernel(tab_ref, own_ref, out_ref, sem):
    def body(m, _):
        at = tab_ref[R_SEND, m] * GR
        pltpu.make_async_copy(own_ref.at[pl.ds(at, GR)], out_ref.at[pl.ds(m * GR, GR)], sem).start()
        return 0

    lax.fori_loop(0, N, body, 0)
    pltpu.make_async_copy(out_ref, out_ref, sem).wait()


def pack(kernel, slots, tab, *arrays):
    return pl.pallas_call(
        kernel,
        out_shape=jax.ShapeDtypeStruct((slots,) + arrays[0].shape[1:], arrays[0].dtype),
        in_specs=[pl.BlockSpec(memory_space=pltpu.SMEM)]
        + [pl.BlockSpec(memory_space=pl.ANY)] * len(arrays),
        out_specs=pl.BlockSpec(memory_space=pl.ANY),
        scratch_shapes=[pltpu.SemaphoreType.DMA],
    )(tab, *arrays)


def place_kernel(c2, me_ref, tab_ref, loc_ref):
    me = me_ref[0]

    def body(s, count):
        if c2 == 0:
            for g in range(GR):
                loc_ref[s * GR + g] = s * GR + g
        else:
            w = tab_ref[R_F1COL, s]
            filled = C1 - (w & 3)
            for k in range(C1):
                code = w >> (2 + 11 * k)

                @pl.when((k < filled) & (((code >> 3) & (N - 1)) == me))
                def _():
                    loc_ref[(s ^ ((code >> 10) & 1)) * GR + (code & 7)] = s * C1 + k

            w = tab_ref[R_F2COL, s]
            filled = c2 - (w & 3)
            for k in range(c2):
                code = w >> (2 + 14 * k)
                kind = code & 3
                via = ((code >> 6) & (N - 1)) ^ ((code >> 13) & 1)
                origin = jnp.where(kind >= 2, via, s ^ (kind & 1))

                @pl.when((k < filled) & (s != me))
                def _():
                    loc_ref[origin * GR + ((code >> 2) & 7)] = C1 * N + s * c2 + k

        is_live = tab_ref[R_GIN, s] > 0

        @pl.when(is_live)
        def _():
            loc_ref[N * GR + count] = s

        return count + is_live.astype(jnp.int32)

    loc_ref[N * GR + N] = lax.fori_loop(0, N, body, jnp.int32(0))


def place(c2, me, tab):
    return pl.pallas_call(
        functools.partial(place_kernel, c2),
        out_shape=jax.ShapeDtypeStruct((N * GR + N + 128,), jnp.int32),
        in_specs=[pl.BlockSpec(memory_space=pltpu.SMEM)] * 2,
        out_specs=pl.BlockSpec(memory_space=pltpu.SMEM),
    )(me, tab)


def match_kernel(n1, tab_ref, loc_ref, lens_ref, own_ref, got1_ref, got2_ref, best_ref, ret_ref, buf, sem):
    scale = 1.0 / jnp.sqrt(jnp.float32(own_ref.shape[2]))
    best_ref[...] = jnp.full(best_ref.shape, lowest, jnp.float32)
    ret_ref[...] = jnp.full(ret_ref.shape, lowest, jnp.float32)
    count = loc_ref[N * GR + N]

    def granules(i, act):
        s = loc_ref[N * GR + i]
        slot = i & 1
        for g in range(GR):

            @pl.when(g < tab_ref[R_GIN, s])
            def _():
                at = loc_ref[s * GR + g]

                @pl.when(at < n1)
                def _():
                    act(pltpu.make_async_copy(got1_ref.at[at], buf.at[slot, g], sem.at[slot, g]))

                @pl.when(at >= n1)
                def _():
                    act(pltpu.make_async_copy(got2_ref.at[at - n1], buf.at[slot, g], sem.at[slot, g]))

    @pl.when(count > 0)
    def _():
        granules(0, lambda c: c.start())

    row = lax.broadcasted_iota(jnp.int32, (N, N), 0)
    col = lax.broadcasted_iota(jnp.int32, (N, N), 1)

    def body(i, _):
        @pl.when(i + 1 < count)
        def _():
            granules(i + 1, lambda c: c.start())

        granules(i, lambda c: c.wait())
        s = loc_ref[N * GR + i]
        p = tab_ref[R_OWN, s]
        len_in = tab_ref[R_LIN, s]
        len_own = lens_ref[p]
        incoming = buf[i & 1].reshape(N, own_ref.shape[2])
        score = (
            lax.dot_general(
                own_ref[p], incoming, (((1,), (1,)), ((), ())), preferred_element_type=jnp.float32
            )
            * scale
        )
        real_in = col < len_in
        real_own = row < len_own
        over_in = jnp.sum(jnp.where(real_in, score, 0.0), 1, keepdims=True) / len_in.astype(jnp.float32)
        own_count = len_own.astype(jnp.float32)
        over_own = jnp.sum(jnp.where(real_own, score, 0.0), 0, keepdims=True) / own_count
        grand = jnp.sum(jnp.where(real_own[:, :1], over_in, 0.0), 0, keepdims=True) / own_count
        own_best = (
            jnp.max(jnp.where(real_in, score - over_own, lowest), 1, keepdims=True) - over_in + grand
        )
        in_best = (
            jnp.max(jnp.where(real_own, score - over_in, lowest), 0, keepdims=True) - over_own + grand
        )
        best = best_ref[...]
        best_ref[...] = jnp.where(col == p, jnp.maximum(best, own_best), best)
        ret_ref[pl.ds(s, 1), :] = in_best
        return 0

    lax.fori_loop(0, count, body, 0)


def match(n1, tab, loc, lens, own, got1, got2):
    return pl.pallas_call(
        functools.partial(match_kernel, n1),
        out_shape=[jax.ShapeDtypeStruct((N, N), jnp.float32)] * 2,
        in_specs=[pl.BlockSpec(memory_space=pltpu.SMEM)] * 3
        + [pl.BlockSpec(memory_space=pltpu.VMEM)]
        + [pl.BlockSpec(memory_space=pl.ANY)] * 2,
        out_specs=[pl.BlockSpec(memory_space=pltpu.VMEM)] * 2,
        scratch_shapes=[
            pltpu.VMEM((2, GR, 16, own.shape[2]), own.dtype),
            pltpu.SemaphoreType.DMA((2, GR)),
        ],
        compiler_params=pltpu.CompilerParams(vmem_limit_bytes=40 << 20),
        name="match",
    )(tab, loc, lens, own, got1, got2)


def centred(score_matrix, row_validity_mask, col_mask):
    row_count = jnp.sum(row_validity_mask, -1)
    col_count = jnp.sum(col_mask, -1)
    row_mean = jnp.sum(score_matrix * col_mask[..., None, :], -1) / col_count[..., None]
    col_mean = jnp.sum(score_matrix * row_validity_mask[..., :, None], -2) / row_count[..., None]
    grand_mean = jnp.sum(row_mean * row_validity_mask, -1) / row_count
    return (
        score_matrix - row_mean[..., :, None] - col_mean[..., None, :] + grand_mean[..., None, None]
    )


def within_cluster(embeddings, masks):
    proteins_here, slots, width = embeddings.shape
    inverse_square_root = 1.0 / jnp.sqrt(jnp.float32(width))
    block_size = 8
    block_count = proteins_here // block_size

    def one_block(block_start):
        block_rows = lax.dynamic_slice_in_dim(embeddings, block_start, block_size, 0)
        block_mask = lax.dynamic_slice_in_dim(masks, block_start, block_size, 0)
        score_matrix = (
            jnp.einsum("bie,qje->bqij", block_rows, embeddings, preferred_element_type=jnp.float32)
            * inverse_square_root
        )
        cent = centred(score_matrix, block_mask[:, None, :], masks[None, :, :])
        row_max = jnp.max(jnp.where(masks[None, :, None, :] > 0, cent, lowest), -1)
        self_pair = (block_start + jnp.arange(block_size))[:, None] == jnp.arange(proteins_here)[
            None, :
        ]
        row_max = jnp.where(self_pair[:, :, None], lowest, row_max)
        best_match = jnp.max(row_max, 1)
        return jnp.where(block_mask > 0, best_match, 0.0)

    start_offsets = jnp.arange(block_count) * block_size
    return lax.map(one_block, start_offsets).reshape(proteins_here, slots)


def exchange(x):
    return lax.all_to_all(x, "shard", split_axis=0, concat_axis=0, tiled=True)


def per_device(embeddings, lengths, requests, query_local):
    proteins_here, slots, width = embeddings.shape
    masks = (jnp.arange(slots)[None, :] < lengths[:, None]).astype(jnp.float32)
    me = lax.axis_index("shard").astype(jnp.int32)[None]
    mate_rows = lax.ppermute(embeddings, "shard", [(d, d ^ 1) for d in range(N)])
    plan = jnp.concatenate([requests, query_local, lengths[None, :]], 1)
    plan = lax.all_gather(plan, "shard", axis=0, tiled=True)
    req, q, lens = plan[:, :N], plan[:, N : 2 * N], plan[:, 2 * N :]
    own = embeddings.reshape(proteins_here * GR, 16, width)
    mate = mate_rows.reshape(proteins_here * GR, 16, width)

    def finish(tab, best, ret, local_best):
        returned = exchange(ret)
        mine = (tab[R_SEND][None, :] == jnp.arange(proteins_here)[:, None]) & (tab[R_GOUT] > 0)[None, :]
        from_ret = jnp.max(jnp.where(mine[:, :, None], returned[None, :, :], lowest), 1)
        best = jnp.maximum(from_ret, best[:, :proteins_here].T)
        cross_best = jnp.where((masks > 0) & (best > -1e29), best, 0.0)
        return local_best, cross_best

    def packed(c2, tab):
        loc = place(c2, me, tab)
        send1 = pack(pack1_kernel, N * C1, tab, own, mate)
        got1 = exchange(send1)
        local_best = within_cluster(embeddings, masks)
        got1, local_best = lax.optimization_barrier((got1, local_best))
        send2 = pack(functools.partial(pack2_kernel, c2), N * c2, tab, own, mate, got1)
        got2 = exchange(send2)
        best, ret = match(N * C1, tab, loc, lengths, embeddings, got1, got2)
        return finish(tab, best, ret, local_best)

    def whole(tab):
        loc = place(0, me, tab)
        got = exchange(pack(pack_whole_kernel, N * GR, tab, own))
        local_best = within_cluster(embeddings, masks)
        best, ret = match(N * GR, tab, loc, lengths, embeddings, got, got)
        return finish(tab, best, ret, local_best)

    def second(_):
        tab = route(2, me, req, q, lens)
        return lax.cond(tab[R_LEFT, 0] == 0, functools.partial(packed, 2), whole, tab)

    tab = route(1, me, req, q, lens)
    return lax.cond(tab[R_LEFT, 0] == 0, functools.partial(packed, 1), second, tab)


def solution(mesh):
    placed = (P("shard", None, None), P("shard"), P("shard", None), P("shard", None))
    return jax.shard_map(
        per_device,
        mesh=mesh,
        in_specs=placed,
        out_specs=(P("shard", None), P("shard", None)),
        check_vma=False,
    )
```

```python
import functools

import jax
import jax.numpy as jnp
from jax import lax
from jax.experimental import pallas as pl
from jax.experimental.pallas import tpu as pltpu
from jax.sharding import PartitionSpec as P

lowest = -1e30
N = 128
GR = 8
C1 = 2
K = 64
DEPTH = 8

R_F1ROW, R_F1COL, R_F1COLM, R_F2ROW, R_F2COL, R_SEND, R_SENDM, R_GIN, R_LIN, R_OWN, R_LEFT, R_GOUT = range(12)


def swap_rows(x, s):
    return jnp.where((s & 1) == 0, pltpu.roll(x, N - 1, 0), pltpu.roll(x, 1, 0))


def swap_cols(x, r):
    return jnp.where((r & 1) == 0, pltpu.roll(x, N - 1, 1), pltpu.roll(x, 1, 1))


def skew(x, by, axis, sign):
    for b in range(7):
        shift = (1 << b) if sign > 0 else N - (1 << b)
        x = jnp.where(((by >> b) & 1) == 1, pltpu.roll(x, shift, axis), x)
    return x


def before(x, s):
    total = x
    for b in range(7):
        total = total + jnp.where(s >= (1 << b), pltpu.roll(total, 1 << b, 0), 0)
    return total - x


def route_kernel(c2, me_ref, req_ref, q_ref, lens_ref, lens_t_ref, tab_ref, tmp_ref):
    s = lax.broadcasted_iota(jnp.int32, (N, N), 0)
    r = lax.broadcasted_iota(jnp.int32, (N, N), 1)
    req = req_ref[...]
    q = q_ref[...]
    live = (req >= 0).astype(jnp.int32)
    req = jnp.maximum(req, 0)
    la = jnp.zeros((N, N), jnp.int32)
    lb = jnp.zeros((N, N), jnp.int32)
    for p in range(16):
        la = jnp.where(q == p, lens_ref[:, p : p + 1], la)
        lb = jnp.where(req == p, lens_t_ref[p : p + 1, :], lb)
    la = la * live
    lb = lb * live
    lb_t = lb.T
    ga = (la + 15) >> 4
    gb = (lb + 15) >> 4
    ga_t = ga.T
    gb_t = gb.T
    anti = live - live.T
    base = 1000 * (gb + gb_t - ga - ga_t) + jnp.where(((s + r) & 1) == 0, 250, -250)
    score = base
    bias_col = jnp.zeros((N, 1), jnp.int32)
    bias_row = jnp.zeros((1, N), jnp.int32)
    for eta in (10, 6, 4):
        gets = score < 0
        net = jnp.where(gets, gb_t, ga) - jnp.where(gets, gb, ga_t)
        bias_row = bias_row + eta * jnp.sum(net, axis=0, keepdims=True)
        bias_col = bias_col - eta * jnp.sum(net, axis=1, keepdims=True)
        score = base + anti * (bias_col - bias_row)
    lister_gets = score < 0
    lin = jnp.where(lister_gets, lb_t, la)
    psend = jnp.where(lister_gets, req.T, q)
    pown = jnp.where(lister_gets, q.T, req)
    m_tot = (lin + 15) >> 4

    diag = s == r
    free1 = jnp.where(diag, 0, C1)
    n = jnp.minimum(m_tot, free1)
    rem = m_tot - n
    w1 = free1 - n
    for k in range(C1):
        w1 = w1 | jnp.where(k < n, ((r << 3) | k) << (2 + 11 * k), 0)
    free2 = jnp.where(diag, 0, c2)
    g_from = m_tot - rem
    n = jnp.minimum(rem, free2)
    rem = rem - n
    w2 = free2 - n
    for k in range(c2):
        w2 = w2 | jnp.where(k < n, ((g_from + k) << 2) << (2 + 14 * k), 0)
    rem_c = swap_cols(rem, r)
    g_from = swap_cols(m_tot, r) - rem_c
    used = C1 - (w1 & 3)
    n = jnp.where(diag, 0, jnp.minimum(rem_c, w1 & 3))
    n = jnp.maximum(jnp.minimum(n, K - before(n, s)), 0)
    w1 = w1 - n
    for k in range(C1):
        code = (1 << 10) | ((r ^ 1) << 3) | (g_from + k - used)
        w1 = w1 | jnp.where((k >= used) & (k < used + n), code << (2 + 11 * k), 0)
    rem = swap_cols(rem_c - n, r)
    rem_s = swap_rows(rem, s)
    g_from = swap_rows(m_tot, s) - rem_s
    used = c2 - (w2 & 3)
    n = jnp.where(diag, 0, jnp.minimum(rem_s, w2 & 3))
    w2 = w2 - n
    for k in range(c2):
        code = 1 | ((g_from + k - used) << 2)
        w2 = w2 | jnp.where((k >= used) & (k < used + n), code << (2 + 14 * k), 0)
    rem = swap_rows(rem_s - n, s)

    w1 = skew(w1, s, 1, -1)
    w2 = skew(w2, r, 0, -1)

    def step(least, w1, w2, rem):
        f1 = w1 & 3
        f2 = w2 & 3
        ok = (jnp.minimum(f1, f2) > 0) & (rem >= least)
        g = m_tot - rem
        code1 = (r << 3) | g
        code2 = 2 | (g << 2) | ((C1 - f1) << 5) | (s << 6)
        new1 = (w1 - 1) | (code1 << jnp.where(f1 == C1, 2, 13))
        new2 = (w2 - 1) | (code2 << jnp.where(f2 == c2, 2, 16))
        w1 = jnp.where(ok, new1, w1)
        w2 = jnp.where(ok, new2, w2)
        rem = jnp.where(ok, rem - 1, rem)
        return pltpu.roll(w1, N - 1, 1), pltpu.roll(w2, N - 1, 0), rem

    def open_count(least, rem):
        return jnp.sum((rem >= least).astype(jnp.int32))

    turns = jnp.int32(0)
    left = jnp.int32(0)
    for least in (4, 2, 1):

        def body(c):
            i, _, w1, w2, rem = c
            for _ in range(8):
                w1, w2, rem = step(least, w1, w2, rem)
            return i + 1, open_count(least, rem), w1, w2, rem

        i, left, w1, w2, rem = lax.while_loop(
            lambda c: (c[0] < N // 8) & (c[1] > 0),
            body,
            (jnp.int32(0), open_count(least, rem), w1, w2, rem),
        )
        turns = turns + 8 * i
    turns = turns & (N - 1)
    w1 = skew(pltpu.roll(w1, turns, 1), s, 1, 1)
    w2 = skew(pltpu.roll(w2, turns, 0), r, 0, 1)

    me = me_ref[0]
    mate = me ^ 1

    def put(x, *rows):
        tmp_ref[...] = x
        for row, at in rows:
            tab_ref[row : row + 1, :] = tmp_ref[pl.ds(at, 1), :]

    put(w1, (R_F1ROW, me))
    put(w1.T, (R_F1COL, me), (R_F1COLM, mate))
    put(w2, (R_F2ROW, me))
    put(w2.T, (R_F2COL, me))
    put(psend, (R_SEND, me), (R_SENDM, mate))
    put(m_tot.T, (R_GIN, me))
    put(lin.T, (R_LIN, me))
    put(pown.T, (R_OWN, me))
    tab_ref[R_LEFT : R_LEFT + 1, :] = jnp.full((1, N), left, jnp.int32)
    put(m_tot, (R_GOUT, me))
    tab_ref[R_GOUT + 1 :, :] = jnp.zeros((16 - R_GOUT - 1, N), jnp.int32)


def route(c2, me, req, q, lens):
    return pl.pallas_call(
        functools.partial(route_kernel, c2),
        out_shape=jax.ShapeDtypeStruct((16, N), jnp.int32),
        in_specs=[pl.BlockSpec(memory_space=pltpu.SMEM)] + [pl.BlockSpec(memory_space=pltpu.VMEM)] * 4,
        out_specs=pl.BlockSpec(memory_space=pltpu.VMEM),
        scratch_shapes=[pltpu.VMEM((N, N), jnp.int32)],
        compiler_params=pltpu.CompilerParams(vmem_limit_bytes=32 << 20),
        name=f"route{c2}",
    )(me, req, q, lens, lens.T)


def pack1_kernel(tab_ref, own_ref, out_ref):
    block = out_ref.shape[0] // C1
    first = pl.program_id(0) * block

    def body(j, _):
        w = tab_ref[R_F1ROW, first + j]
        for k in range(C1):
            code = w >> (2 + 11 * k)
            out_ref[j * C1 + k] = own_ref[tab_ref[R_SEND, (code >> 3) & (N - 1)] * GR + (code & 7)]
        return 0

    lax.fori_loop(0, block, body, 0, unroll=4)


def pack1(tab, own):
    steps = 8
    return pl.pallas_call(
        pack1_kernel,
        grid=(steps,),
        out_shape=jax.ShapeDtypeStruct((N * C1,) + own.shape[1:], own.dtype),
        in_specs=[
            pl.BlockSpec(memory_space=pltpu.SMEM),
            pl.BlockSpec(own.shape, lambda i: (0, 0, 0)),
        ],
        out_specs=pl.BlockSpec((N * C1 // steps,) + own.shape[1:], lambda i: (i, 0, 0)),
        compiler_params=pltpu.CompilerParams(vmem_limit_bytes=40 << 20),
        name="pack1",
    )(tab, own)


def pack2_kernel(c2, tab_ref, own_ref, mate_ref, got_ref, out_ref, buf, in_sem, out_sem):
    parts = in_sem.shape[0]
    each = N // parts

    def fetch(part):
        def body(j, _):
            to = part * each + j
            w = tab_ref[R_F2ROW, to]
            for k in range(c2):
                code = w >> (2 + 14 * k)
                kind = code & 3
                g = (code >> 2) & 7
                slot = ((code >> 6) & (N - 1)) * C1 + ((code >> 5) & 1)
                dst = buf.at[to * c2 + k]

                @pl.when(kind == 0)
                def _():
                    src = own_ref.at[tab_ref[R_SEND, to] * GR + g]
                    pltpu.make_async_copy(src, dst, in_sem.at[part]).start()

                @pl.when(kind == 1)
                def _():
                    src = mate_ref.at[tab_ref[R_SENDM, to] * GR + g]
                    pltpu.make_async_copy(src, dst, in_sem.at[part]).start()

                @pl.when(kind >= 2)
                def _():
                    pltpu.make_async_copy(got_ref.at[slot], dst, in_sem.at[part]).start()

            return 0

        lax.fori_loop(0, each, body, 0, unroll=4)

    def piece(ref, part):
        return ref.at[pl.ds(part * each * c2, each * c2)]

    for part in range(parts):
        fetch(part)
    for part in range(parts):
        pltpu.make_async_copy(piece(buf, part), piece(buf, part), in_sem.at[part]).wait()
        pltpu.make_async_copy(piece(buf, part), piece(out_ref, part), out_sem.at[part]).start()
    for part in range(parts):
        pltpu.make_async_copy(piece(buf, part), piece(out_ref, part), out_sem.at[part]).wait()


def pack2(c2, tab, own, mate, got):
    parts = 4
    shape = (N * c2,) + own.shape[1:]
    return pl.pallas_call(
        functools.partial(pack2_kernel, c2),
        out_shape=jax.ShapeDtypeStruct(shape, own.dtype),
        in_specs=[pl.BlockSpec(memory_space=pltpu.SMEM)] + [pl.BlockSpec(memory_space=pl.ANY)] * 3,
        out_specs=pl.BlockSpec(memory_space=pl.ANY),
        scratch_shapes=[
            pltpu.VMEM(shape, own.dtype),
            pltpu.SemaphoreType.DMA((parts,)),
            pltpu.SemaphoreType.DMA((parts,)),
        ],
        compiler_params=pltpu.CompilerParams(vmem_limit_bytes=40 << 20),
        name="pack2",
    )(tab, own, mate, got)


def hand_kernel(tab_ref, got_ref, out_ref, sem):
    def body(s, count):
        w = tab_ref[R_F1COL, s]
        for k in range(C1):
            mine = (w >> (2 + 11 * k + 10)) & 1

            @pl.when(mine == 1)
            def _():
                pltpu.make_async_copy(got_ref.at[s * C1 + k], out_ref.at[count], sem).start()

            count = count + mine
        return count

    count = lax.fori_loop(0, N, body, jnp.int32(0))

    def fill(j, _):
        pltpu.make_async_copy(got_ref.at[0], out_ref.at[j], sem).start()
        return 0

    lax.fori_loop(count, K, fill, 0)
    pltpu.make_async_copy(out_ref, out_ref, sem).wait()


def hand(tab, got):
    return pl.pallas_call(
        hand_kernel,
        out_shape=jax.ShapeDtypeStruct((K,) + got.shape[1:], got.dtype),
        in_specs=[pl.BlockSpec(memory_space=pltpu.SMEM), pl.BlockSpec(memory_space=pl.ANY)],
        out_specs=pl.BlockSpec(memory_space=pltpu.VMEM),
        scratch_shapes=[pltpu.SemaphoreType.DMA],
        compiler_params=pltpu.CompilerParams(vmem_limit_bytes=40 << 20),
        name="hand",
    )(tab, got)


def pack_whole_kernel(tab_ref, own_ref, out_ref):
    out_ref[...] = own_ref[...]


def pack_whole(tab, own):
    block = (GR,) + own.shape[1:]
    return pl.pallas_call(
        pack_whole_kernel,
        grid_spec=pltpu.PrefetchScalarGridSpec(
            num_scalar_prefetch=1,
            grid=(N,),
            in_specs=[pl.BlockSpec(block, lambda i, tab: (tab[R_SEND, i], 0, 0))],
            out_specs=pl.BlockSpec(block, lambda i, tab: (i, 0, 0)),
        ),
        out_shape=jax.ShapeDtypeStruct((N * GR,) + own.shape[1:], own.dtype),
        name="pack_whole",
    )(tab, own)


def place_kernel(c2, me_ref, tab_ref, loc_ref):
    me = me_ref[0]

    def body(s, c):
        count, handed = c
        if c2 == 0:
            for g in range(GR):
                loc_ref[s * GR + g] = s * GR + g
        else:
            w = tab_ref[R_F1COL, s]
            filled = C1 - (w & 3)
            for k in range(C1):
                code = w >> (2 + 11 * k)

                @pl.when((k < filled) & (((code >> 3) & 0xFF) == me) & (s != me))
                def _():
                    loc_ref[s * GR + (code & 7)] = s * C1 + k

            w = tab_ref[R_F1COLM, s]
            for k in range(C1):
                code = w >> (2 + 11 * k)
                handed_here = (code >> 10) & 1

                @pl.when(handed_here == 1)
                def _():
                    loc_ref[s * GR + (code & 7)] = (C1 + c2) * N + handed

                handed = handed + handed_here

            w = tab_ref[R_F2COL, s]
            filled = c2 - (w & 3)
            for k in range(c2):
                code = w >> (2 + 14 * k)
                kind = code & 3
                origin = jnp.where(kind >= 2, (code >> 6) & (N - 1), s ^ (kind & 1))

                @pl.when((k < filled) & (s != me))
                def _():
                    loc_ref[origin * GR + ((code >> 2) & 7)] = C1 * N + s * c2 + k

        is_live = tab_ref[R_GIN, s] > 0

        @pl.when(is_live)
        def _():
            loc_ref[N * GR + count] = s

        return count + is_live.astype(jnp.int32), handed

    loc_ref[N * GR + N], _ = lax.fori_loop(0, N, body, (jnp.int32(0), jnp.int32(0)))


def place(c2, me, tab):
    return pl.pallas_call(
        functools.partial(place_kernel, c2),
        out_shape=jax.ShapeDtypeStruct((N * GR + N + 128,), jnp.int32),
        in_specs=[pl.BlockSpec(memory_space=pltpu.SMEM)] * 2,
        out_specs=pl.BlockSpec(memory_space=pltpu.SMEM),
        name="place",
    )(me, tab)


def match_kernel(ends, tab_ref, loc_ref, lens_ref, own_ref, *refs):
    gots, (best_ref, ret_ref, buf, sem) = refs[: len(ends)], refs[len(ends) :]
    scale = 1.0 / jnp.sqrt(jnp.float32(own_ref.shape[2]))
    best_ref[...] = jnp.full(best_ref.shape, lowest, jnp.float32)
    ret_ref[...] = jnp.full(ret_ref.shape, lowest, jnp.float32)
    count = loc_ref[N * GR + N]

    def fetch(i):
        @pl.when(i < count)
        def _():
            s = loc_ref[N * GR + i]
            slot = i & (DEPTH - 1)
            granules = tab_ref[R_GIN, s]
            for g in range(GR):
                at = loc_ref[s * GR + g]
                start = 0
                for got_ref, end in zip(gots, ends):

                    @pl.when((g < granules) & (at >= start) & (at < end))
                    def _(got_ref=got_ref, start=start):
                        pltpu.make_async_copy(
                            got_ref.at[at - start], buf.at[slot, g], sem.at[slot, g]
                        ).start()

                    start = end

    for i in range(DEPTH - 1):
        fetch(i)
    row = lax.broadcasted_iota(jnp.int32, (N, N), 0)
    col = lax.broadcasted_iota(jnp.int32, (N, N), 1)

    def body(i, _):
        fetch(i + DEPTH - 1)
        s = loc_ref[N * GR + i]
        slot = i & (DEPTH - 1)
        for g in range(GR):

            @pl.when(g < tab_ref[R_GIN, s])
            def _():
                pltpu.make_async_copy(gots[0].at[0], buf.at[slot, g], sem.at[slot, g]).wait()

        p = tab_ref[R_OWN, s]
        len_in = tab_ref[R_LIN, s]
        len_own = lens_ref[p]
        incoming = buf[slot].reshape(N, own_ref.shape[2])
        score = (
            lax.dot_general(
                own_ref[p], incoming, (((1,), (1,)), ((), ())), preferred_element_type=jnp.float32
            )
            * scale
        )
        real_in = col < len_in
        real_own = row < len_own
        over_in = jnp.sum(jnp.where(real_in, score, 0.0), 1, keepdims=True) / len_in.astype(jnp.float32)
        own_count = len_own.astype(jnp.float32)
        over_own = jnp.sum(jnp.where(real_own, score, 0.0), 0, keepdims=True) / own_count
        grand = jnp.sum(jnp.where(real_own[:, :1], over_in, 0.0), 0, keepdims=True) / own_count
        own_best = (
            jnp.max(jnp.where(real_in, score - over_own, lowest), 1, keepdims=True) - over_in + grand
        )
        in_best = (
            jnp.max(jnp.where(real_own, score - over_in, lowest), 0, keepdims=True) - over_own + grand
        )
        best = best_ref[...]
        best_ref[...] = jnp.where(col == p, jnp.maximum(best, own_best), best)
        ret_ref[pl.ds(s, 1), :] = in_best
        return 0

    lax.fori_loop(0, count, body, 0)


def match(tab, loc, lens, own, *gots):
    ends = []
    for got in gots:
        ends.append((ends[-1] if ends else 0) + got.shape[0])
    return pl.pallas_call(
        functools.partial(match_kernel, tuple(ends)),
        out_shape=[jax.ShapeDtypeStruct((N, N), jnp.float32)] * 2,
        in_specs=[pl.BlockSpec(memory_space=pltpu.SMEM)] * 3
        + [pl.BlockSpec(memory_space=pltpu.VMEM)]
        + [pl.BlockSpec(memory_space=pl.ANY)] * len(gots),
        out_specs=[pl.BlockSpec(memory_space=pltpu.VMEM)] * 2,
        scratch_shapes=[
            pltpu.VMEM((DEPTH, GR, 16, own.shape[2]), own.dtype),
            pltpu.SemaphoreType.DMA((DEPTH, GR)),
        ],
        compiler_params=pltpu.CompilerParams(vmem_limit_bytes=40 << 20),
        name="match",
    )(tab, loc, lens, own, *gots)


def centred(score_matrix, row_validity_mask, col_mask):
    row_count = jnp.sum(row_validity_mask, -1)
    col_count = jnp.sum(col_mask, -1)
    row_mean = jnp.sum(score_matrix * col_mask[..., None, :], -1) / col_count[..., None]
    col_mean = jnp.sum(score_matrix * row_validity_mask[..., :, None], -2) / row_count[..., None]
    grand_mean = jnp.sum(row_mean * row_validity_mask, -1) / row_count
    return (
        score_matrix - row_mean[..., :, None] - col_mean[..., None, :] + grand_mean[..., None, None]
    )


def within_cluster(embeddings, masks):
    proteins_here, slots, width = embeddings.shape
    inverse_square_root = 1.0 / jnp.sqrt(jnp.float32(width))
    block_size = 8
    block_count = proteins_here // block_size

    def one_block(block_start):
        block_rows = lax.dynamic_slice_in_dim(embeddings, block_start, block_size, 0)
        block_mask = lax.dynamic_slice_in_dim(masks, block_start, block_size, 0)
        score_matrix = (
            jnp.einsum("bie,qje->bqij", block_rows, embeddings, preferred_element_type=jnp.float32)
            * inverse_square_root
        )
        cent = centred(score_matrix, block_mask[:, None, :], masks[None, :, :])
        row_max = jnp.max(jnp.where(masks[None, :, None, :] > 0, cent, lowest), -1)
        self_pair = (block_start + jnp.arange(block_size))[:, None] == jnp.arange(proteins_here)[
            None, :
        ]
        row_max = jnp.where(self_pair[:, :, None], lowest, row_max)
        best_match = jnp.max(row_max, 1)
        return jnp.where(block_mask > 0, best_match, 0.0)

    start_offsets = jnp.arange(block_count) * block_size
    return lax.map(one_block, start_offsets).reshape(proteins_here, slots)


def exchange(x):
    return lax.all_to_all(x, "shard", split_axis=0, concat_axis=0, tiled=True)


def other_core(x):
    return lax.ppermute(x, "shard", [(d, d ^ 1) for d in range(N)])


def per_device(embeddings, lengths, requests, query_local):
    proteins_here, slots, width = embeddings.shape
    masks = (jnp.arange(slots)[None, :] < lengths[:, None]).astype(jnp.float32)
    me = lax.axis_index("shard").astype(jnp.int32)[None]
    plan = jnp.concatenate([requests, query_local, lengths[None, :]], 1)
    plan = lax.all_gather(plan, "shard", axis=0, tiled=True)
    req, q, lens = plan[:, :N], plan[:, N : 2 * N], plan[:, 2 * N :]
    own = embeddings.reshape(proteins_here * GR, 16, width)

    def finish(tab, best, ret, local_best):
        returned = exchange(ret)
        mine = (tab[R_SEND][None, :] == jnp.arange(proteins_here)[:, None]) & (tab[R_GOUT] > 0)[None, :]
        from_ret = jnp.max(jnp.where(mine[:, :, None], returned[None, :, :], lowest), 1)
        best = jnp.maximum(from_ret, best[:, :proteins_here].T)
        cross_best = jnp.where((masks > 0) & (best > -1e29), best, 0.0)
        return local_best, cross_best

    def packed(c2, tab):
        loc = place(c2, me, tab)
        got1 = exchange(pack1(tab, own))
        local_best = within_cluster(embeddings, masks)
        rows, local_best = lax.optimization_barrier((own, local_best))
        mate = other_core(rows)
        got1, local_best, mate = lax.optimization_barrier((got1, local_best, mate))
        send2 = pack2(c2, tab, own, mate, got1)
        send2, got1 = lax.optimization_barrier((send2, got1))
        got2 = exchange(send2)
        handed = other_core(hand(tab, got1))
        best, ret = match(tab, loc, lengths, embeddings, got1, got2, handed)
        return finish(tab, best, ret, local_best)

    def whole(tab):
        loc = place(0, me, tab)
        got = exchange(pack_whole(tab, own))
        local_best = within_cluster(embeddings, masks)
        best, ret = match(tab, loc, lengths, embeddings, got)
        return finish(tab, best, ret, local_best)

    def second(_):
        tab = route(2, me, req, q, lens)
        return lax.cond(tab[R_LEFT, 0] == 0, functools.partial(packed, 2), whole, tab)

    tab = route(1, me, req, q, lens)
    return lax.cond(tab[R_LEFT, 0] == 0, functools.partial(packed, 1), second, tab)


def solution(mesh):
    placed = (P("shard", None, None), P("shard"), P("shard", None), P("shard", None))
    return jax.shard_map(
        per_device,
        mesh=mesh,
        in_specs=placed,
        out_specs=(P("shard", None), P("shard", None)),
        check_vma=False,
    )
```

```python
import functools

import jax
import jax.numpy as jnp
from jax import lax
from jax.experimental import pallas as pl
from jax.experimental.pallas import tpu as pltpu
from jax.sharding import PartitionSpec as P

lowest = -1e30
N = 128
GR = 8
C1 = 2
K = 64
DEPTH = 16
GROUP = 4
URGENT = 64
TRIES = 6

R_F1ROW, R_F1COL, R_F1COLM, R_F2ROW, R_F2COL, R_SEND, R_SENDM, R_GIN, R_LIN, R_OWN, R_LEFT, R_GOUT = range(12)


def swap_rows(x, s):
    return jnp.where((s & 1) == 0, pltpu.roll(x, N - 1, 0), pltpu.roll(x, 1, 0))


def swap_cols(x, r):
    return jnp.where((r & 1) == 0, pltpu.roll(x, N - 1, 1), pltpu.roll(x, 1, 1))


def skew(x, by, axis, sign):
    for b in range(7):
        shift = (1 << b) if sign > 0 else N - (1 << b)
        x = jnp.where(((by >> b) & 1) == 1, pltpu.roll(x, shift, axis), x)
    return x


def before(x, s):
    total = x
    for b in range(7):
        total = total + jnp.where(s >= (1 << b), pltpu.roll(total, 1 << b, 0), 0)
    return total - x


def route_kernel(c2, me_ref, plan_ref, tab_ref, tmp_ref, first_ref):
    s = lax.broadcasted_iota(jnp.int32, (N, N), 0)
    r = lax.broadcasted_iota(jnp.int32, (N, N), 1)
    req = plan_ref[:, :N]
    q = plan_ref[:, N : 2 * N]
    lens = plan_ref[:, 2 * N :]
    lens_t = lens.T
    live = (req >= 0).astype(jnp.int32)
    req = jnp.maximum(req, 0)
    la = jnp.zeros((N, N), jnp.int32)
    lb = jnp.zeros((N, N), jnp.int32)
    for p in range(16):
        la = jnp.where(q == p, lens[:, p : p + 1], la)
        lb = jnp.where(req == p, lens_t[p : p + 1, :], lb)
    la = la * live
    lb = lb * live
    lb_t = lb.T
    ga = (la + 15) >> 4
    gb = (lb + 15) >> 4
    ga_t = ga.T
    gb_t = gb.T
    anti = live - live.T
    base = 1000 * (gb + gb_t - ga - ga_t) + jnp.where(((s + r) & 1) == 0, 250, -250)
    score = base
    bias_col = jnp.zeros((N, 1), jnp.int32)
    bias_row = jnp.zeros((1, N), jnp.int32)
    for eta in (10, 6, 4):
        gets = score < 0
        net = jnp.where(gets, gb_t, ga) - jnp.where(gets, gb, ga_t)
        bias_row = bias_row + eta * jnp.sum(net, axis=0, keepdims=True)
        bias_col = bias_col - eta * jnp.sum(net, axis=1, keepdims=True)
        score = base + anti * (bias_col - bias_row)
    lister_gets = score < 0
    lin = jnp.where(lister_gets, lb_t, la)
    psend = jnp.where(lister_gets, req.T, q)
    pown = jnp.where(lister_gets, q.T, req)
    m_tot = (lin + 15) >> 4

    diag = s == r
    free1 = jnp.where(diag, 0, C1)
    n = jnp.minimum(m_tot, free1)
    rem = m_tot - n
    w1 = free1 - n
    for k in range(C1):
        w1 = w1 | jnp.where(k < n, ((r << 3) | k) << (2 + 11 * k), 0)
    free2 = jnp.where(diag, 0, c2)
    g_from = m_tot - rem
    n = jnp.minimum(rem, free2)
    rem = rem - n
    w2 = free2 - n
    for k in range(c2):
        w2 = w2 | jnp.where(k < n, ((g_from + k) << 2) << (2 + 14 * k), 0)
    rem_c = swap_cols(rem, r)
    g_from = swap_cols(m_tot, r) - rem_c
    used = C1 - (w1 & 3)
    n = jnp.where(diag, 0, jnp.minimum(rem_c, w1 & 3))
    n = jnp.maximum(jnp.minimum(n, K - before(n, s)), 0)
    w1 = w1 - n
    for k in range(C1):
        code = (1 << 10) | ((r ^ 1) << 3) | (g_from + k - used)
        w1 = w1 | jnp.where((k >= used) & (k < used + n), code << (2 + 11 * k), 0)
    rem = swap_cols(rem_c - n, r)
    rem_s = swap_rows(rem, s)
    g_from = swap_rows(m_tot, s) - rem_s
    used = c2 - (w2 & 3)
    n = jnp.where(diag, 0, jnp.minimum(rem_s, w2 & 3))
    w2 = w2 - n
    for k in range(c2):
        code = 1 | ((g_from + k - used) << 2)
        w2 = w2 | jnp.where((k >= used) & (k < used + n), code << (2 + 14 * k), 0)
    rem = swap_rows(rem_s - n, s)

    w1 = skew(w1, s, 1, -1)
    w2 = skew(w2, r, 0, -1)

    def step(least, urgent, w1, w2, rem):
        f1 = w1 & 3
        f2 = w2 & 3
        ok = (jnp.minimum(jnp.minimum(f1, f2), rem) > 0) & (rem + urgent >= least)
        g = m_tot - rem
        code1 = (r << 3) | g
        code2 = 2 | (g << 2) | ((C1 - f1) << 5) | (s << 6)
        new1 = (w1 - 1) | (code1 << jnp.where(f1 == C1, 2, 13))
        new2 = (w2 - 1) | (code2 << jnp.where(f2 == c2, 2, 16))
        w1 = jnp.where(ok, new1, w1)
        w2 = jnp.where(ok, new2, w2)
        rem = jnp.where(ok, rem - 1, rem)
        return pltpu.roll(w1, N - 1, 1), pltpu.roll(w2, N - 1, 0), rem

    first_ref[0] = w1
    first_ref[1] = w2
    first_ref[2] = rem

    def attempt(c):
        tries, _, _, _, _, urgent = c
        w1, w2, rem = first_ref[0], first_ref[1], first_ref[2]
        turns = jnp.int32(0)
        left = jnp.int32(0)
        for least in (URGENT, 4, 2, 1):

            def open_count(rem):
                return jnp.sum(((rem > 0) & (rem + urgent >= least)).astype(jnp.int32))

            def body(c):
                i, _, w1, w2, rem = c
                for _ in range(8):
                    w1, w2, rem = step(least, urgent, w1, w2, rem)
                return i + 1, open_count(rem), w1, w2, rem

            i, left, w1, w2, rem = lax.while_loop(
                lambda c: (c[0] < N // 8) & (c[1] > 0),
                body,
                (jnp.int32(0), open_count(rem), w1, w2, rem),
            )
            turns = turns + 8 * i
        return tries + 1, left, turns, w1, w2, jnp.where(rem > 0, URGENT, urgent)

    _, left, turns, w1, w2, _ = lax.while_loop(
        lambda c: (c[0] < TRIES) & (c[1] > 0),
        attempt,
        (jnp.int32(0), jnp.int32(1), jnp.int32(0), w1, w2, jnp.zeros((N, N), jnp.int32)),
    )
    turns = turns & (N - 1)
    w1 = skew(pltpu.roll(w1, turns, 1), s, 1, 1)
    w2 = skew(pltpu.roll(w2, turns, 0), r, 0, 1)

    me = me_ref[0]
    mate = me ^ 1

    def put(x, *rows):
        tmp_ref[...] = x
        for row, at in rows:
            tab_ref[row : row + 1, :] = tmp_ref[pl.ds(at, 1), :]

    put(w1, (R_F1ROW, me))
    put(w1.T, (R_F1COL, me), (R_F1COLM, mate))
    put(w2, (R_F2ROW, me))
    put(w2.T, (R_F2COL, me))
    put(psend, (R_SEND, me), (R_SENDM, mate))
    put(m_tot.T, (R_GIN, me))
    put(lin.T, (R_LIN, me))
    put(pown.T, (R_OWN, me))
    tab_ref[R_LEFT : R_LEFT + 1, :] = jnp.full((1, N), left, jnp.int32)
    put(m_tot, (R_GOUT, me))
    tab_ref[R_GOUT + 1 :, :] = jnp.zeros((16 - R_GOUT - 1, N), jnp.int32)


def route(c2, me, plan):
    return pl.pallas_call(
        functools.partial(route_kernel, c2),
        out_shape=jax.ShapeDtypeStruct((16, N), jnp.int32),
        in_specs=[pl.BlockSpec(memory_space=pltpu.SMEM), pl.BlockSpec(memory_space=pltpu.VMEM)],
        out_specs=pl.BlockSpec(memory_space=pltpu.VMEM),
        scratch_shapes=[pltpu.VMEM((N, N), jnp.int32), pltpu.VMEM((3, N, N), jnp.int32)],
        compiler_params=pltpu.CompilerParams(vmem_limit_bytes=32 << 20),
        name=f"route{c2}",
    )(me, plan)


def pack1_kernel(tab_ref, own_ref, out_ref, buf, sem):
    parts = sem.shape[0]
    each = N // parts

    def piece(ref, part):
        return ref.at[pl.ds(part * each * C1, each * C1)]

    for part in range(parts):

        def body(j, _):
            w = tab_ref[R_F1ROW, j]
            for k in range(C1):
                code = w >> (2 + 11 * k)
                buf[j * C1 + k] = own_ref[tab_ref[R_SEND, (code >> 3) & (N - 1)] * GR + (code & 7)]
            return 0

        lax.fori_loop(part * each, (part + 1) * each, body, 0, unroll=4)
        pltpu.make_async_copy(piece(buf, part), piece(out_ref, part), sem.at[part]).start()
    for part in range(parts):
        pltpu.make_async_copy(piece(buf, part), piece(out_ref, part), sem.at[part]).wait()


def pack1(tab, own):
    parts = 8
    shape = (N * C1,) + own.shape[1:]
    return pl.pallas_call(
        pack1_kernel,
        out_shape=jax.ShapeDtypeStruct(shape, own.dtype),
        in_specs=[pl.BlockSpec(memory_space=pltpu.SMEM), pl.BlockSpec(memory_space=pltpu.VMEM)],
        out_specs=pl.BlockSpec(memory_space=pltpu.HBM),
        scratch_shapes=[pltpu.VMEM(shape, own.dtype), pltpu.SemaphoreType.DMA((parts,))],
        compiler_params=pltpu.CompilerParams(vmem_limit_bytes=40 << 20),
        name="pack1",
    )(tab, own)


def pack2_kernel(c2, tab_ref, own_ref, mate_ref, got_ref, out_ref, buf, in_sem, out_sem):
    parts = in_sem.shape[0]
    each = N // parts

    def fetch(part):
        def body(j, _):
            to = part * each + j
            w = tab_ref[R_F2ROW, to]
            for k in range(c2):
                code = w >> (2 + 14 * k)
                kind = code & 3
                g = (code >> 2) & 7
                slot = ((code >> 6) & (N - 1)) * C1 + ((code >> 5) & 1)
                dst = buf.at[to * c2 + k]

                @pl.when(kind == 0)
                def _():
                    src = own_ref.at[tab_ref[R_SEND, to] * GR + g]
                    pltpu.make_async_copy(src, dst, in_sem.at[part]).start()

                @pl.when(kind == 1)
                def _():
                    src = mate_ref.at[tab_ref[R_SENDM, to] * GR + g]
                    pltpu.make_async_copy(src, dst, in_sem.at[part]).start()

                @pl.when(kind >= 2)
                def _():
                    pltpu.make_async_copy(got_ref.at[slot], dst, in_sem.at[part]).start()

            return 0

        lax.fori_loop(0, each, body, 0, unroll=4)

    def piece(ref, part):
        return ref.at[pl.ds(part * each * c2, each * c2)]

    for part in range(parts):
        fetch(part)
    for part in range(parts):
        pltpu.make_async_copy(piece(buf, part), piece(buf, part), in_sem.at[part]).wait()
        pltpu.make_async_copy(piece(buf, part), piece(out_ref, part), out_sem.at[part]).start()
    for part in range(parts):
        pltpu.make_async_copy(piece(buf, part), piece(out_ref, part), out_sem.at[part]).wait()


def pack2(c2, tab, own, mate, got):
    parts = 4
    shape = (N * c2,) + own.shape[1:]
    return pl.pallas_call(
        functools.partial(pack2_kernel, c2),
        out_shape=jax.ShapeDtypeStruct(shape, own.dtype),
        in_specs=[pl.BlockSpec(memory_space=pltpu.SMEM)] + [pl.BlockSpec(memory_space=pltpu.HBM)] * 3,
        out_specs=pl.BlockSpec(memory_space=pltpu.HBM),
        scratch_shapes=[
            pltpu.VMEM(shape, own.dtype),
            pltpu.SemaphoreType.DMA((parts,)),
            pltpu.SemaphoreType.DMA((parts,)),
        ],
        compiler_params=pltpu.CompilerParams(vmem_limit_bytes=40 << 20),
        name="pack2",
    )(tab, own, mate, got)


def hand_kernel(tab_ref, got_ref, out_ref, sem):
    def body(s, count):
        w = tab_ref[R_F1COL, s]
        for k in range(C1):
            mine = (w >> (2 + 11 * k + 10)) & 1

            @pl.when(mine == 1)
            def _():
                pltpu.make_async_copy(got_ref.at[s * C1 + k], out_ref.at[count], sem).start()

            count = count + mine
        return count

    count = lax.fori_loop(0, N, body, jnp.int32(0))

    def fill(j, _):
        pltpu.make_async_copy(got_ref.at[0], out_ref.at[j], sem).start()
        return 0

    lax.fori_loop(count, K, fill, 0)
    pltpu.make_async_copy(out_ref, out_ref, sem).wait()


def hand(tab, got):
    return pl.pallas_call(
        hand_kernel,
        out_shape=jax.ShapeDtypeStruct((K,) + got.shape[1:], got.dtype),
        in_specs=[pl.BlockSpec(memory_space=pltpu.SMEM), pl.BlockSpec(memory_space=pltpu.HBM)],
        out_specs=pl.BlockSpec(memory_space=pltpu.VMEM),
        scratch_shapes=[pltpu.SemaphoreType.DMA],
        compiler_params=pltpu.CompilerParams(vmem_limit_bytes=40 << 20),
        name="hand",
    )(tab, got)


def pack_whole_kernel(tab_ref, own_ref, out_ref):
    out_ref[...] = own_ref[...]


def pack_whole(tab, own):
    block = (GR,) + own.shape[1:]
    return pl.pallas_call(
        pack_whole_kernel,
        grid_spec=pltpu.PrefetchScalarGridSpec(
            num_scalar_prefetch=1,
            grid=(N,),
            in_specs=[pl.BlockSpec(block, lambda i, tab: (tab[R_SEND, i], 0, 0))],
            out_specs=pl.BlockSpec(block, lambda i, tab: (i, 0, 0)),
        ),
        out_shape=jax.ShapeDtypeStruct((N * GR,) + own.shape[1:], own.dtype),
        name="pack_whole",
    )(tab, own)


def place_kernel(c2, me_ref, tab_ref, loc_ref):
    me = me_ref[0]

    def body(s, c):
        count, handed = c
        if c2 == 0:
            for g in range(GR):
                loc_ref[s * GR + g] = s * GR + g
        else:
            w = tab_ref[R_F1COL, s]
            filled = C1 - (w & 3)
            for k in range(C1):
                code = w >> (2 + 11 * k)

                @pl.when((k < filled) & (((code >> 3) & 0xFF) == me) & (s != me))
                def _():
                    loc_ref[s * GR + (code & 7)] = s * C1 + k

            w = tab_ref[R_F1COLM, s]
            for k in range(C1):
                code = w >> (2 + 11 * k)
                handed_here = (code >> 10) & 1

                @pl.when(handed_here == 1)
                def _():
                    loc_ref[s * GR + (code & 7)] = (C1 + c2) * N + handed

                handed = handed + handed_here

            w = tab_ref[R_F2COL, s]
            filled = c2 - (w & 3)
            for k in range(c2):
                code = w >> (2 + 14 * k)
                kind = code & 3
                origin = jnp.where(kind >= 2, (code >> 6) & (N - 1), s ^ (kind & 1))

                @pl.when((k < filled) & (s != me))
                def _():
                    loc_ref[origin * GR + ((code >> 2) & 7)] = C1 * N + s * c2 + k

        is_live = tab_ref[R_GIN, s] > 0

        is_late = is_live & (tab_ref[R_GIN, s] > C1)
        early, late = count

        @pl.when(is_live)
        def _():
            loc_ref[N * GR + jnp.where(is_late, N - 1 - late, early)] = s

        late = late + is_late.astype(jnp.int32)
        return (early + (is_live.astype(jnp.int32) - is_late.astype(jnp.int32)), late), handed

    zero = jnp.int32(0)
    (early, late), _ = lax.fori_loop(0, N, body, ((zero, zero), zero))
    loc_ref[N * GR + N] = early
    loc_ref[N * GR + N + 1] = late


def place(c2, me, tab):
    return pl.pallas_call(
        functools.partial(place_kernel, c2),
        out_shape=jax.ShapeDtypeStruct((N * GR + N + 128,), jnp.int32),
        in_specs=[pl.BlockSpec(memory_space=pltpu.SMEM)] * 2,
        out_specs=pl.BlockSpec(memory_space=pltpu.SMEM),
        name="place",
    )(me, tab)


def match_kernel(late, ends, tab_ref, loc_ref, lens_ref, own_ref, best0_ref, ret0_ref, *refs):
    gots, (best_ref, ret_ref, buf, sem) = refs[: len(ends)], refs[len(ends) :]
    scale = 1.0 / jnp.sqrt(jnp.float32(own_ref.shape[2]))
    best_ref[...] = best0_ref[...]
    ret_ref[...] = ret0_ref[...]
    count = loc_ref[N * GR + N + int(late)]

    def sender(i):
        return loc_ref[N * GR + (N - 1 - i if late else i)]

    def fetch(i):
        @pl.when(i < count)
        def _():
            s = sender(i)
            slot = i & (DEPTH - 1)
            granules = tab_ref[R_GIN, s]
            for g in range(GR if late else min(GR, C1)):

                @pl.when(g < granules)
                def _():
                    at = loc_ref[s * GR + g]
                    start = 0
                    for got_ref, end in zip(gots, ends):

                        @pl.when((at >= start) & (at < end))
                        def _(got_ref=got_ref, start=start):
                            pltpu.make_async_copy(
                                got_ref.at[at - start], buf.at[slot, g], sem.at[slot, g]
                            ).start()

                        start = end

    def arrive(i):
        @pl.when(i < count)
        def _():
            s = sender(i)
            slot = i & (DEPTH - 1)
            granules = tab_ref[R_GIN, s]
            for g in range(GR if late else min(GR, C1)):

                @pl.when(g < granules)
                def _():
                    pltpu.make_async_copy(gots[0].at[0], buf.at[slot, g], sem.at[slot, g]).wait()

    for i in range(DEPTH - GROUP):
        fetch(i)
    row = lax.broadcasted_iota(jnp.int32, (N, N), 0)
    col = lax.broadcasted_iota(jnp.int32, (N, N), 1)

    def score_of(i):
        s = sender(i)
        p = tab_ref[R_OWN, s]
        incoming = buf[i & (DEPTH - 1)].reshape(N, own_ref.shape[2])
        score = lax.dot_general(
            own_ref[p], incoming, (((1,), (1,)), ((), ())), preferred_element_type=jnp.float32
        )
        return s, p, score * scale

    def best_of(s, p, score):
        len_in = tab_ref[R_LIN, s]
        len_own = lens_ref[p]
        real_in = col < len_in
        real_own = row < len_own
        over_in = jnp.sum(jnp.where(real_in, score, 0.0), 1, keepdims=True) / len_in.astype(jnp.float32)
        own_count = len_own.astype(jnp.float32)
        over_own = jnp.sum(jnp.where(real_own, score, 0.0), 0, keepdims=True) / own_count
        grand = jnp.sum(jnp.where(real_own[:, :1], over_in, 0.0), 0, keepdims=True) / own_count
        own_best = (
            jnp.max(jnp.where(real_in, score - over_own, lowest), 1, keepdims=True) - over_in + grand
        )
        in_best = (
            jnp.max(jnp.where(real_own, score - over_in, lowest), 0, keepdims=True) - over_own + grand
        )
        return own_best, in_best

    def body(j, _):
        first = j * GROUP
        for u in range(GROUP):
            fetch(first + u + DEPTH - GROUP)
        for u in range(GROUP):
            arrive(first + u)
        scores = [score_of(jnp.minimum(first + u, count - 1)) for u in range(GROUP)]
        found = [best_of(*x) for x in scores]
        best = best_ref[...]
        for (s, p, _), (own_best, in_best) in zip(scores, found):
            best = jnp.where(col == p, jnp.maximum(best, own_best), best)
            ret_ref[pl.ds(s, 1), :] = in_best
        best_ref[...] = best
        return 0

    lax.fori_loop(0, (count + GROUP - 1) // GROUP, body, 0)


def match(late, tab, loc, lens, own, best, ret, *gots):
    ends = []
    for got in gots:
        ends.append((ends[-1] if ends else 0) + got.shape[0])
    return pl.pallas_call(
        functools.partial(match_kernel, late, tuple(ends)),
        out_shape=[jax.ShapeDtypeStruct((N, N), jnp.float32)] * 2,
        in_specs=[pl.BlockSpec(memory_space=pltpu.SMEM)] * 3
        + [pl.BlockSpec(memory_space=pltpu.VMEM)] * 3
        + [pl.BlockSpec(memory_space=pltpu.HBM)] * len(gots),
        out_specs=[pl.BlockSpec(memory_space=pltpu.VMEM)] * 2,
        scratch_shapes=[
            pltpu.VMEM((DEPTH, GR, 16, own.shape[2]), own.dtype),
            pltpu.SemaphoreType.DMA((DEPTH, GR)),
        ],
        compiler_params=pltpu.CompilerParams(vmem_limit_bytes=40 << 20),
        name="match_late" if late else "match_early",
    )(tab, loc, lens, own, best, ret, *gots)


def centred(score_matrix, row_validity_mask, col_mask):
    row_count = jnp.sum(row_validity_mask, -1)
    col_count = jnp.sum(col_mask, -1)
    row_mean = jnp.sum(score_matrix * col_mask[..., None, :], -1) / col_count[..., None]
    col_mean = jnp.sum(score_matrix * row_validity_mask[..., :, None], -2) / row_count[..., None]
    grand_mean = jnp.sum(row_mean * row_validity_mask, -1) / row_count
    return (
        score_matrix - row_mean[..., :, None] - col_mean[..., None, :] + grand_mean[..., None, None]
    )


def within_cluster(embeddings, masks):
    proteins_here, slots, width = embeddings.shape
    inverse_square_root = 1.0 / jnp.sqrt(jnp.float32(width))
    block_size = 8
    block_count = proteins_here // block_size

    def one_block(block_start):
        block_rows = lax.dynamic_slice_in_dim(embeddings, block_start, block_size, 0)
        block_mask = lax.dynamic_slice_in_dim(masks, block_start, block_size, 0)
        score_matrix = (
            jnp.einsum("bie,qje->bqij", block_rows, embeddings, preferred_element_type=jnp.float32)
            * inverse_square_root
        )
        cent = centred(score_matrix, block_mask[:, None, :], masks[None, :, :])
        row_max = jnp.max(jnp.where(masks[None, :, None, :] > 0, cent, lowest), -1)
        self_pair = (block_start + jnp.arange(block_size))[:, None] == jnp.arange(proteins_here)[
            None, :
        ]
        row_max = jnp.where(self_pair[:, :, None], lowest, row_max)
        best_match = jnp.max(row_max, 1)
        return jnp.where(block_mask > 0, best_match, 0.0)

    start_offsets = jnp.arange(block_count) * block_size
    return lax.map(one_block, start_offsets).reshape(proteins_here, slots)


def exchange(x):
    return lax.all_to_all(x, "shard", split_axis=0, concat_axis=0, tiled=True)


def other_core(x):
    return lax.ppermute(x, "shard", [(d, d ^ 1) for d in range(N)])


def per_device(embeddings, lengths, requests, query_local):
    proteins_here, slots, width = embeddings.shape
    masks = (jnp.arange(slots)[None, :] < lengths[:, None]).astype(jnp.float32)
    me = lax.axis_index("shard").astype(jnp.int32)[None]
    plan = jnp.concatenate([requests, query_local, lengths[None, :]], 1)
    plan = jnp.pad(plan, ((0, 0), (0, 3 * N - plan.shape[1])))
    plan = exchange(jnp.broadcast_to(plan, (N, 3 * N)))
    own = embeddings.reshape(proteins_here * GR, 16, width)

    nothing = jnp.full((N, N), lowest, jnp.float32)

    def finish(tab, best, ret, local_best):
        returned = exchange(ret)
        mine = (tab[R_SEND][None, :] == jnp.arange(proteins_here)[:, None]) & (tab[R_GOUT] > 0)[None, :]
        from_ret = jnp.max(jnp.where(mine[:, :, None], returned[None, :, :], lowest), 1)
        best = jnp.maximum(from_ret, best[:, :proteins_here].T)
        cross_best = jnp.where((masks > 0) & (best > -1e29), best, 0.0)
        return local_best, cross_best

    def packed(c2, tab):
        loc = place(c2, me, tab)
        got1 = exchange(pack1(tab, own))
        local_best = within_cluster(embeddings, masks)
        rows, local_best = lax.optimization_barrier((own, local_best))
        mate = other_core(rows)
        got1, local_best, mate = lax.optimization_barrier((got1, local_best, mate))
        send2 = pack2(c2, tab, own, mate, got1)
        send2, got1 = lax.optimization_barrier((send2, got1))
        got2 = exchange(send2)
        handed = other_core(hand(tab, got1))
        best, ret = match(False, tab, loc, lengths, embeddings, nothing, nothing, got1)
        best, ret, got2 = lax.optimization_barrier((best, ret, got2))
        best, ret = match(True, tab, loc, lengths, embeddings, best, ret, got1, got2, handed)
        return finish(tab, best, ret, local_best)

    def whole(tab):
        loc = place(0, me, tab)
        got = exchange(pack_whole(tab, own))
        local_best = within_cluster(embeddings, masks)
        best, ret = match(False, tab, loc, lengths, embeddings, nothing, nothing, got)
        best, ret = match(True, tab, loc, lengths, embeddings, best, ret, got)
        return finish(tab, best, ret, local_best)

    def second(_):
        tab = route(2, me, plan)
        return lax.cond(tab[R_LEFT, 0] == 0, functools.partial(packed, 2), whole, tab)

    tab = route(1, me, plan)
    return lax.cond(tab[R_LEFT, 0] == 0, functools.partial(packed, 1), second, tab)


def solution(mesh):
    placed = (P("shard", None, None), P("shard"), P("shard", None), P("shard", None))
    return jax.shard_map(
        per_device,
        mesh=mesh,
        in_specs=placed,
        out_specs=(P("shard", None), P("shard", None)),
        check_vma=False,
    )
```

```python
import functools

import jax
import jax.numpy as jnp
from jax import lax
from jax.experimental import pallas as pl
from jax.experimental.pallas import tpu as pltpu
from jax.sharding import PartitionSpec as P

lowest = -1e30
N = 128
GR = 8
C1 = 2
K = 64
DEPTH = 16
GROUP = 4
TRIES = 6

R_F1ROW, R_F1COL, R_F1COLM, R_F2ROW, R_F2COL, R_SEND, R_SENDM, R_GIN, R_LIN, R_OWN, R_LEFT, R_GOUT = range(12)


def swap_rows(x, s):
    return jnp.where((s & 1) == 0, pltpu.roll(x, N - 1, 0), pltpu.roll(x, 1, 0))


def swap_cols(x, r):
    return jnp.where((r & 1) == 0, pltpu.roll(x, N - 1, 1), pltpu.roll(x, 1, 1))


def skew(x, by, axis, sign):
    for b in range(7):
        shift = (1 << b) if sign > 0 else N - (1 << b)
        x = jnp.where(((by >> b) & 1) == 1, pltpu.roll(x, shift, axis), x)
    return x


def before(x, s):
    total = x
    for b in range(7):
        total = total + jnp.where(s >= (1 << b), pltpu.roll(total, 1 << b, 0), 0)
    return total - x


def route_kernel(c2, me_ref, plan_ref, tab_ref, tmp_ref, first_ref):
    s = lax.broadcasted_iota(jnp.int32, (N, N), 0)
    r = lax.broadcasted_iota(jnp.int32, (N, N), 1)
    req = plan_ref[:, :N]
    q = plan_ref[:, N : 2 * N]
    lens = plan_ref[:, 2 * N :]
    lens_t = lens.T
    live = (req >= 0).astype(jnp.int32)
    req = jnp.maximum(req, 0)
    la = jnp.zeros((N, N), jnp.int32)
    lb = jnp.zeros((N, N), jnp.int32)
    for p in range(16):
        la = jnp.where(q == p, lens[:, p : p + 1], la)
        lb = jnp.where(req == p, lens_t[p : p + 1, :], lb)
    la = la * live
    lb = lb * live
    lb_t = lb.T
    ga = (la + 15) >> 4
    gb = (lb + 15) >> 4
    ga_t = ga.T
    gb_t = gb.T
    anti = live - live.T
    base = 1000 * (gb + gb_t - ga - ga_t) + jnp.where(((s + r) & 1) == 0, 250, -250)
    score = base
    bias_col = jnp.zeros((N, 1), jnp.int32)
    bias_row = jnp.zeros((1, N), jnp.int32)
    for eta in (10, 6, 4):
        gets = score < 0
        net = jnp.where(gets, gb_t, ga) - jnp.where(gets, gb, ga_t)
        bias_row = bias_row + eta * jnp.sum(net, axis=0, keepdims=True)
        bias_col = bias_col - eta * jnp.sum(net, axis=1, keepdims=True)
        score = base + anti * (bias_col - bias_row)
    lister_gets = score < 0
    lin = jnp.where(lister_gets, lb_t, la)
    psend = jnp.where(lister_gets, req.T, q)
    pown = jnp.where(lister_gets, q.T, req)
    m_tot = (lin + 15) >> 4

    diag = s == r
    free1 = jnp.where(diag, 0, C1)
    n = jnp.minimum(m_tot, free1)
    rem = m_tot - n
    w1 = free1 - n
    for k in range(C1):
        w1 = w1 | jnp.where(k < n, ((r << 3) | k) << (2 + 12 * k), 0)
    free2 = jnp.where(diag, 0, c2)
    g_from = m_tot - rem
    n = jnp.minimum(rem, free2)
    rem = rem - n
    w2 = free2 - n
    for k in range(c2):
        w2 = w2 | jnp.where(k < n, ((g_from + k) << 2) << (2 + 14 * k), 0)
    m_swap = swap_rows(m_tot, s)
    rem_s = swap_rows(rem, s)
    used = C1 - (w1 & 3)
    n = jnp.where(diag, 0, jnp.minimum(rem_s, w1 & 3))
    w1 = w1 - n
    for k in range(C1):
        code = (1 << 11) | (r << 3) | (m_swap - rem_s + k - used)
        w1 = w1 | jnp.where((k >= used) & (k < used + n), code << (2 + 12 * k), 0)
    rem_s = rem_s - n
    used = c2 - (w2 & 3)
    n = jnp.where(diag, 0, jnp.minimum(rem_s, w2 & 3))
    w2 = w2 - n
    for k in range(c2):
        code = 1 | ((m_swap - rem_s + k - used) << 2)
        w2 = w2 | jnp.where((k >= used) & (k < used + n), code << (2 + 14 * k), 0)
    rem = swap_rows(rem_s - n, s)
    rem_c = swap_cols(rem, r)
    g_from = swap_cols(m_tot, r) - rem_c
    used = C1 - (w1 & 3)
    n = jnp.where(diag, 0, jnp.minimum(rem_c, w1 & 3))
    n = jnp.maximum(jnp.minimum(n, K - before(n, s)), 0)
    w1 = w1 - n
    for k in range(C1):
        code = (1 << 10) | ((r ^ 1) << 3) | (g_from + k - used)
        w1 = w1 | jnp.where((k >= used) & (k < used + n), code << (2 + 12 * k), 0)
    rem = swap_cols(rem_c - n, r)

    w1 = skew(w1, s, 1, -1)
    w2 = skew(w2, r, 0, -1)

    last = m_tot - 1
    kept2 = ((s << 6) | 2) << 2

    def step(limit, w1, w2, g):
        f1 = w1 & 3
        f2 = w2 & 3
        ok = (jnp.minimum(f1, f2) > 0) & (g <= limit)
        first = f1 == C1
        at = g << 2
        code1 = (r << 5) | at
        w1_new = w1 + jnp.where(first, code1, code1 << 12) - 1
        code2 = kept2 + (at << 2) + jnp.where(first, 0, 1 << 7)
        if c2 > 1:
            code2 = jnp.where(f2 == c2, code2, code2 << 14)
        w2_new = w2 + code2 - 1
        w1 = jnp.where(ok, w1_new, w1)
        w2 = jnp.where(ok, w2_new, w2)
        g = jnp.where(ok, g + 1, g)
        return pltpu.roll(w1, N - 1, 1), pltpu.roll(w2, N - 1, 0), g

    first_ref[0] = w1
    first_ref[1] = w2
    first_ref[2] = m_tot - rem

    def sweep(limit, turns, w1, w2, g):
        def body(c):
            i, _, w1, w2, g = c
            for _ in range(8):
                w1, w2, g = step(limit, w1, w2, g)
            return i + 1, jnp.max(limit - g), w1, w2, g

        i, most, w1, w2, g = lax.while_loop(
            lambda c: (c[0] < N // 8) & (c[1] >= 0),
            body,
            (jnp.int32(0), jnp.max(limit - g), w1, w2, g),
        )
        return most, turns + 8 * i, w1, w2, g

    def attempt(c):
        tries, _, _, _, _, urgent = c
        limit = jnp.where(urgent > 0, last, -1)
        _, turns, w1, w2, g = sweep(limit, 0, first_ref[0], first_ref[1], first_ref[2])
        most, turns, w1, w2, g = sweep(last, turns, w1, w2, g)
        return tries + 1, most + 1, turns, w1, w2, jnp.where(g <= last, 1, urgent)

    _, left, turns, w1, w2, _ = lax.while_loop(
        lambda c: (c[0] < TRIES) & (c[1] > 0),
        attempt,
        (jnp.int32(0), jnp.int32(1), jnp.int32(0), w1, w2, jnp.zeros((N, N), jnp.int32)),
    )
    turns = turns & (N - 1)
    w1 = skew(pltpu.roll(w1, turns, 1), s, 1, 1)
    w2 = skew(pltpu.roll(w2, turns, 0), r, 0, 1)

    me = me_ref[0]
    mate = me ^ 1

    def put(x, *rows):
        tmp_ref[...] = x
        for row, at in rows:
            tab_ref[row : row + 1, :] = tmp_ref[pl.ds(at, 1), :]

    put(w1, (R_F1ROW, me))
    put(w1.T, (R_F1COL, me), (R_F1COLM, mate))
    put(w2, (R_F2ROW, me))
    put(w2.T, (R_F2COL, me))
    put(psend, (R_SEND, me), (R_SENDM, mate))
    put(m_tot.T, (R_GIN, me))
    put(lin.T, (R_LIN, me))
    put(pown.T, (R_OWN, me))
    tab_ref[R_LEFT : R_LEFT + 1, :] = jnp.full((1, N), left, jnp.int32)
    put(m_tot, (R_GOUT, me))
    tab_ref[R_GOUT + 1 :, :] = jnp.zeros((16 - R_GOUT - 1, N), jnp.int32)


def route(c2, me, plan):
    return pl.pallas_call(
        functools.partial(route_kernel, c2),
        out_shape=jax.ShapeDtypeStruct((16, N), jnp.int32),
        in_specs=[pl.BlockSpec(memory_space=pltpu.SMEM), pl.BlockSpec(memory_space=pltpu.VMEM)],
        out_specs=pl.BlockSpec(memory_space=pltpu.VMEM),
        scratch_shapes=[pltpu.VMEM((N, N), jnp.int32), pltpu.VMEM((3, N, N), jnp.int32)],
        compiler_params=pltpu.CompilerParams(vmem_limit_bytes=32 << 20),
        name=f"route{c2}",
    )(me, plan)


def pack1_kernel(tab_ref, own_ref, mate_ref, out_ref, buf, sem):
    parts = sem.shape[0]
    each = N // parts

    def piece(ref, part):
        return ref.at[pl.ds(part * each * C1, each * C1)]

    for part in range(parts):

        def body(j, _):
            w = tab_ref[R_F1ROW, j]
            for k in range(C1):
                code = w >> (2 + 12 * k)
                to = (code >> 3) & (N - 1)
                from_mate = (code >> 11) & 1

                @pl.when(from_mate == 0)
                def _():
                    buf[j * C1 + k] = own_ref[tab_ref[R_SEND, to] * GR + (code & 7)]

                @pl.when(from_mate == 1)
                def _():
                    buf[j * C1 + k] = mate_ref[tab_ref[R_SENDM, to] * GR + (code & 7)]

            return 0

        lax.fori_loop(part * each, (part + 1) * each, body, 0, unroll=4)
        pltpu.make_async_copy(piece(buf, part), piece(out_ref, part), sem.at[part]).start()
    for part in range(parts):
        pltpu.make_async_copy(piece(buf, part), piece(out_ref, part), sem.at[part]).wait()


def pack1(tab, own, mate):
    parts = 8
    shape = (N * C1,) + own.shape[1:]
    return pl.pallas_call(
        pack1_kernel,
        out_shape=pltpu.HBM(shape, own.dtype),
        in_specs=[pl.BlockSpec(memory_space=pltpu.SMEM)] + [pl.BlockSpec(memory_space=pltpu.VMEM)] * 2,
        out_specs=pl.BlockSpec(memory_space=pltpu.HBM),
        scratch_shapes=[pltpu.VMEM(shape, own.dtype), pltpu.SemaphoreType.DMA((parts,))],
        compiler_params=pltpu.CompilerParams(vmem_limit_bytes=40 << 20),
        name="pack1",
    )(tab, own, mate)


def pack2_kernel(c2, tab_ref, own_ref, mate_ref, got_ref, out_ref, buf, in_sem, out_sem):
    parts = in_sem.shape[0]
    each = N // parts

    def fetch(part):
        def body(j, _):
            to = part * each + j
            w = tab_ref[R_F2ROW, to]
            for k in range(c2):
                code = w >> (2 + 14 * k)
                kind = code & 3
                g = (code >> 2) & 7
                slot = ((code >> 6) & (N - 1)) * C1 + ((code >> 5) & 1)
                dst = buf.at[to * c2 + k]

                @pl.when(kind == 0)
                def _():
                    src = own_ref.at[tab_ref[R_SEND, to] * GR + g]
                    pltpu.make_async_copy(src, dst, in_sem.at[part]).start()

                @pl.when(kind == 1)
                def _():
                    src = mate_ref.at[tab_ref[R_SENDM, to] * GR + g]
                    pltpu.make_async_copy(src, dst, in_sem.at[part]).start()

                @pl.when(kind >= 2)
                def _():
                    pltpu.make_async_copy(got_ref.at[slot], dst, in_sem.at[part]).start()

            return 0

        lax.fori_loop(0, each, body, 0, unroll=4)

    def piece(ref, part):
        return ref.at[pl.ds(part * each * c2, each * c2)]

    for part in range(parts):
        fetch(part)
    for part in range(parts):
        pltpu.make_async_copy(piece(buf, part), piece(buf, part), in_sem.at[part]).wait()
        pltpu.make_async_copy(piece(buf, part), piece(out_ref, part), out_sem.at[part]).start()
    for part in range(parts):
        pltpu.make_async_copy(piece(buf, part), piece(out_ref, part), out_sem.at[part]).wait()


def pack2(c2, tab, own, mate, got):
    parts = 4
    shape = (N * c2,) + own.shape[1:]
    return pl.pallas_call(
        functools.partial(pack2_kernel, c2),
        out_shape=pltpu.HBM(shape, own.dtype),
        in_specs=[pl.BlockSpec(memory_space=pltpu.SMEM)] + [pl.BlockSpec(memory_space=pltpu.HBM)] * 3,
        out_specs=pl.BlockSpec(memory_space=pltpu.HBM),
        scratch_shapes=[
            pltpu.VMEM(shape, own.dtype),
            pltpu.SemaphoreType.DMA((parts,)),
            pltpu.SemaphoreType.DMA((parts,)),
        ],
        compiler_params=pltpu.CompilerParams(vmem_limit_bytes=40 << 20),
        name="pack2",
    )(tab, *(pltpu.with_memory_space_constraint(x, pltpu.HBM) for x in (own, mate, got)))


def hand_kernel(tab_ref, got_ref, out_ref, sem):
    def body(s, count):
        w = tab_ref[R_F1COL, s]
        for k in range(C1):
            mine = (w >> (2 + 12 * k + 10)) & 1

            @pl.when(mine == 1)
            def _():
                pltpu.make_async_copy(got_ref.at[s * C1 + k], out_ref.at[count], sem).start()

            count = count + mine
        return count

    count = lax.fori_loop(0, N, body, jnp.int32(0))

    def fill(j, _):
        pltpu.make_async_copy(got_ref.at[0], out_ref.at[j], sem).start()
        return 0

    lax.fori_loop(count, K, fill, 0)
    pltpu.make_async_copy(out_ref, out_ref, sem).wait()


def hand(tab, got):
    return pl.pallas_call(
        hand_kernel,
        out_shape=jax.ShapeDtypeStruct((K,) + got.shape[1:], got.dtype),
        in_specs=[pl.BlockSpec(memory_space=pltpu.SMEM), pl.BlockSpec(memory_space=pltpu.HBM)],
        out_specs=pl.BlockSpec(memory_space=pltpu.VMEM),
        scratch_shapes=[pltpu.SemaphoreType.DMA],
        compiler_params=pltpu.CompilerParams(vmem_limit_bytes=40 << 20),
        name="hand",
    )(tab, got)


def pack_whole_kernel(tab_ref, own_ref, out_ref):
    out_ref[...] = own_ref[...]


def pack_whole(tab, own):
    block = (GR,) + own.shape[1:]
    return pl.pallas_call(
        pack_whole_kernel,
        grid_spec=pltpu.PrefetchScalarGridSpec(
            num_scalar_prefetch=1,
            grid=(N,),
            in_specs=[pl.BlockSpec(block, lambda i, tab: (tab[R_SEND, i], 0, 0))],
            out_specs=pl.BlockSpec(block, lambda i, tab: (i, 0, 0)),
        ),
        out_shape=jax.ShapeDtypeStruct((N * GR,) + own.shape[1:], own.dtype),
        name="pack_whole",
    )(tab, own)


def place_kernel(c2, me_ref, tab_ref, loc_ref):
    me = me_ref[0]

    def body(s, c):
        count, handed = c
        if c2 == 0:
            for g in range(GR):
                loc_ref[s * GR + g] = s * GR + g
        else:
            w = tab_ref[R_F1COL, s]
            filled = C1 - (w & 3)
            for k in range(C1):
                code = w >> (2 + 12 * k)

                @pl.when((k < filled) & (((code >> 3) & 0xFF) == me) & (s != me))
                def _():
                    loc_ref[(s ^ ((code >> 11) & 1)) * GR + (code & 7)] = s * C1 + k

            w = tab_ref[R_F1COLM, s]
            for k in range(C1):
                code = w >> (2 + 12 * k)
                handed_here = (code >> 10) & 1

                @pl.when(handed_here == 1)
                def _():
                    loc_ref[s * GR + (code & 7)] = (C1 + c2) * N + handed

                handed = handed + handed_here

            w = tab_ref[R_F2COL, s]
            filled = c2 - (w & 3)
            for k in range(c2):
                code = w >> (2 + 14 * k)
                kind = code & 3
                origin = jnp.where(kind >= 2, (code >> 6) & (N - 1), s ^ (kind & 1))

                @pl.when((k < filled) & (s != me))
                def _():
                    loc_ref[origin * GR + ((code >> 2) & 7)] = C1 * N + s * c2 + k

        is_live = tab_ref[R_GIN, s] > 0

        is_late = is_live & (tab_ref[R_GIN, s] > C1)
        early, late = count

        @pl.when(is_live)
        def _():
            loc_ref[N * GR + jnp.where(is_late, N - 1 - late, early)] = s

        late = late + is_late.astype(jnp.int32)
        return (early + (is_live.astype(jnp.int32) - is_late.astype(jnp.int32)), late), handed

    zero = jnp.int32(0)
    (early, late), _ = lax.fori_loop(0, N, body, ((zero, zero), zero))
    loc_ref[N * GR + N] = early
    loc_ref[N * GR + N + 1] = late


def place(c2, me, tab):
    return pl.pallas_call(
        functools.partial(place_kernel, c2),
        out_shape=jax.ShapeDtypeStruct((N * GR + N + 128,), jnp.int32),
        in_specs=[pl.BlockSpec(memory_space=pltpu.SMEM)] * 2,
        out_specs=pl.BlockSpec(memory_space=pltpu.SMEM),
        name="place",
    )(me, tab)


def match_kernel(late, ends, tab_ref, loc_ref, lens_ref, own_t_ref, best0_ref, ret0_ref, *refs):
    gots, (best_ref, ret_ref, buf, sem) = refs[: len(ends)], refs[len(ends) :]
    width = own_t_ref.shape[1]
    scale = 1.0 / jnp.sqrt(jnp.float32(width))
    best_ref[...] = best0_ref[...]
    ret_ref[...] = ret0_ref[...]
    count = loc_ref[N * GR + N + int(late)]

    def sender(i):
        return loc_ref[N * GR + (N - 1 - i if late else i)]

    def fetch(i):
        @pl.when(i < count)
        def _():
            s = sender(i)
            slot = i & (DEPTH - 1)
            granules = tab_ref[R_GIN, s]
            for g in range(GR if late else min(GR, C1)):

                @pl.when(g < granules)
                def _():
                    at = loc_ref[s * GR + g]
                    start = 0
                    for got_ref, end in zip(gots, ends):

                        @pl.when((at >= start) & (at < end))
                        def _(got_ref=got_ref, start=start):
                            pltpu.make_async_copy(
                                got_ref.at[at - start], buf.at[slot, g], sem.at[slot, g]
                            ).start()

                        start = end

    def arrive(i):
        @pl.when(i < count)
        def _():
            s = sender(i)
            slot = i & (DEPTH - 1)
            granules = tab_ref[R_GIN, s]
            for g in range(GR if late else min(GR, C1)):

                @pl.when(g < granules)
                def _():
                    pltpu.make_async_copy(gots[0].at[0], buf.at[slot, g], sem.at[slot, g]).wait()

    for i in range(DEPTH - GROUP):
        fetch(i)
    row = lax.broadcasted_iota(jnp.int32, (N, N), 0)
    col = lax.broadcasted_iota(jnp.int32, (N, N), 1)

    def score_of(i):
        s = sender(i)
        p = tab_ref[R_OWN, s]
        incoming = buf[i & (DEPTH - 1)].reshape(N, width)
        return s, p, jnp.dot(incoming, own_t_ref[p], preferred_element_type=jnp.float32) * scale

    def best_of(s, p, score):
        len_in = tab_ref[R_LIN, s]
        len_own = lens_ref[p]
        in_count = len_in.astype(jnp.float32)
        real_in = row < len_in
        real_own = col < len_own
        over_own = jnp.sum(jnp.where(real_own, score, 0.0), 1, keepdims=True) / len_own.astype(jnp.float32)
        over_in = jnp.sum(jnp.where(real_in, score, 0.0), 0, keepdims=True) / in_count
        grand = jnp.sum(jnp.where(real_in[:, :1], over_own, 0.0), 0, keepdims=True) / in_count
        own_best = (
            jnp.max(jnp.where(real_in, score - over_own, lowest), 0, keepdims=True) - over_in + grand
        )
        in_best = (
            jnp.max(jnp.where(real_own, score - over_in, lowest), 1, keepdims=True) - over_own + grand
        )
        return own_best, in_best

    def body(j, _):
        first = j * GROUP
        for u in range(GROUP):
            fetch(first + u + DEPTH - GROUP)
        for u in range(GROUP):
            arrive(first + u)
        scores = [score_of(jnp.minimum(first + u, count - 1)) for u in range(GROUP)]
        found = [best_of(*x) for x in scores]
        ret = ret_ref[...]
        for (s, p, _), (own_best, in_best) in zip(scores, found):
            best_ref[pl.ds(p, 1), :] = jnp.maximum(best_ref[pl.ds(p, 1), :], own_best)
            ret = jnp.where(col == s, in_best, ret)
        ret_ref[...] = ret
        return 0

    lax.fori_loop(0, (count + GROUP - 1) // GROUP, body, 0)
    if late:
        ret_ref[...] = ret_ref[...].T


def match(late, tab, loc, lens, own_t, best, ret, *gots):
    ends = []
    for got in gots:
        ends.append((ends[-1] if ends else 0) + got.shape[0])
    return pl.pallas_call(
        functools.partial(match_kernel, late, tuple(ends)),
        out_shape=[jax.ShapeDtypeStruct(x.shape, x.dtype) for x in (best, ret)],
        in_specs=[pl.BlockSpec(memory_space=pltpu.SMEM)] * 3
        + [pl.BlockSpec(memory_space=pltpu.VMEM)] * 3
        + [pl.BlockSpec(memory_space=pltpu.HBM)] * len(gots),
        out_specs=[pl.BlockSpec(memory_space=pltpu.VMEM)] * 2,
        scratch_shapes=[
            pltpu.VMEM((DEPTH, GR, 16, own_t.shape[1]), own_t.dtype),
            pltpu.SemaphoreType.DMA((DEPTH, GR)),
        ],
        compiler_params=pltpu.CompilerParams(vmem_limit_bytes=40 << 20),
        name="match_late" if late else "match_early",
    )(tab, loc, lens, own_t, best, ret, *gots)


def centred(score_matrix, row_validity_mask, col_mask):
    row_count = jnp.sum(row_validity_mask, -1)
    col_count = jnp.sum(col_mask, -1)
    row_mean = jnp.sum(score_matrix * col_mask[..., None, :], -1) / col_count[..., None]
    col_mean = jnp.sum(score_matrix * row_validity_mask[..., :, None], -2) / row_count[..., None]
    grand_mean = jnp.sum(row_mean * row_validity_mask, -1) / row_count
    return (
        score_matrix - row_mean[..., :, None] - col_mean[..., None, :] + grand_mean[..., None, None]
    )


def within_cluster(embeddings, masks):
    proteins_here, slots, width = embeddings.shape
    inverse_square_root = 1.0 / jnp.sqrt(jnp.float32(width))
    block_size = 8
    block_count = proteins_here // block_size

    def one_block(block_start):
        block_rows = lax.dynamic_slice_in_dim(embeddings, block_start, block_size, 0)
        block_mask = lax.dynamic_slice_in_dim(masks, block_start, block_size, 0)
        score_matrix = (
            jnp.einsum("bie,qje->bqij", block_rows, embeddings, preferred_element_type=jnp.float32)
            * inverse_square_root
        )
        cent = centred(score_matrix, block_mask[:, None, :], masks[None, :, :])
        row_max = jnp.max(jnp.where(masks[None, :, None, :] > 0, cent, lowest), -1)
        self_pair = (block_start + jnp.arange(block_size))[:, None] == jnp.arange(proteins_here)[
            None, :
        ]
        row_max = jnp.where(self_pair[:, :, None], lowest, row_max)
        best_match = jnp.max(row_max, 1)
        return jnp.where(block_mask > 0, best_match, 0.0)

    start_offsets = jnp.arange(block_count) * block_size
    return lax.map(one_block, start_offsets).reshape(proteins_here, slots)


def exchange(x):
    return lax.all_to_all(x, "shard", split_axis=0, concat_axis=0, tiled=True)


def other_core(x):
    return lax.ppermute(x, "shard", [(d, d ^ 1) for d in range(N)])


def per_device(embeddings, lengths, requests, query_local):
    proteins_here, slots, width = embeddings.shape
    masks = (jnp.arange(slots)[None, :] < lengths[:, None]).astype(jnp.float32)
    me = lax.axis_index("shard").astype(jnp.int32)[None]
    plan = jnp.concatenate([requests, query_local, lengths[None, :]], 1)
    plan = jnp.pad(plan, ((0, 0), (0, 3 * N - plan.shape[1])))
    plan = exchange(jnp.broadcast_to(plan, (N, 3 * N)))
    own = embeddings.reshape(proteins_here * GR, 16, width)

    mate = other_core(own)
    none_own = jnp.full((proteins_here, slots), lowest, jnp.float32)
    none_in = jnp.full((N, slots), lowest, jnp.float32)

    def finish(tab, best, ret, local_best):
        returned = exchange(ret)
        mine = (tab[R_SEND][None, :] == jnp.arange(proteins_here)[:, None]) & (tab[R_GOUT] > 0)[None, :]
        from_ret = jnp.max(jnp.where(mine[:, :, None], returned[None, :, :], lowest), 1)
        best = jnp.maximum(from_ret, best)
        cross_best = jnp.where((masks > 0) & (best > -1e29), best, 0.0)
        return local_best, cross_best

    def packed(c2, tab):
        loc = place(c2, me, tab)
        got1 = exchange(pack1(tab, own, mate))
        local_best = within_cluster(embeddings, masks)
        rows, local_best = lax.optimization_barrier((embeddings, local_best))
        own_t = jnp.swapaxes(rows, 1, 2)
        got1, local_best, own_t = lax.optimization_barrier((got1, local_best, own_t))
        send2 = pack2(c2, tab, own, mate, got1)
        send2, got1 = lax.optimization_barrier((send2, got1))
        got2 = exchange(send2)
        handed = other_core(hand(tab, got1))
        best, ret = match(False, tab, loc, lengths, own_t, none_own, none_in, got1)
        best, ret, got2 = lax.optimization_barrier((best, ret, got2))
        best, ret = match(True, tab, loc, lengths, own_t, best, ret, got1, got2, handed)
        return finish(tab, best, ret, local_best)

    def whole(tab):
        loc = place(0, me, tab)
        got = exchange(pack_whole(tab, own))
        own_t = jnp.swapaxes(embeddings, 1, 2)
        local_best = within_cluster(embeddings, masks)
        best, ret = match(False, tab, loc, lengths, own_t, none_own, none_in, got)
        best, ret = match(True, tab, loc, lengths, own_t, best, ret, got)
        return finish(tab, best, ret, local_best)

    def second(_):
        tab = route(2, me, plan)
        return lax.cond(tab[R_LEFT, 0] == 0, functools.partial(packed, 2), whole, tab)

    tab = route(1, me, plan)
    return lax.cond(tab[R_LEFT, 0] == 0, functools.partial(packed, 1), second, tab)


def solution(mesh):
    placed = (P("shard", None, None), P("shard"), P("shard", None), P("shard", None))
    return jax.shard_map(
        per_device,
        mesh=mesh,
        in_specs=placed,
        out_specs=(P("shard", None), P("shard", None)),
        check_vma=False,
    )
```

```python
import functools

import jax
import jax.numpy as jnp
from jax import lax
from jax.experimental import pallas as pl
from jax.experimental.pallas import tpu as pltpu
from jax.sharding import PartitionSpec as P

lowest = -1e30
N = 128
GR = 8
C1 = 2
K = 64
DEPTH = 16
GROUP = 4
TRIES = 6

R_F1ROW, R_F1COL, R_F1COLM, R_F2ROW, R_F2COL, R_SEND, R_SENDM, R_GIN, R_LIN, R_OWN, R_GOUT = range(11)


def swap_rows(x, s):
    return jnp.where((s & 1) == 0, pltpu.roll(x, N - 1, 0), pltpu.roll(x, 1, 0))


def swap_cols(x, r):
    return jnp.where((r & 1) == 0, pltpu.roll(x, N - 1, 1), pltpu.roll(x, 1, 1))


def skew(x, by, axis, sign):
    for b in range(7):
        shift = (1 << b) if sign > 0 else N - (1 << b)
        x = jnp.where(((by >> b) & 1) == 1, pltpu.roll(x, shift, axis), x)
    return x


def before(x, s):
    total = x
    for b in range(7):
        total = total + jnp.where(s >= (1 << b), pltpu.roll(total, 1 << b, 0), 0)
    return total - x


def route_kernel(c2, me_ref, plan_ref, tab_ref, left_ref, tmp_ref, first_ref):
    s = lax.broadcasted_iota(jnp.int32, (N, N), 0)
    r = lax.broadcasted_iota(jnp.int32, (N, N), 1)
    req = plan_ref[:, :N]
    q = plan_ref[:, N : 2 * N]
    lens = plan_ref[:, 2 * N :]
    lens_t = lens.T
    live = (req >= 0).astype(jnp.int32)
    req = jnp.maximum(req, 0)
    la = jnp.zeros((N, N), jnp.int32)
    lb = jnp.zeros((N, N), jnp.int32)
    for p in range(16):
        la = jnp.where(q == p, lens[:, p : p + 1], la)
        lb = jnp.where(req == p, lens_t[p : p + 1, :], lb)
    la = la * live
    lb = lb * live
    lb_t = lb.T
    ga = (la + 15) >> 4
    gb = (lb + 15) >> 4
    ga_t = ga.T
    gb_t = gb.T
    anti = live - live.T
    base = 1000 * (gb + gb_t - ga - ga_t) + jnp.where(((s + r) & 1) == 0, 250, -250)
    score = base
    bias_col = jnp.zeros((N, 1), jnp.int32)
    bias_row = jnp.zeros((1, N), jnp.int32)
    for eta in (10, 6, 4):
        gets = score < 0
        net = jnp.where(gets, gb_t, ga) - jnp.where(gets, gb, ga_t)
        bias_row = bias_row + eta * jnp.sum(net, axis=0, keepdims=True)
        bias_col = bias_col - eta * jnp.sum(net, axis=1, keepdims=True)
        score = base + anti * (bias_col - bias_row)
    lister_gets = score < 0
    lin = jnp.where(lister_gets, lb_t, la)
    psend = jnp.where(lister_gets, req.T, q)
    pown = jnp.where(lister_gets, q.T, req)
    m_tot = (lin + 15) >> 4

    diag = s == r
    free1 = jnp.where(diag, 0, C1)
    n = jnp.minimum(m_tot, free1)
    rem = m_tot - n
    w1 = free1 - n
    for k in range(C1):
        w1 = w1 | jnp.where(k < n, ((r << 3) | k) << (2 + 12 * k), 0)
    m_swap = swap_rows(m_tot, s)
    rem_s = swap_rows(rem, s)
    used = C1 - (w1 & 3)
    n = jnp.where(diag, 0, jnp.minimum(rem_s, w1 & 3))
    w1 = w1 - n
    for k in range(C1):
        code = (1 << 11) | (r << 3) | (m_swap - rem_s + k - used)
        w1 = w1 | jnp.where((k >= used) & (k < used + n), code << (2 + 12 * k), 0)
    rem = swap_rows(rem_s - n, s)
    free2 = jnp.where(diag, 0, c2)
    g_from = m_tot - rem
    n = jnp.minimum(rem, free2)
    rem = rem - n
    w2 = free2 - n
    for k in range(c2):
        w2 = w2 | jnp.where(k < n, ((g_from + k) << 2) << (2 + 14 * k), 0)
    rem_s = swap_rows(rem, s)
    used = c2 - (w2 & 3)
    n = jnp.where(diag, 0, jnp.minimum(rem_s, w2 & 3))
    w2 = w2 - n
    for k in range(c2):
        code = 1 | ((m_swap - rem_s + k - used) << 2)
        w2 = w2 | jnp.where((k >= used) & (k < used + n), code << (2 + 14 * k), 0)
    rem = swap_rows(rem_s - n, s)
    rem_c = swap_cols(rem, r)
    g_from = swap_cols(m_tot, r) - rem_c
    used = C1 - (w1 & 3)
    n = jnp.where(diag, 0, jnp.minimum(rem_c, w1 & 3))
    n = jnp.maximum(jnp.minimum(n, K - before(n, s)), 0)
    w1 = w1 - n
    for k in range(C1):
        code = (1 << 10) | ((r ^ 1) << 3) | (g_from + k - used)
        w1 = w1 | jnp.where((k >= used) & (k < used + n), code << (2 + 12 * k), 0)
    rem = swap_cols(rem_c - n, r)

    w1 = skew(w1, s, 1, -1)
    w2 = skew(w2, r, 0, -1)

    last = m_tot - 1
    kept2 = ((s << 6) | 2) << 2

    def step(limit, w1, w2, g):
        f1 = w1 & 3
        f2 = w2 & 3
        ok = (jnp.minimum(f1, f2) > 0) & (g <= limit)
        first = f1 == C1
        at = g << 2
        code1 = (r << 5) | at
        w1_new = w1 + jnp.where(first, code1, code1 << 12) - 1
        code2 = kept2 + (at << 2) + jnp.where(first, 0, 1 << 7)
        if c2 > 1:
            code2 = jnp.where(f2 == c2, code2, code2 << 14)
        w2_new = w2 + code2 - 1
        w1 = jnp.where(ok, w1_new, w1)
        w2 = jnp.where(ok, w2_new, w2)
        g = jnp.where(ok, g + 1, g)
        return pltpu.roll(w1, N - 1, 1), pltpu.roll(w2, N - 1, 0), g

    first_ref[0] = w1
    first_ref[1] = w2
    first_ref[2] = m_tot - rem

    def sweep(limit, turns, w1, w2, g):
        def body(c):
            i, _, w1, w2, g = c
            for _ in range(8):
                w1, w2, g = step(limit, w1, w2, g)
            return i + 1, jnp.max(limit - g), w1, w2, g

        i, most, w1, w2, g = lax.while_loop(
            lambda c: (c[0] < N // 8) & (c[1] >= 0),
            body,
            (jnp.int32(0), jnp.max(limit - g), w1, w2, g),
        )
        return most, turns + 8 * i, w1, w2, g

    def attempt(c):
        tries, _, _, _, _, urgent = c
        limit = jnp.where(urgent > 0, last, -1)
        _, turns, w1, w2, g = sweep(limit, 0, first_ref[0], first_ref[1], first_ref[2])
        most, turns, w1, w2, g = sweep(last, turns, w1, w2, g)
        return tries + 1, most + 1, turns, w1, w2, jnp.where(g <= last, 1, urgent)

    _, left, turns, w1, w2, _ = lax.while_loop(
        lambda c: (c[0] < TRIES) & (c[1] > 0),
        attempt,
        (jnp.int32(0), jnp.int32(1), jnp.int32(0), w1, w2, jnp.zeros((N, N), jnp.int32)),
    )
    turns = turns & (N - 1)
    w1 = skew(pltpu.roll(w1, turns, 1), s, 1, 1)
    w2 = skew(pltpu.roll(w2, turns, 0), r, 0, 1)

    me = me_ref[0]
    mate = me ^ 1

    def put(x, *rows):
        tmp_ref[...] = x
        for row, at in rows:
            tab_ref[row : row + 1, :] = tmp_ref[pl.ds(at, 1), :]

    put(w1, (R_F1ROW, me))
    put(w1.T, (R_F1COL, me), (R_F1COLM, mate))
    put(w2, (R_F2ROW, me))
    put(w2.T, (R_F2COL, me))
    put(psend, (R_SEND, me), (R_SENDM, mate))
    put(m_tot.T, (R_GIN, me))
    put(lin.T, (R_LIN, me))
    put(pown.T, (R_OWN, me))
    left_ref[0] = left
    put(m_tot, (R_GOUT, me))
    tab_ref[R_GOUT + 1 :, :] = jnp.zeros((16 - R_GOUT - 1, N), jnp.int32)


def route(c2, me, plan):
    return pl.pallas_call(
        functools.partial(route_kernel, c2),
        out_shape=[jax.ShapeDtypeStruct((16, N), jnp.int32), jax.ShapeDtypeStruct((1,), jnp.int32)],
        in_specs=[pl.BlockSpec(memory_space=pltpu.SMEM), pl.BlockSpec(memory_space=pltpu.VMEM)],
        out_specs=[pl.BlockSpec(memory_space=pltpu.VMEM), pl.BlockSpec(memory_space=pltpu.SMEM)],
        scratch_shapes=[pltpu.VMEM((N, N), jnp.int32), pltpu.VMEM((3, N, N), jnp.int32)],
        compiler_params=pltpu.CompilerParams(vmem_limit_bytes=32 << 20),
        name=f"route{c2}",
    )(me, plan)


def pack1_kernel(tab_ref, own_ref, mate_ref, out_ref, buf, in_sem, out_sem):
    parts = out_sem.shape[0]
    each = N // parts

    def piece(ref, part):
        return ref.at[pl.ds(part * each * C1, each * C1)]

    def codes(j):
        w = tab_ref[R_F1ROW, j]
        return [(k, w >> (2 + 12 * k)) for k in range(C1)]

    def from_mate(part, j, k, code):
        at = tab_ref[R_SENDM, (code >> 3) & (N - 1)] * GR + (code & 7)
        return pltpu.make_async_copy(mate_ref.at[at], buf.at[j * C1 + k], in_sem.at[part])

    for part in range(parts):

        def start(j, count, part=part):
            for k, code in codes(j):
                is_mate = (code >> 11) & 1

                @pl.when(is_mate == 1)
                def _():
                    from_mate(part, j, k, code).start()

                @pl.when(is_mate == 0)
                def _():
                    at = tab_ref[R_SEND, (code >> 3) & (N - 1)] * GR + (code & 7)
                    buf[j * C1 + k] = own_ref[at]

                count = count + is_mate
            return count

        count = lax.fori_loop(part * each, (part + 1) * each, start, jnp.int32(0), unroll=4)

        def finish(i, _, part=part):
            pltpu.make_async_copy(mate_ref.at[0], buf.at[0], in_sem.at[part]).wait()
            return 0

        lax.fori_loop(0, count, finish, 0)
        pltpu.make_async_copy(piece(buf, part), piece(out_ref, part), out_sem.at[part]).start()
    for part in range(parts):
        pltpu.make_async_copy(piece(buf, part), piece(out_ref, part), out_sem.at[part]).wait()


def pack1(tab, own, mate):
    parts = 8
    shape = (N * C1,) + own.shape[1:]
    return pl.pallas_call(
        pack1_kernel,
        out_shape=pltpu.HBM(shape, own.dtype),
        in_specs=[
            pl.BlockSpec(memory_space=pltpu.SMEM),
            pl.BlockSpec(memory_space=pltpu.VMEM),
            pl.BlockSpec(memory_space=pltpu.HBM),
        ],
        out_specs=pl.BlockSpec(memory_space=pltpu.HBM),
        scratch_shapes=[
            pltpu.VMEM(shape, own.dtype),
            pltpu.SemaphoreType.DMA((parts,)),
            pltpu.SemaphoreType.DMA((parts,)),
        ],
        compiler_params=pltpu.CompilerParams(vmem_limit_bytes=24 << 20),
        name="pack1",
    )(tab, own, pltpu.with_memory_space_constraint(mate, pltpu.HBM))


def pack2_kernel(c2, tab_ref, own_ref, mate_ref, got_ref, out_ref, buf, in_sem, out_sem):
    parts = in_sem.shape[0]
    each = N // parts

    def fetch(part):
        def body(j, _):
            to = part * each + j
            w = tab_ref[R_F2ROW, to]
            for k in range(c2):
                code = w >> (2 + 14 * k)
                kind = code & 3
                g = (code >> 2) & 7
                slot = ((code >> 6) & (N - 1)) * C1 + ((code >> 5) & 1)
                dst = buf.at[to * c2 + k]

                @pl.when(kind == 0)
                def _():
                    src = own_ref.at[tab_ref[R_SEND, to] * GR + g]
                    pltpu.make_async_copy(src, dst, in_sem.at[part]).start()

                @pl.when(kind == 1)
                def _():
                    src = mate_ref.at[tab_ref[R_SENDM, to] * GR + g]
                    pltpu.make_async_copy(src, dst, in_sem.at[part]).start()

                @pl.when(kind >= 2)
                def _():
                    pltpu.make_async_copy(got_ref.at[slot], dst, in_sem.at[part]).start()

            return 0

        lax.fori_loop(0, each, body, 0, unroll=4)

    def piece(ref, part):
        return ref.at[pl.ds(part * each * c2, each * c2)]

    for part in range(parts):
        fetch(part)
    for part in range(parts):
        pltpu.make_async_copy(piece(buf, part), piece(buf, part), in_sem.at[part]).wait()
        pltpu.make_async_copy(piece(buf, part), piece(out_ref, part), out_sem.at[part]).start()
    for part in range(parts):
        pltpu.make_async_copy(piece(buf, part), piece(out_ref, part), out_sem.at[part]).wait()


def pack2(c2, tab, own, mate, got):
    parts = 4
    shape = (N * c2,) + own.shape[1:]
    return pl.pallas_call(
        functools.partial(pack2_kernel, c2),
        out_shape=pltpu.HBM(shape, own.dtype),
        in_specs=[pl.BlockSpec(memory_space=pltpu.SMEM)] + [pl.BlockSpec(memory_space=pltpu.HBM)] * 3,
        out_specs=pl.BlockSpec(memory_space=pltpu.HBM),
        scratch_shapes=[
            pltpu.VMEM(shape, own.dtype),
            pltpu.SemaphoreType.DMA((parts,)),
            pltpu.SemaphoreType.DMA((parts,)),
        ],
        compiler_params=pltpu.CompilerParams(vmem_limit_bytes=40 << 20),
        name="pack2",
    )(tab, *(pltpu.with_memory_space_constraint(x, pltpu.HBM) for x in (own, mate, got)))


def hand_kernel(tab_ref, got_ref, out_ref, sem):
    def body(s, count):
        w = tab_ref[R_F1COL, s]
        for k in range(C1):
            mine = (w >> (2 + 12 * k + 10)) & 1

            @pl.when(mine == 1)
            def _():
                pltpu.make_async_copy(got_ref.at[s * C1 + k], out_ref.at[count], sem).start()

            count = count + mine
        return count

    count = lax.fori_loop(0, N, body, jnp.int32(0))

    def fill(j, _):
        pltpu.make_async_copy(got_ref.at[0], out_ref.at[j], sem).start()
        return 0

    lax.fori_loop(count, K, fill, 0)
    pltpu.make_async_copy(out_ref, out_ref, sem).wait()


def hand(tab, got):
    return pl.pallas_call(
        hand_kernel,
        out_shape=jax.ShapeDtypeStruct((K,) + got.shape[1:], got.dtype),
        in_specs=[pl.BlockSpec(memory_space=pltpu.SMEM), pl.BlockSpec(memory_space=pltpu.HBM)],
        out_specs=pl.BlockSpec(memory_space=pltpu.VMEM),
        scratch_shapes=[pltpu.SemaphoreType.DMA],
        compiler_params=pltpu.CompilerParams(vmem_limit_bytes=40 << 20),
        name="hand",
    )(tab, got)


def pack_whole_kernel(tab_ref, own_ref, out_ref):
    out_ref[...] = own_ref[...]


def pack_whole(tab, own):
    block = (GR,) + own.shape[1:]
    return pl.pallas_call(
        pack_whole_kernel,
        grid_spec=pltpu.PrefetchScalarGridSpec(
            num_scalar_prefetch=1,
            grid=(N,),
            in_specs=[pl.BlockSpec(block, lambda i, tab: (tab[R_SEND, i], 0, 0))],
            out_specs=pl.BlockSpec(block, lambda i, tab: (i, 0, 0)),
        ),
        out_shape=jax.ShapeDtypeStruct((N * GR,) + own.shape[1:], own.dtype),
        name="pack_whole",
    )(tab, own)


def place_kernel(c2, me_ref, tab_ref, loc_ref):
    me = me_ref[0]
    order, counts, late_of = N * GR, N * GR + N, N * GR + 2 * N

    def clear(s, _):
        loc_ref[late_of + s] = 0
        if c2 == 0:
            for g in range(GR):
                loc_ref[s * GR + g] = s * GR + g
        return 0

    lax.fori_loop(0, N, clear, 0)

    def find(s, handed):
        w = tab_ref[R_F1COL, s]
        filled = C1 - (w & 3)
        for k in range(C1):
            code = w >> (2 + 12 * k)

            @pl.when((k < filled) & (((code >> 3) & 0xFF) == me) & (s != me))
            def _():
                loc_ref[(s ^ ((code >> 11) & 1)) * GR + (code & 7)] = s * C1 + k

        w = tab_ref[R_F1COLM, s]
        for k in range(C1):
            code = w >> (2 + 12 * k)
            handed_here = (code >> 10) & 1

            @pl.when(handed_here == 1)
            def _():
                loc_ref[s * GR + (code & 7)] = (C1 + c2) * N + handed
                loc_ref[late_of + s] = 1

            handed = handed + handed_here

        w = tab_ref[R_F2COL, s]
        filled = c2 - (w & 3)
        for k in range(c2):
            code = w >> (2 + 14 * k)
            kind = code & 3
            origin = jnp.where(kind >= 2, (code >> 6) & (N - 1), s ^ (kind & 1))

            @pl.when((k < filled) & (s != me))
            def _():
                loc_ref[origin * GR + ((code >> 2) & 7)] = C1 * N + s * c2 + k
                loc_ref[late_of + origin] = 1

        return handed

    if c2 > 0:
        lax.fori_loop(0, N, find, jnp.int32(0))

    def sort(s, c):
        early, late = c
        is_live = (tab_ref[R_GIN, s] > 0).astype(jnp.int32)
        is_late = loc_ref[late_of + s]

        @pl.when(is_live == 1)
        def _():
            loc_ref[order + jnp.where(is_late == 1, N - 1 - late, early)] = s

        return early + is_live * (1 - is_late), late + is_live * is_late

    early, late = lax.fori_loop(0, N, sort, (jnp.int32(0), jnp.int32(0)))
    loc_ref[counts] = early
    loc_ref[counts + 1] = late


def place(c2, me, tab):
    return pl.pallas_call(
        functools.partial(place_kernel, c2),
        out_shape=jax.ShapeDtypeStruct((N * GR + 3 * N,), jnp.int32),
        in_specs=[pl.BlockSpec(memory_space=pltpu.SMEM)] * 2,
        out_specs=pl.BlockSpec(memory_space=pltpu.SMEM),
        name="place",
    )(me, tab)


def best_of(row, col, len_in, len_own, incoming, own_t):
    scale = 1.0 / jnp.sqrt(jnp.float32(own_t.shape[0]))
    score = jnp.dot(incoming, own_t, preferred_element_type=jnp.float32) * scale
    in_count = len_in.astype(jnp.float32)
    real_in = row < len_in
    real_own = col < len_own
    over_own = jnp.sum(jnp.where(real_own, score, 0.0), 1, keepdims=True) / len_own.astype(jnp.float32)
    over_in = jnp.sum(jnp.where(real_in, score, 0.0), 0, keepdims=True) / in_count
    grand = jnp.sum(jnp.where(real_in[:, :1], over_own, 0.0), 0, keepdims=True) / in_count
    own_best = jnp.max(jnp.where(real_in, score - over_own, lowest), 0, keepdims=True) - over_in + grand
    in_best = jnp.max(jnp.where(real_own, score - over_in, lowest), 1, keepdims=True) - over_own + grand
    return own_best, in_best


def match_kernel(late, ends, tab_ref, loc_ref, lens_ref, own_t_ref, best0_ref, ret0_ref, *refs):
    gots, (best_ref, ret_ref, buf, sem) = refs[: len(ends)], refs[len(ends) :]
    width = own_t_ref.shape[1]
    best_ref[...] = best0_ref[...]
    ret_ref[...] = ret0_ref[...]
    count = loc_ref[N * GR + N + int(late)]

    def sender(i):
        return loc_ref[N * GR + (N - 1 - i if late else i)]

    def fetch(i):
        @pl.when(i < count)
        def _():
            s = sender(i)
            slot = i & (DEPTH - 1)
            granules = tab_ref[R_GIN, s]
            for g in range(GR):

                @pl.when(g < granules)
                def _():
                    at = loc_ref[s * GR + g]
                    start = 0
                    for got_ref, end in zip(gots, ends):

                        @pl.when((at >= start) & (at < end))
                        def _(got_ref=got_ref, start=start):
                            pltpu.make_async_copy(
                                got_ref.at[at - start], buf.at[slot, g], sem.at[slot, g]
                            ).start()

                        start = end

    def arrive(i):
        @pl.when(i < count)
        def _():
            s = sender(i)
            slot = i & (DEPTH - 1)
            granules = tab_ref[R_GIN, s]
            for g in range(GR):

                @pl.when(g < granules)
                def _():
                    pltpu.make_async_copy(gots[0].at[0], buf.at[slot, g], sem.at[slot, g]).wait()

    for i in range(DEPTH - GROUP):
        fetch(i)
    row = lax.broadcasted_iota(jnp.int32, (N, N), 0)
    col = lax.broadcasted_iota(jnp.int32, (N, N), 1)

    def body(j, _):
        first = j * GROUP
        for u in range(GROUP):
            fetch(first + u + DEPTH - GROUP)
        for u in range(GROUP):
            arrive(first + u)
        found = []
        for u in range(GROUP):
            i = jnp.minimum(first + u, count - 1)
            s = sender(i)
            p = tab_ref[R_OWN, s]
            incoming = buf[i & (DEPTH - 1)].reshape(N, width)
            found.append((s, p) + best_of(
                row, col, tab_ref[R_LIN, s], lens_ref[p], incoming, own_t_ref[p]
            ))
        ret = ret_ref[...]
        for s, p, own_best, in_best in found:
            best_ref[pl.ds(p, 1), :] = jnp.maximum(best_ref[pl.ds(p, 1), :], own_best)
            ret = jnp.where(col == s, in_best, ret)
        ret_ref[...] = ret
        return 0

    lax.fori_loop(0, (count + GROUP - 1) // GROUP, body, 0)
    if late:
        ret_ref[...] = ret_ref[...].T


def match(late, tab, loc, lens, own_t, best, ret, *gots):
    ends = []
    for got in gots:
        ends.append((ends[-1] if ends else 0) + got.shape[0])
    return pl.pallas_call(
        functools.partial(match_kernel, late, tuple(ends)),
        out_shape=[jax.ShapeDtypeStruct(x.shape, x.dtype) for x in (best, ret)],
        in_specs=[pl.BlockSpec(memory_space=pltpu.SMEM)] * 3
        + [pl.BlockSpec(memory_space=pltpu.VMEM)] * 3
        + [pl.BlockSpec(memory_space=pltpu.HBM)] * len(gots),
        out_specs=[pl.BlockSpec(memory_space=pltpu.VMEM)] * 2,
        scratch_shapes=[
            pltpu.VMEM((DEPTH, GR, 16, own_t.shape[1]), own_t.dtype),
            pltpu.SemaphoreType.DMA((DEPTH, GR)),
        ],
        compiler_params=pltpu.CompilerParams(vmem_limit_bytes=40 << 20),
        name="match_late" if late else "match_early",
    )(tab, loc, lens, own_t, best, ret, *gots)


def near_kernel(late, ends, tab_ref, loc_ref, lens_ref, own_t_ref, best0_ref, ret0_ref, *refs):
    gots, (best_ref, ret_ref, buf) = refs[: len(ends)], refs[len(ends) :]
    width = own_t_ref.shape[1]
    best_ref[...] = best0_ref[...]
    ret_ref[...] = ret0_ref[...]
    count = loc_ref[N * GR + N + int(late)]

    def sender(i):
        i = jnp.minimum(i, count - 1)
        return loc_ref[N * GR + (N - 1 - i if late else i)]

    def gather(i, u):
        s = sender(i)
        granules = tab_ref[R_GIN, s]
        for g in range(GR):

            @pl.when(g < granules)
            def _():
                at = loc_ref[s * GR + g]
                start = 0
                for got_ref, end in zip(gots, ends):

                    @pl.when((at >= start) & (at < end))
                    def _(got_ref=got_ref, start=start):
                        buf[u, g] = got_ref[at - start]

                    start = end

    row = lax.broadcasted_iota(jnp.int32, (N, N), 0)
    col = lax.broadcasted_iota(jnp.int32, (N, N), 1)

    def body(j, _):
        first = j * GROUP
        for u in range(GROUP):
            gather(first + u, u)
        found = []
        for u in range(GROUP):
            s = sender(first + u)
            p = tab_ref[R_OWN, s]
            found.append((s, p) + best_of(
                row, col, tab_ref[R_LIN, s], lens_ref[p], buf[u].reshape(N, width), own_t_ref[p]
            ))
        ret = ret_ref[...]
        for s, p, own_best, in_best in found:
            best_ref[pl.ds(p, 1), :] = jnp.maximum(best_ref[pl.ds(p, 1), :], own_best)
            ret = jnp.where(col == s, in_best, ret)
        ret_ref[...] = ret
        return 0

    lax.fori_loop(0, (count + GROUP - 1) // GROUP, body, 0)
    if late:
        ret_ref[...] = ret_ref[...].T


def near(late, tab, loc, lens, own_t, best, ret, *gots):
    ends = []
    for got in gots:
        ends.append((ends[-1] if ends else 0) + got.shape[0])
    return pl.pallas_call(
        functools.partial(near_kernel, late, tuple(ends)),
        out_shape=[jax.ShapeDtypeStruct(x.shape, x.dtype) for x in (best, ret)],
        in_specs=[pl.BlockSpec(memory_space=pltpu.SMEM)] * 3
        + [pl.BlockSpec(memory_space=pltpu.VMEM)] * (3 + len(gots)),
        out_specs=[pl.BlockSpec(memory_space=pltpu.VMEM)] * 2,
        scratch_shapes=[pltpu.VMEM((GROUP, GR, 16, own_t.shape[1]), own_t.dtype)],
        compiler_params=pltpu.CompilerParams(vmem_limit_bytes=40 << 20),
        name="near_late" if late else "near_early",
    )(tab, loc, lens, own_t, best, ret, *gots)


def centred(score_matrix, row_validity_mask, col_mask):
    row_count = jnp.sum(row_validity_mask, -1)
    col_count = jnp.sum(col_mask, -1)
    row_mean = jnp.sum(score_matrix * col_mask[..., None, :], -1) / col_count[..., None]
    col_mean = jnp.sum(score_matrix * row_validity_mask[..., :, None], -2) / row_count[..., None]
    grand_mean = jnp.sum(row_mean * row_validity_mask, -1) / row_count
    return (
        score_matrix - row_mean[..., :, None] - col_mean[..., None, :] + grand_mean[..., None, None]
    )


def within_cluster(embeddings, masks):
    proteins_here, slots, width = embeddings.shape
    inverse_square_root = 1.0 / jnp.sqrt(jnp.float32(width))
    block_size = 8
    block_count = proteins_here // block_size

    def one_block(block_start):
        block_rows = lax.dynamic_slice_in_dim(embeddings, block_start, block_size, 0)
        block_mask = lax.dynamic_slice_in_dim(masks, block_start, block_size, 0)
        score_matrix = (
            jnp.einsum("bie,qje->bqij", block_rows, embeddings, preferred_element_type=jnp.float32)
            * inverse_square_root
        )
        cent = centred(score_matrix, block_mask[:, None, :], masks[None, :, :])
        row_max = jnp.max(jnp.where(masks[None, :, None, :] > 0, cent, lowest), -1)
        self_pair = (block_start + jnp.arange(block_size))[:, None] == jnp.arange(proteins_here)[
            None, :
        ]
        row_max = jnp.where(self_pair[:, :, None], lowest, row_max)
        best_match = jnp.max(row_max, 1)
        return jnp.where(block_mask > 0, best_match, 0.0)

    start_offsets = jnp.arange(block_count) * block_size
    return lax.map(one_block, start_offsets).reshape(proteins_here, slots)


def exchange(x):
    return lax.all_to_all(x, "shard", split_axis=0, concat_axis=0, tiled=True)


def other_core(x):
    return lax.ppermute(x, "shard", [(d, d ^ 1) for d in range(N)])


def per_device(embeddings, lengths, requests, query_local):
    proteins_here, slots, width = embeddings.shape
    masks = (jnp.arange(slots)[None, :] < lengths[:, None]).astype(jnp.float32)
    me = lax.axis_index("shard").astype(jnp.int32)[None]
    plan = jnp.concatenate([requests, query_local, lengths[None, :]], 1)
    plan = jnp.pad(plan, ((0, 0), (0, 3 * N - plan.shape[1])))
    plan = exchange(jnp.broadcast_to(plan, (N, 3 * N)))
    own = embeddings.reshape(proteins_here * GR, 16, width)

    mate = other_core(own)
    none_own = jnp.full((proteins_here, slots), lowest, jnp.float32)
    none_in = jnp.full((N, slots), lowest, jnp.float32)

    def finish(tab, best, ret, local_best):
        returned = exchange(ret)
        mine = (tab[R_SEND][None, :] == jnp.arange(proteins_here)[:, None]) & (tab[R_GOUT] > 0)[None, :]
        from_ret = jnp.max(jnp.where(mine[:, :, None], returned[None, :, :], lowest), 1)
        best = jnp.maximum(from_ret, best)
        cross_best = jnp.where((masks > 0) & (best > -1e29), best, 0.0)
        return local_best, cross_best

    def packed(c2, tab):
        loc = place(c2, me, tab)
        got1 = exchange(pack1(tab, own, mate))
        local_best = within_cluster(embeddings, masks)
        rows, local_best = lax.optimization_barrier((embeddings, local_best))
        own_t = jnp.swapaxes(rows, 1, 2)
        got1, local_best, own_t = lax.optimization_barrier((got1, local_best, own_t))
        send2 = pack2(c2, tab, own, mate, got1)
        send2, got1 = lax.optimization_barrier((send2, got1))
        got2 = exchange(send2)
        handed = other_core(hand(tab, got1))
        best, ret = near(False, tab, loc, lengths, own_t, none_own, none_in, got1)
        best, ret, got2 = lax.optimization_barrier((best, ret, got2))
        best, ret = near(True, tab, loc, lengths, own_t, best, ret, got1, got2, handed)
        return finish(tab, best, ret, local_best)

    def whole(tab):
        loc = place(0, me, tab)
        got = exchange(pack_whole(tab, own))
        own_t = jnp.swapaxes(embeddings, 1, 2)
        local_best = within_cluster(embeddings, masks)
        best, ret = match(False, tab, loc, lengths, own_t, none_own, none_in, got)
        best, ret = match(True, tab, loc, lengths, own_t, best, ret, got)
        return finish(tab, best, ret, local_best)

    def second(_):
        tab, left = route(2, me, plan)
        return lax.cond(left[0] == 0, functools.partial(packed, 2), whole, tab)

    tab, left = route(1, me, plan)
    return lax.cond(left[0] == 0, functools.partial(packed, 1), second, tab)


def solution(mesh):
    placed = (P("shard", None, None), P("shard"), P("shard", None), P("shard", None))
    return jax.shard_map(
        per_device,
        mesh=mesh,
        in_specs=placed,
        out_specs=(P("shard", None), P("shard", None)),
        check_vma=False,
    )
```

```python
import functools

import jax
import jax.numpy as jnp
from jax import lax
from jax.experimental import pallas as pl
from jax.experimental.pallas import tpu as pltpu
from jax.sharding import PartitionSpec as P

lowest = -1e30
N = 128
GR = 8
C1 = 2
K = 64
DEPTH = 16
GROUP = 4
TRIES = 6

R_F1ROW, R_F1COL, R_F1COLM, R_F2ROW, R_F2COL, R_SEND, R_SENDM, R_GIN, R_LIN, R_OWN, R_GOUT = range(11)


def swap_rows(x, s):
    return jnp.where((s & 1) == 0, pltpu.roll(x, N - 1, 0), pltpu.roll(x, 1, 0))


def swap_cols(x, r):
    return jnp.where((r & 1) == 0, pltpu.roll(x, N - 1, 1), pltpu.roll(x, 1, 1))


def skew(x, by, axis, sign):
    for b in range(7):
        shift = (1 << b) if sign > 0 else N - (1 << b)
        x = jnp.where(((by >> b) & 1) == 1, pltpu.roll(x, shift, axis), x)
    return x


def before(x, s):
    total = x
    for b in range(7):
        total = total + jnp.where(s >= (1 << b), pltpu.roll(total, 1 << b, 0), 0)
    return total - x


def route_kernel(c2, me_ref, plan_ref, tab_ref, left_ref, tmp_ref, first_ref):
    s = lax.broadcasted_iota(jnp.int32, (N, N), 0)
    r = lax.broadcasted_iota(jnp.int32, (N, N), 1)
    req = plan_ref[:, :N]
    q = plan_ref[:, N : 2 * N]
    lens = plan_ref[:, 2 * N :]
    lens_t = lens.T
    live = (req >= 0).astype(jnp.int32)
    req = jnp.maximum(req, 0)
    la = jnp.zeros((N, N), jnp.int32)
    lb = jnp.zeros((N, N), jnp.int32)
    for p in range(16):
        la = jnp.where(q == p, lens[:, p : p + 1], la)
        lb = jnp.where(req == p, lens_t[p : p + 1, :], lb)
    la = la * live
    lb = lb * live
    lb_t = lb.T
    ga = (la + 15) >> 4
    gb = (lb + 15) >> 4
    ga_t = ga.T
    gb_t = gb.T
    anti = live - live.T
    base = 1000 * (gb + gb_t - ga - ga_t) + jnp.where(((s + r) & 1) == 0, 250, -250)
    score = base
    bias_col = jnp.zeros((N, 1), jnp.int32)
    bias_row = jnp.zeros((1, N), jnp.int32)
    for eta in (10, 6, 4):
        gets = score < 0
        net = jnp.where(gets, gb_t, ga) - jnp.where(gets, gb, ga_t)
        bias_row = bias_row + eta * jnp.sum(net, axis=0, keepdims=True)
        bias_col = bias_col - eta * jnp.sum(net, axis=1, keepdims=True)
        score = base + anti * (bias_col - bias_row)
    lister_gets = score < 0
    lin = jnp.where(lister_gets, lb_t, la)
    psend = jnp.where(lister_gets, req.T, q)
    pown = jnp.where(lister_gets, q.T, req)
    m_tot = (lin + 15) >> 4

    diag = s == r
    free1 = jnp.where(diag, 0, C1)
    n = jnp.minimum(m_tot, free1)
    rem = m_tot - n
    w1 = free1 - n
    for k in range(C1):
        w1 = w1 | jnp.where(k < n, ((r << 3) | k) << (2 + 12 * k), 0)
    m_swap = swap_rows(m_tot, s)
    rem_s = swap_rows(rem, s)
    used = C1 - (w1 & 3)
    n = jnp.where(diag, 0, jnp.minimum(rem_s, w1 & 3))
    w1 = w1 - n
    for k in range(C1):
        code = (1 << 11) | (r << 3) | (m_swap - rem_s + k - used)
        w1 = w1 | jnp.where((k >= used) & (k < used + n), code << (2 + 12 * k), 0)
    rem = swap_rows(rem_s - n, s)
    free2 = jnp.where(diag, 0, c2)
    g_from = m_tot - rem
    n = jnp.minimum(rem, free2)
    rem = rem - n
    w2 = free2 - n
    for k in range(c2):
        w2 = w2 | jnp.where(k < n, ((g_from + k) << 2) << (2 + 14 * k), 0)
    rem_s = swap_rows(rem, s)
    used = c2 - (w2 & 3)
    n = jnp.where(diag, 0, jnp.minimum(rem_s, w2 & 3))
    w2 = w2 - n
    for k in range(c2):
        code = 1 | ((m_swap - rem_s + k - used) << 2)
        w2 = w2 | jnp.where((k >= used) & (k < used + n), code << (2 + 14 * k), 0)
    rem = swap_rows(rem_s - n, s)
    rem_c = swap_cols(rem, r)
    g_from = swap_cols(m_tot, r) - rem_c
    used = C1 - (w1 & 3)
    n = jnp.where(diag, 0, jnp.minimum(rem_c, w1 & 3))
    n = jnp.maximum(jnp.minimum(n, K - before(n, s)), 0)
    w1 = w1 - n
    for k in range(C1):
        code = (1 << 10) | ((r ^ 1) << 3) | (g_from + k - used)
        w1 = w1 | jnp.where((k >= used) & (k < used + n), code << (2 + 12 * k), 0)
    rem = swap_cols(rem_c - n, r)

    w1 = skew(w1, s, 1, -1)
    w2 = skew(w2, r, 0, -1)

    last = m_tot - 1
    kept2 = ((s << 6) | 2) << 2

    def step(limit, w1, w2, g):
        f1 = w1 & 3
        f2 = w2 & 3
        ok = (jnp.minimum(f1, f2) > 0) & (g <= limit)
        first = f1 == C1
        at = g << 2
        code1 = (r << 5) | at
        w1_new = w1 + jnp.where(first, code1, code1 << 12) - 1
        code2 = kept2 + (at << 2) + jnp.where(first, 0, 1 << 7)
        if c2 > 1:
            code2 = jnp.where(f2 == c2, code2, code2 << 14)
        w2_new = w2 + code2 - 1
        w1 = jnp.where(ok, w1_new, w1)
        w2 = jnp.where(ok, w2_new, w2)
        g = jnp.where(ok, g + 1, g)
        return pltpu.roll(w1, N - 1, 1), pltpu.roll(w2, N - 1, 0), g

    first_ref[0] = w1
    first_ref[1] = w2
    first_ref[2] = m_tot - rem

    def sweep(limit, turns, w1, w2, g):
        def body(c):
            i, _, w1, w2, g = c
            for _ in range(8):
                w1, w2, g = step(limit, w1, w2, g)
            return i + 1, jnp.max(limit - g), w1, w2, g

        i, most, w1, w2, g = lax.while_loop(
            lambda c: (c[0] < N // 8) & (c[1] >= 0),
            body,
            (jnp.int32(0), jnp.max(limit - g), w1, w2, g),
        )
        return most, turns + 8 * i, w1, w2, g

    def attempt(c):
        tries, _, _, _, _, urgent = c
        limit = jnp.where(urgent > 0, last, -1)
        _, turns, w1, w2, g = sweep(limit, 0, first_ref[0], first_ref[1], first_ref[2])
        most, turns, w1, w2, g = sweep(last, turns, w1, w2, g)
        return tries + 1, most + 1, turns, w1, w2, jnp.where(g <= last, 1, urgent)

    _, left, turns, w1, w2, _ = lax.while_loop(
        lambda c: (c[0] < TRIES) & (c[1] > 0),
        attempt,
        (jnp.int32(0), jnp.int32(1), jnp.int32(0), w1, w2, jnp.zeros((N, N), jnp.int32)),
    )
    turns = turns & (N - 1)
    w1 = skew(pltpu.roll(w1, turns, 1), s, 1, 1)
    w2 = skew(pltpu.roll(w2, turns, 0), r, 0, 1)

    me = me_ref[0]
    mate = me ^ 1

    def put(x, *rows):
        tmp_ref[...] = x
        for row, at in rows:
            tab_ref[row : row + 1, :] = tmp_ref[pl.ds(at, 1), :]

    put(w1, (R_F1ROW, me))
    put(w1.T, (R_F1COL, me), (R_F1COLM, mate))
    put(w2, (R_F2ROW, me))
    put(w2.T, (R_F2COL, me))
    put(psend, (R_SEND, me), (R_SENDM, mate))
    put(m_tot.T, (R_GIN, me))
    put(lin.T, (R_LIN, me))
    put(pown.T, (R_OWN, me))
    left_ref[0] = left
    put(m_tot, (R_GOUT, me))
    tab_ref[R_GOUT + 1 :, :] = jnp.zeros((16 - R_GOUT - 1, N), jnp.int32)


def route(c2, me, plan):
    return pl.pallas_call(
        functools.partial(route_kernel, c2),
        out_shape=[jax.ShapeDtypeStruct((16, N), jnp.int32), jax.ShapeDtypeStruct((1,), jnp.int32)],
        in_specs=[pl.BlockSpec(memory_space=pltpu.SMEM), pl.BlockSpec(memory_space=pltpu.VMEM)],
        out_specs=[pl.BlockSpec(memory_space=pltpu.VMEM), pl.BlockSpec(memory_space=pltpu.SMEM)],
        scratch_shapes=[pltpu.VMEM((N, N), jnp.int32), pltpu.VMEM((3, N, N), jnp.int32)],
        compiler_params=pltpu.CompilerParams(vmem_limit_bytes=32 << 20),
        name=f"route{c2}",
    )(me, plan)


def pack1_kernel(tab_ref, own_ref, mate_ref, out_ref, buf, in_sem, out_sem):
    parts = out_sem.shape[0]
    each = N // parts

    def piece(ref, part):
        return ref.at[pl.ds(part * each * C1, each * C1)]

    def codes(j):
        w = tab_ref[R_F1ROW, j]
        return [(k, w >> (2 + 12 * k)) for k in range(C1)]

    def from_mate(part, j, k, code):
        at = tab_ref[R_SENDM, (code >> 3) & (N - 1)] * GR + (code & 7)
        return pltpu.make_async_copy(mate_ref.at[at], buf.at[j * C1 + k], in_sem.at[part])

    def fill(part):
        def start(j, count):
            for k, code in codes(j):
                is_mate = (code >> 11) & 1

                @pl.when(is_mate == 1)
                def _():
                    from_mate(part, j, k, code).start()

                @pl.when(is_mate == 0)
                def _():
                    at = tab_ref[R_SEND, (code >> 3) & (N - 1)] * GR + (code & 7)
                    buf[j * C1 + k] = own_ref[at]

                count = count + is_mate
            return count

        return lax.fori_loop(part * each, (part + 1) * each, start, jnp.int32(0), unroll=4)

    def send(part, count):
        def finish(i, _):
            pltpu.make_async_copy(mate_ref.at[0], buf.at[0], in_sem.at[part]).wait()
            return 0

        lax.fori_loop(0, count, finish, 0)
        pltpu.make_async_copy(piece(buf, part), piece(out_ref, part), out_sem.at[part]).start()

    counts = []
    for part in range(parts):
        counts.append(fill(part))
        if part >= 2:
            send(part - 2, counts[part - 2])
    for part in range(parts - 2, parts):
        send(part, counts[part])
    for part in range(parts):
        pltpu.make_async_copy(piece(buf, part), piece(out_ref, part), out_sem.at[part]).wait()


def pack1(tab, own, mate):
    parts = 8
    shape = (N * C1,) + own.shape[1:]
    return pl.pallas_call(
        pack1_kernel,
        out_shape=pltpu.HBM(shape, own.dtype),
        in_specs=[
            pl.BlockSpec(memory_space=pltpu.SMEM),
            pl.BlockSpec(memory_space=pltpu.VMEM),
            pl.BlockSpec(memory_space=pltpu.HBM),
        ],
        out_specs=pl.BlockSpec(memory_space=pltpu.HBM),
        scratch_shapes=[
            pltpu.VMEM(shape, own.dtype),
            pltpu.SemaphoreType.DMA((parts,)),
            pltpu.SemaphoreType.DMA((parts,)),
        ],
        compiler_params=pltpu.CompilerParams(vmem_limit_bytes=24 << 20),
        name="pack1",
    )(tab, own, pltpu.with_memory_space_constraint(mate, pltpu.HBM))


def pack2_kernel(c2, tab_ref, own_ref, mate_ref, got_ref, out_ref, buf, in_sem, out_sem):
    parts = in_sem.shape[0]
    each = N // parts

    def fetch(part):
        def body(j, count):
            to = part * each + j
            w = tab_ref[R_F2ROW, to]
            filled = c2 - (w & 3)
            for k in range(c2):
                code = w >> (2 + 14 * k)
                kind = code & 3
                g = (code >> 2) & 7
                slot = ((code >> 6) & (N - 1)) * C1 + ((code >> 5) & 1)
                dst = buf.at[to * c2 + k]

                @pl.when((k < filled) & (kind == 0))
                def _():
                    src = own_ref.at[tab_ref[R_SEND, to] * GR + g]
                    pltpu.make_async_copy(src, dst, in_sem.at[part]).start()

                @pl.when((k < filled) & (kind == 1))
                def _():
                    src = mate_ref.at[tab_ref[R_SENDM, to] * GR + g]
                    pltpu.make_async_copy(src, dst, in_sem.at[part]).start()

                @pl.when((k < filled) & (kind >= 2))
                def _():
                    pltpu.make_async_copy(got_ref.at[slot], dst, in_sem.at[part]).start()

            return count + filled

        return lax.fori_loop(0, each, body, jnp.int32(0), unroll=4)

    def piece(ref, part):
        return ref.at[pl.ds(part * each * c2, each * c2)]

    counts = [fetch(part) for part in range(parts)]
    for part in range(parts):

        def arrive(i, _, part=part):
            pltpu.make_async_copy(own_ref.at[0], buf.at[0], in_sem.at[part]).wait()
            return 0

        lax.fori_loop(0, counts[part], arrive, 0)
        pltpu.make_async_copy(piece(buf, part), piece(out_ref, part), out_sem.at[part]).start()
    for part in range(parts):
        pltpu.make_async_copy(piece(buf, part), piece(out_ref, part), out_sem.at[part]).wait()


def pack2(c2, tab, own, mate, got):
    parts = 4
    shape = (N * c2,) + own.shape[1:]
    return pl.pallas_call(
        functools.partial(pack2_kernel, c2),
        out_shape=pltpu.HBM(shape, own.dtype),
        in_specs=[pl.BlockSpec(memory_space=pltpu.SMEM)] + [pl.BlockSpec(memory_space=pltpu.HBM)] * 3,
        out_specs=pl.BlockSpec(memory_space=pltpu.HBM),
        scratch_shapes=[
            pltpu.VMEM(shape, own.dtype),
            pltpu.SemaphoreType.DMA((parts,)),
            pltpu.SemaphoreType.DMA((parts,)),
        ],
        compiler_params=pltpu.CompilerParams(vmem_limit_bytes=40 << 20),
        name="pack2",
    )(tab, *(pltpu.with_memory_space_constraint(x, pltpu.HBM) for x in (own, mate, got)))


def hand_kernel(tab_ref, got_ref, out_ref, sem):
    def body(s, count):
        w = tab_ref[R_F1COL, s]
        for k in range(C1):
            mine = (w >> (2 + 12 * k + 10)) & 1

            @pl.when(mine == 1)
            def _():
                pltpu.make_async_copy(got_ref.at[s * C1 + k], out_ref.at[count], sem).start()

            count = count + mine
        return count

    count = lax.fori_loop(0, N, body, jnp.int32(0))

    def fill(j, _):
        pltpu.make_async_copy(got_ref.at[0], out_ref.at[j], sem).start()
        return 0

    lax.fori_loop(count, K, fill, 0)
    pltpu.make_async_copy(out_ref, out_ref, sem).wait()


def hand(tab, got):
    return pl.pallas_call(
        hand_kernel,
        out_shape=jax.ShapeDtypeStruct((K,) + got.shape[1:], got.dtype),
        in_specs=[pl.BlockSpec(memory_space=pltpu.SMEM), pl.BlockSpec(memory_space=pltpu.HBM)],
        out_specs=pl.BlockSpec(memory_space=pltpu.VMEM),
        scratch_shapes=[pltpu.SemaphoreType.DMA],
        compiler_params=pltpu.CompilerParams(vmem_limit_bytes=40 << 20),
        name="hand",
    )(tab, got)


def pack_whole_kernel(tab_ref, own_ref, out_ref):
    out_ref[...] = own_ref[...]


def pack_whole(tab, own):
    block = (GR,) + own.shape[1:]
    return pl.pallas_call(
        pack_whole_kernel,
        grid_spec=pltpu.PrefetchScalarGridSpec(
            num_scalar_prefetch=1,
            grid=(N,),
            in_specs=[pl.BlockSpec(block, lambda i, tab: (tab[R_SEND, i], 0, 0))],
            out_specs=pl.BlockSpec(block, lambda i, tab: (i, 0, 0)),
        ),
        out_shape=jax.ShapeDtypeStruct((N * GR,) + own.shape[1:], own.dtype),
        name="pack_whole",
    )(tab, own)


def place_kernel(c2, me_ref, tab_ref, loc_ref):
    me = me_ref[0]
    order, counts, late_of = N * GR, N * GR + N, N * GR + 2 * N

    def clear(s, _):
        loc_ref[late_of + s] = 0
        for g in range(GR):
            loc_ref[s * GR + g] = s * GR + g if c2 == 0 else 0
        return 0

    lax.fori_loop(0, N, clear, 0)

    def find(s, handed):
        w = tab_ref[R_F1COL, s]
        filled = C1 - (w & 3)
        for k in range(C1):
            code = w >> (2 + 12 * k)

            @pl.when((k < filled) & (((code >> 3) & 0xFF) == me) & (s != me))
            def _():
                loc_ref[(s ^ ((code >> 11) & 1)) * GR + (code & 7)] = s * C1 + k

        w = tab_ref[R_F1COLM, s]
        for k in range(C1):
            code = w >> (2 + 12 * k)
            handed_here = (code >> 10) & 1

            @pl.when(handed_here == 1)
            def _():
                loc_ref[s * GR + (code & 7)] = (C1 + c2) * N + handed
                loc_ref[late_of + s] = 1

            handed = handed + handed_here

        w = tab_ref[R_F2COL, s]
        filled = c2 - (w & 3)
        for k in range(c2):
            code = w >> (2 + 14 * k)
            kind = code & 3
            origin = jnp.where(kind >= 2, (code >> 6) & (N - 1), s ^ (kind & 1))

            @pl.when((k < filled) & (s != me))
            def _():
                loc_ref[origin * GR + ((code >> 2) & 7)] = C1 * N + s * c2 + k
                loc_ref[late_of + origin] = 1

        return handed

    if c2 > 0:
        lax.fori_loop(0, N, find, jnp.int32(0))

    def sort(s, c):
        early, late = c
        is_live = (tab_ref[R_GIN, s] > 0).astype(jnp.int32)
        is_late = loc_ref[late_of + s]

        @pl.when(is_live == 1)
        def _():
            loc_ref[order + jnp.where(is_late == 1, N - 1 - late, early)] = s

        return early + is_live * (1 - is_late), late + is_live * is_late

    early, late = lax.fori_loop(0, N, sort, (jnp.int32(0), jnp.int32(0)))
    loc_ref[counts] = early
    loc_ref[counts + 1] = late


def place(c2, me, tab):
    return pl.pallas_call(
        functools.partial(place_kernel, c2),
        out_shape=jax.ShapeDtypeStruct((N * GR + 3 * N,), jnp.int32),
        in_specs=[pl.BlockSpec(memory_space=pltpu.SMEM)] * 2,
        out_specs=pl.BlockSpec(memory_space=pltpu.SMEM),
        name="place",
    )(me, tab)


def best_of(row, col, len_in, len_own, incoming, own_t):
    scale = 1.0 / jnp.sqrt(jnp.float32(own_t.shape[0]))
    score = jnp.dot(incoming, own_t, preferred_element_type=jnp.float32) * scale
    in_count = len_in.astype(jnp.float32)
    real_in = row < len_in
    real_own = col < len_own
    over_own = jnp.sum(jnp.where(real_own, score, 0.0), 1, keepdims=True) / len_own.astype(jnp.float32)
    over_in = jnp.sum(jnp.where(real_in, score, 0.0), 0, keepdims=True) / in_count
    grand = jnp.sum(jnp.where(real_in[:, :1], over_own, 0.0), 0, keepdims=True) / in_count
    own_best = jnp.max(jnp.where(real_in, score - over_own, lowest), 0, keepdims=True) - over_in + grand
    in_best = jnp.max(jnp.where(real_own, score - over_in, lowest), 1, keepdims=True) - over_own + grand
    return own_best, in_best


def match_kernel(late, ends, tab_ref, loc_ref, lens_ref, own_t_ref, best0_ref, ret0_ref, *refs):
    gots, (best_ref, ret_ref, buf, sem) = refs[: len(ends)], refs[len(ends) :]
    width = own_t_ref.shape[1]
    best_ref[...] = best0_ref[...]
    ret_ref[...] = ret0_ref[...]
    count = loc_ref[N * GR + N + int(late)]

    def sender(i):
        return loc_ref[N * GR + (N - 1 - i if late else i)]

    def fetch(i):
        @pl.when(i < count)
        def _():
            s = sender(i)
            slot = i & (DEPTH - 1)
            granules = tab_ref[R_GIN, s]
            for g in range(GR):

                @pl.when(g < granules)
                def _():
                    at = loc_ref[s * GR + g]
                    start = 0
                    for got_ref, end in zip(gots, ends):

                        @pl.when((at >= start) & (at < end))
                        def _(got_ref=got_ref, start=start):
                            pltpu.make_async_copy(
                                got_ref.at[at - start], buf.at[slot, g], sem.at[slot, g]
                            ).start()

                        start = end

    def arrive(i):
        @pl.when(i < count)
        def _():
            s = sender(i)
            slot = i & (DEPTH - 1)
            granules = tab_ref[R_GIN, s]
            for g in range(GR):

                @pl.when(g < granules)
                def _():
                    pltpu.make_async_copy(gots[0].at[0], buf.at[slot, g], sem.at[slot, g]).wait()

    for i in range(DEPTH - GROUP):
        fetch(i)
    row = lax.broadcasted_iota(jnp.int32, (N, N), 0)
    col = lax.broadcasted_iota(jnp.int32, (N, N), 1)

    def body(j, _):
        first = j * GROUP
        for u in range(GROUP):
            fetch(first + u + DEPTH - GROUP)
        for u in range(GROUP):
            arrive(first + u)
        found = []
        for u in range(GROUP):
            i = jnp.minimum(first + u, count - 1)
            s = sender(i)
            p = tab_ref[R_OWN, s]
            incoming = buf[i & (DEPTH - 1)].reshape(N, width)
            found.append((s, p) + best_of(
                row, col, tab_ref[R_LIN, s], lens_ref[p], incoming, own_t_ref[p]
            ))
        ret = ret_ref[...]
        for s, p, own_best, in_best in found:
            best_ref[pl.ds(p, 1), :] = jnp.maximum(best_ref[pl.ds(p, 1), :], own_best)
            ret = jnp.where(col == s, in_best, ret)
        ret_ref[...] = ret
        return 0

    lax.fori_loop(0, (count + GROUP - 1) // GROUP, body, 0)
    if late:
        ret_ref[...] = ret_ref[...].T


def match(late, tab, loc, lens, own_t, best, ret, *gots):
    ends = []
    for got in gots:
        ends.append((ends[-1] if ends else 0) + got.shape[0])
    return pl.pallas_call(
        functools.partial(match_kernel, late, tuple(ends)),
        out_shape=[jax.ShapeDtypeStruct(x.shape, x.dtype) for x in (best, ret)],
        in_specs=[pl.BlockSpec(memory_space=pltpu.SMEM)] * 3
        + [pl.BlockSpec(memory_space=pltpu.VMEM)] * 3
        + [pl.BlockSpec(memory_space=pltpu.HBM)] * len(gots),
        out_specs=[pl.BlockSpec(memory_space=pltpu.VMEM)] * 2,
        scratch_shapes=[
            pltpu.VMEM((DEPTH, GR, 16, own_t.shape[1]), own_t.dtype),
            pltpu.SemaphoreType.DMA((DEPTH, GR)),
        ],
        compiler_params=pltpu.CompilerParams(vmem_limit_bytes=40 << 20),
        name="match_late" if late else "match_early",
    )(tab, loc, lens, own_t, best, ret, *gots)


def near_kernel(late, tab_ref, loc_ref, lens_ref, own_t_hbm, best0_ref, ret0_ref, *refs):
    gots, (best_ref, ret_ref, own_t_ref, all_ref, buf, sem) = refs[:-6], refs[-6:]
    copies = [pltpu.make_async_copy(own_t_hbm, own_t_ref, sem.at[0])]
    start = 0
    for i, got in enumerate(gots):
        end = start + got.shape[0]
        copies.append(pltpu.make_async_copy(got, all_ref.at[pl.ds(start, end - start)], sem.at[i + 1]))
        start = end
    for copy in copies:
        copy.start()
    width = own_t_ref.shape[1]
    best_ref[...] = best0_ref[...]
    ret_ref[...] = ret0_ref[...]
    count = loc_ref[N * GR + N + int(late)]

    def sender(i):
        i = jnp.minimum(i, count - 1)
        return loc_ref[N * GR + (N - 1 - i if late else i)]

    def gather(i, u):
        s = sender(i)
        for g in range(GR):
            buf[u, g] = all_ref[loc_ref[s * GR + g]]

    for copy in copies:
        copy.wait()
    row = lax.broadcasted_iota(jnp.int32, (N, N), 0)
    col = lax.broadcasted_iota(jnp.int32, (N, N), 1)

    def body(j, _):
        first = j * GROUP
        for u in range(GROUP):
            gather(first + u, u)
        found = []
        for u in range(GROUP):
            s = sender(first + u)
            p = tab_ref[R_OWN, s]
            found.append((s, p) + best_of(
                row, col, tab_ref[R_LIN, s], lens_ref[p], buf[u].reshape(N, width), own_t_ref[p]
            ))
        ret = ret_ref[...]
        for s, p, own_best, in_best in found:
            best_ref[pl.ds(p, 1), :] = jnp.maximum(best_ref[pl.ds(p, 1), :], own_best)
            ret = jnp.where(col == s, in_best, ret)
        ret_ref[...] = ret
        return 0

    lax.fori_loop(0, (count + GROUP - 1) // GROUP, body, 0)
    if late:
        ret_ref[...] = ret_ref[...].T


def near(late, tab, loc, lens, own_t, best, ret, *gots):
    total = sum(got.shape[0] for got in gots)
    far = [pltpu.with_memory_space_constraint(x, pltpu.HBM) for x in (own_t,) + gots]
    return pl.pallas_call(
        functools.partial(near_kernel, late),
        out_shape=[jax.ShapeDtypeStruct(x.shape, x.dtype) for x in (best, ret)],
        in_specs=[pl.BlockSpec(memory_space=pltpu.SMEM)] * 3
        + [pl.BlockSpec(memory_space=pltpu.HBM)]
        + [pl.BlockSpec(memory_space=pltpu.VMEM)] * 2
        + [pl.BlockSpec(memory_space=pltpu.HBM)] * len(gots),
        out_specs=[pl.BlockSpec(memory_space=pltpu.VMEM)] * 2,
        scratch_shapes=[
            pltpu.VMEM(own_t.shape, own_t.dtype),
            pltpu.VMEM((total,) + gots[0].shape[1:], own_t.dtype),
            pltpu.VMEM((GROUP, GR, 16, own_t.shape[1]), own_t.dtype),
            pltpu.SemaphoreType.DMA((1 + len(gots),)),
        ],
        compiler_params=pltpu.CompilerParams(vmem_limit_bytes=44 << 20),
        name="near_late" if late else "near_early",
    )(tab, loc, lens, far[0], best, ret, *far[1:])


def centred(score_matrix, row_validity_mask, col_mask):
    row_count = jnp.sum(row_validity_mask, -1)
    col_count = jnp.sum(col_mask, -1)
    row_mean = jnp.sum(score_matrix * col_mask[..., None, :], -1) / col_count[..., None]
    col_mean = jnp.sum(score_matrix * row_validity_mask[..., :, None], -2) / row_count[..., None]
    grand_mean = jnp.sum(row_mean * row_validity_mask, -1) / row_count
    return (
        score_matrix - row_mean[..., :, None] - col_mean[..., None, :] + grand_mean[..., None, None]
    )


def within_cluster(embeddings, masks):
    proteins_here, slots, width = embeddings.shape
    inverse_square_root = 1.0 / jnp.sqrt(jnp.float32(width))
    block_size = 8
    block_count = proteins_here // block_size

    def one_block(block_start):
        block_rows = lax.dynamic_slice_in_dim(embeddings, block_start, block_size, 0)
        block_mask = lax.dynamic_slice_in_dim(masks, block_start, block_size, 0)
        score_matrix = (
            jnp.einsum("bie,qje->bqij", block_rows, embeddings, preferred_element_type=jnp.float32)
            * inverse_square_root
        )
        cent = centred(score_matrix, block_mask[:, None, :], masks[None, :, :])
        row_max = jnp.max(jnp.where(masks[None, :, None, :] > 0, cent, lowest), -1)
        self_pair = (block_start + jnp.arange(block_size))[:, None] == jnp.arange(proteins_here)[
            None, :
        ]
        row_max = jnp.where(self_pair[:, :, None], lowest, row_max)
        best_match = jnp.max(row_max, 1)
        return jnp.where(block_mask > 0, best_match, 0.0)

    start_offsets = jnp.arange(block_count) * block_size
    return lax.map(one_block, start_offsets).reshape(proteins_here, slots)


def exchange(x):
    return lax.all_to_all(x, "shard", split_axis=0, concat_axis=0, tiled=True)


def other_core(x):
    return lax.ppermute(x, "shard", [(d, d ^ 1) for d in range(N)])


def per_device(embeddings, lengths, requests, query_local):
    proteins_here, slots, width = embeddings.shape
    masks = (jnp.arange(slots)[None, :] < lengths[:, None]).astype(jnp.float32)
    me = lax.axis_index("shard").astype(jnp.int32)[None]
    plan = jnp.concatenate([requests, query_local, lengths[None, :]], 1)
    plan = jnp.pad(plan, ((0, 0), (0, 3 * N - plan.shape[1])))
    plan = exchange(jnp.broadcast_to(plan, (N, 3 * N)))
    own = embeddings.reshape(proteins_here * GR, 16, width)

    mate = other_core(own)
    none_own = jnp.full((proteins_here, slots), lowest, jnp.float32)
    none_in = jnp.full((N, slots), lowest, jnp.float32)

    def finish(tab, best, ret, local_best):
        returned = exchange(ret)
        mine = (tab[R_SEND][None, :] == jnp.arange(proteins_here)[:, None]) & (tab[R_GOUT] > 0)[None, :]
        from_ret = jnp.max(jnp.where(mine[:, :, None], returned[None, :, :], lowest), 1)
        best = jnp.maximum(from_ret, best)
        cross_best = jnp.where((masks > 0) & (best > -1e29), best, 0.0)
        return local_best, cross_best

    def packed(c2, tab):
        loc = place(c2, me, tab)
        got1 = exchange(pack1(tab, own, mate))
        local_best = within_cluster(embeddings, masks)
        rows, local_best = lax.optimization_barrier((embeddings, local_best))
        own_t = jnp.swapaxes(rows, 1, 2)
        got1, local_best, own_t = lax.optimization_barrier((got1, local_best, own_t))
        send2 = pack2(c2, tab, own, mate, got1)
        send2, got1 = lax.optimization_barrier((send2, got1))
        got2 = exchange(send2)
        handed = other_core(hand(tab, got1))
        best, ret = near(False, tab, loc, lengths, own_t, none_own, none_in, got1)
        best, ret, got2 = lax.optimization_barrier((best, ret, got2))
        best, ret = near(True, tab, loc, lengths, own_t, best, ret, got1, got2, handed)
        return finish(tab, best, ret, local_best)

    def whole(tab):
        loc = place(0, me, tab)
        got = exchange(pack_whole(tab, own))
        own_t = jnp.swapaxes(embeddings, 1, 2)
        local_best = within_cluster(embeddings, masks)
        best, ret = match(False, tab, loc, lengths, own_t, none_own, none_in, got)
        best, ret = match(True, tab, loc, lengths, own_t, best, ret, got)
        return finish(tab, best, ret, local_best)

    def second(_):
        tab, left = route(2, me, plan)
        return lax.cond(left[0] == 0, functools.partial(packed, 2), whole, tab)

    tab, left = route(1, me, plan)
    return lax.cond(left[0] == 0, functools.partial(packed, 1), second, tab)


def solution(mesh):
    placed = (P("shard", None, None), P("shard"), P("shard", None), P("shard", None))
    return jax.shard_map(
        per_device,
        mesh=mesh,
        in_specs=placed,
        out_specs=(P("shard", None), P("shard", None)),
        check_vma=False,
    )
```

```python
import functools

import jax
import jax.numpy as jnp
from jax import lax
from jax.experimental import pallas as pl
from jax.experimental.pallas import tpu as pltpu
from jax.sharding import PartitionSpec as P

lowest = -1e30
N = 128
GR = 8
C1 = 2
K = 64
DEPTH = 16
GROUP = 4
PIECES = 4
TRIES = 6

R_F1ROW, R_F1COL, R_F1COLM, R_F2ROW, R_F2COL, R_SEND, R_SENDM, R_GIN, R_LIN, R_OWN, R_GOUT = range(11)


def swap_rows(x, s):
    return jnp.where((s & 1) == 0, pltpu.roll(x, N - 1, 0), pltpu.roll(x, 1, 0))


def swap_cols(x, r):
    return jnp.where((r & 1) == 0, pltpu.roll(x, N - 1, 1), pltpu.roll(x, 1, 1))


def skew(x, by, axis, sign):
    for b in range(7):
        shift = (1 << b) if sign > 0 else N - (1 << b)
        x = jnp.where(((by >> b) & 1) == 1, pltpu.roll(x, shift, axis), x)
    return x


def before(x, s):
    total = x
    for b in range(7):
        total = total + jnp.where(s >= (1 << b), pltpu.roll(total, 1 << b, 0), 0)
    return total - x


def route_kernel(c2, me_ref, plan_ref, tab_ref, left_ref, tmp_ref, first_ref):
    s = lax.broadcasted_iota(jnp.int32, (N, N), 0)
    r = lax.broadcasted_iota(jnp.int32, (N, N), 1)
    req = plan_ref[:, :N]
    q = plan_ref[:, N : 2 * N]
    lens = plan_ref[:, 2 * N :]
    lens_t = lens.T
    live = (req >= 0).astype(jnp.int32)
    req = jnp.maximum(req, 0)
    la = jnp.zeros((N, N), jnp.int32)
    lb = jnp.zeros((N, N), jnp.int32)
    for p in range(16):
        la = jnp.where(q == p, lens[:, p : p + 1], la)
        lb = jnp.where(req == p, lens_t[p : p + 1, :], lb)
    la = la * live
    lb = lb * live
    lb_t = lb.T
    ga = (la + 15) >> 4
    gb = (lb + 15) >> 4
    ga_t = ga.T
    gb_t = gb.T
    anti = live - live.T
    base = 1000 * (gb + gb_t - ga - ga_t) + jnp.where(((s + r) & 1) == 0, 250, -250)
    score = base
    bias_col = jnp.zeros((N, 1), jnp.int32)
    bias_row = jnp.zeros((1, N), jnp.int32)
    for eta in (10, 6, 4):
        gets = score < 0
        net = jnp.where(gets, gb_t, ga) - jnp.where(gets, gb, ga_t)
        bias_row = bias_row + eta * jnp.sum(net, axis=0, keepdims=True)
        bias_col = bias_col - eta * jnp.sum(net, axis=1, keepdims=True)
        score = base + anti * (bias_col - bias_row)
    lister_gets = score < 0
    lin = jnp.where(lister_gets, lb_t, la)
    psend = jnp.where(lister_gets, req.T, q)
    pown = jnp.where(lister_gets, q.T, req)
    m_tot = (lin + 15) >> 4

    diag = s == r
    free1 = jnp.where(diag, 0, C1)
    n = jnp.minimum(m_tot, free1)
    rem = m_tot - n
    w1 = free1 - n
    for k in range(C1):
        w1 = w1 | jnp.where(k < n, ((r << 3) | k) << (2 + 12 * k), 0)
    m_swap = swap_rows(m_tot, s)
    rem_s = swap_rows(rem, s)
    used = C1 - (w1 & 3)
    n = jnp.where(diag, 0, jnp.minimum(rem_s, w1 & 3))
    w1 = w1 - n
    for k in range(C1):
        code = (1 << 11) | (r << 3) | (m_swap - rem_s + k - used)
        w1 = w1 | jnp.where((k >= used) & (k < used + n), code << (2 + 12 * k), 0)
    rem = swap_rows(rem_s - n, s)
    free2 = jnp.where(diag, 0, c2)
    g_from = m_tot - rem
    n = jnp.minimum(rem, free2)
    rem = rem - n
    w2 = free2 - n
    for k in range(c2):
        w2 = w2 | jnp.where(k < n, ((g_from + k) << 2) << (2 + 14 * k), 0)
    rem_s = swap_rows(rem, s)
    used = c2 - (w2 & 3)
    n = jnp.where(diag, 0, jnp.minimum(rem_s, w2 & 3))
    w2 = w2 - n
    for k in range(c2):
        code = 1 | ((m_swap - rem_s + k - used) << 2)
        w2 = w2 | jnp.where((k >= used) & (k < used + n), code << (2 + 14 * k), 0)
    rem = swap_rows(rem_s - n, s)
    rem_c = swap_cols(rem, r)
    g_from = swap_cols(m_tot, r) - rem_c
    used = C1 - (w1 & 3)
    n = jnp.where(diag, 0, jnp.minimum(rem_c, w1 & 3))
    n = jnp.maximum(jnp.minimum(n, K - before(n, s)), 0)
    w1 = w1 - n
    for k in range(C1):
        code = (1 << 10) | ((r ^ 1) << 3) | (g_from + k - used)
        w1 = w1 | jnp.where((k >= used) & (k < used + n), code << (2 + 12 * k), 0)
    rem = swap_cols(rem_c - n, r)

    w1 = skew(w1, s, 1, -1)
    w2 = skew(w2, r, 0, -1)

    last = m_tot - 1
    kept2 = ((s << 6) | 2) << 2

    def step(limit, w1, w2, g):
        f1 = w1 & 3
        f2 = w2 & 3
        ok = (jnp.minimum(f1, f2) > 0) & (g <= limit)
        first = f1 == C1
        at = g << 2
        code1 = (r << 5) | at
        w1_new = w1 + jnp.where(first, code1, code1 << 12) - 1
        code2 = kept2 + (at << 2) + jnp.where(first, 0, 1 << 7)
        if c2 > 1:
            code2 = jnp.where(f2 == c2, code2, code2 << 14)
        w2_new = w2 + code2 - 1
        w1 = jnp.where(ok, w1_new, w1)
        w2 = jnp.where(ok, w2_new, w2)
        g = jnp.where(ok, g + 1, g)
        return pltpu.roll(w1, N - 1, 1), pltpu.roll(w2, N - 1, 0), g

    first_ref[0] = w1
    first_ref[1] = w2
    first_ref[2] = m_tot - rem

    def sweep(limit, turns, w1, w2, g):
        def body(c):
            i, _, w1, w2, g = c
            for _ in range(8):
                w1, w2, g = step(limit, w1, w2, g)
            return i + 1, jnp.max(limit - g), w1, w2, g

        i, most, w1, w2, g = lax.while_loop(
            lambda c: (c[0] < N // 8) & (c[1] >= 0),
            body,
            (jnp.int32(0), jnp.max(limit - g), w1, w2, g),
        )
        return most, turns + 8 * i, w1, w2, g

    def attempt(c):
        tries, _, _, _, _, urgent = c
        limit = jnp.where(urgent > 0, last, -1)
        _, turns, w1, w2, g = sweep(limit, 0, first_ref[0], first_ref[1], first_ref[2])
        most, turns, w1, w2, g = sweep(last, turns, w1, w2, g)
        return tries + 1, most + 1, turns, w1, w2, jnp.where(g <= last, 1, urgent)

    _, left, turns, w1, w2, _ = lax.while_loop(
        lambda c: (c[0] < TRIES) & (c[1] > 0),
        attempt,
        (jnp.int32(0), jnp.int32(1), jnp.int32(0), w1, w2, jnp.zeros((N, N), jnp.int32)),
    )
    turns = turns & (N - 1)
    w1 = skew(pltpu.roll(w1, turns, 1), s, 1, 1)
    w2 = skew(pltpu.roll(w2, turns, 0), r, 0, 1)

    me = me_ref[0]
    mate = me ^ 1

    def put(x, *rows):
        tmp_ref[...] = x
        for row, at in rows:
            tab_ref[row : row + 1, :] = tmp_ref[pl.ds(at, 1), :]

    put(w1, (R_F1ROW, me))
    put(w1.T, (R_F1COL, me), (R_F1COLM, mate))
    put(w2, (R_F2ROW, me))
    put(w2.T, (R_F2COL, me))
    put(psend, (R_SEND, me), (R_SENDM, mate))
    put(m_tot.T, (R_GIN, me))
    put(lin.T, (R_LIN, me))
    put(pown.T, (R_OWN, me))
    left_ref[0] = left
    put(m_tot, (R_GOUT, me))
    tab_ref[R_GOUT + 1 :, :] = jnp.zeros((16 - R_GOUT - 1, N), jnp.int32)


def route(c2, me, plan):
    return pl.pallas_call(
        functools.partial(route_kernel, c2),
        out_shape=[jax.ShapeDtypeStruct((16, N), jnp.int32), jax.ShapeDtypeStruct((1,), jnp.int32)],
        in_specs=[pl.BlockSpec(memory_space=pltpu.SMEM), pl.BlockSpec(memory_space=pltpu.VMEM)],
        out_specs=[pl.BlockSpec(memory_space=pltpu.VMEM), pl.BlockSpec(memory_space=pltpu.SMEM)],
        scratch_shapes=[pltpu.VMEM((N, N), jnp.int32), pltpu.VMEM((3, N, N), jnp.int32)],
        compiler_params=pltpu.CompilerParams(vmem_limit_bytes=32 << 20),
        name=f"route{c2}",
    )(me, plan)


def pack1_kernel(tab_ref, own_ref, mate_ref, out_ref, both, buf, in_sem, out_sem):
    parts = out_sem.shape[0]
    each = N // parts
    held = own_ref.shape[0]

    def piece(ref, part):
        return ref.at[pl.ds(part * each * C1, each * C1)]

    copies = [
        pltpu.make_async_copy(ref, both.at[pl.ds(i * held, held)], in_sem.at[i])
        for i, ref in enumerate((own_ref, mate_ref))
    ]
    for copy in copies:
        copy.start()
    for copy in copies:
        copy.wait()
    for part in range(parts):

        def body(j, _):
            w = tab_ref[R_F1ROW, j]
            for k in range(C1):
                code = w >> (2 + 12 * k)
                core = (code >> 11) & 1
                protein = tab_ref[R_SEND + core, (code >> 3) & (N - 1)]
                buf[j * C1 + k] = both[core * held + protein * GR + (code & 7)]
            return 0

        lax.fori_loop(part * each, (part + 1) * each, body, 0, unroll=8)
        pltpu.make_async_copy(piece(buf, part), piece(out_ref, part), out_sem.at[part]).start()
    for part in range(parts):
        pltpu.make_async_copy(piece(buf, part), piece(out_ref, part), out_sem.at[part]).wait()


def pack1(tab, own, mate):
    parts = 8
    shape = (N * C1,) + own.shape[1:]
    return pl.pallas_call(
        pack1_kernel,
        out_shape=pltpu.HBM(shape, own.dtype),
        in_specs=[pl.BlockSpec(memory_space=pltpu.SMEM)] + [pl.BlockSpec(memory_space=pltpu.HBM)] * 2,
        out_specs=pl.BlockSpec(memory_space=pltpu.HBM),
        scratch_shapes=[
            pltpu.VMEM((2 * own.shape[0],) + own.shape[1:], own.dtype),
            pltpu.VMEM(shape, own.dtype),
            pltpu.SemaphoreType.DMA((2,)),
            pltpu.SemaphoreType.DMA((parts,)),
        ],
        compiler_params=pltpu.CompilerParams(vmem_limit_bytes=40 << 20),
        name="pack1",
    )(tab, *(pltpu.with_memory_space_constraint(x, pltpu.HBM) for x in (own, mate)))


def pack2_kernel(c2, tab_ref, own_ref, mate_ref, got_ref, out_ref, buf, in_sem, out_sem):
    parts = in_sem.shape[0]
    each = N // parts

    def fetch(part):
        def body(j, count):
            to = part * each + j
            w = tab_ref[R_F2ROW, to]
            filled = c2 - (w & 3)
            for k in range(c2):
                code = w >> (2 + 14 * k)
                kind = code & 3
                g = (code >> 2) & 7
                slot = ((code >> 6) & (N - 1)) * C1 + ((code >> 5) & 1)
                dst = buf.at[to * c2 + k]

                @pl.when((k < filled) & (kind == 0))
                def _():
                    src = own_ref.at[tab_ref[R_SEND, to] * GR + g]
                    pltpu.make_async_copy(src, dst, in_sem.at[part]).start()

                @pl.when((k < filled) & (kind == 1))
                def _():
                    src = mate_ref.at[tab_ref[R_SENDM, to] * GR + g]
                    pltpu.make_async_copy(src, dst, in_sem.at[part]).start()

                @pl.when((k < filled) & (kind >= 2))
                def _():
                    pltpu.make_async_copy(got_ref.at[slot], dst, in_sem.at[part]).start()

            return count + filled

        return lax.fori_loop(0, each, body, jnp.int32(0), unroll=4)

    def piece(ref, part):
        return ref.at[pl.ds(part * each * c2, each * c2)]

    counts = [fetch(part) for part in range(parts)]
    for part in range(parts):

        def arrive(i, _, part=part):
            pltpu.make_async_copy(own_ref.at[0], buf.at[0], in_sem.at[part]).wait()
            return 0

        lax.fori_loop(0, counts[part], arrive, 0)
        pltpu.make_async_copy(piece(buf, part), piece(out_ref, part), out_sem.at[part]).start()
    for part in range(parts):
        pltpu.make_async_copy(piece(buf, part), piece(out_ref, part), out_sem.at[part]).wait()


def pack2(c2, tab, own, mate, got):
    parts = 4
    shape = (N * c2,) + own.shape[1:]
    return pl.pallas_call(
        functools.partial(pack2_kernel, c2),
        out_shape=pltpu.HBM(shape, own.dtype),
        in_specs=[pl.BlockSpec(memory_space=pltpu.SMEM)] + [pl.BlockSpec(memory_space=pltpu.HBM)] * 3,
        out_specs=pl.BlockSpec(memory_space=pltpu.HBM),
        scratch_shapes=[
            pltpu.VMEM(shape, own.dtype),
            pltpu.SemaphoreType.DMA((parts,)),
            pltpu.SemaphoreType.DMA((parts,)),
        ],
        compiler_params=pltpu.CompilerParams(vmem_limit_bytes=40 << 20),
        name="pack2",
    )(tab, *(pltpu.with_memory_space_constraint(x, pltpu.HBM) for x in (own, mate, got)))


def hand_kernel(tab_ref, got_ref, out_ref, sem):
    def body(s, count):
        w = tab_ref[R_F1COL, s]
        for k in range(C1):
            mine = (w >> (2 + 12 * k + 10)) & 1

            @pl.when(mine == 1)
            def _():
                pltpu.make_async_copy(got_ref.at[s * C1 + k], out_ref.at[count], sem).start()

            count = count + mine
        return count

    count = lax.fori_loop(0, N, body, jnp.int32(0))

    def fill(j, _):
        pltpu.make_async_copy(got_ref.at[0], out_ref.at[j], sem).start()
        return 0

    lax.fori_loop(count, K, fill, 0)
    pltpu.make_async_copy(out_ref, out_ref, sem).wait()


def hand(tab, got):
    return pl.pallas_call(
        hand_kernel,
        out_shape=jax.ShapeDtypeStruct((K,) + got.shape[1:], got.dtype),
        in_specs=[pl.BlockSpec(memory_space=pltpu.SMEM), pl.BlockSpec(memory_space=pltpu.HBM)],
        out_specs=pl.BlockSpec(memory_space=pltpu.VMEM),
        scratch_shapes=[pltpu.SemaphoreType.DMA],
        compiler_params=pltpu.CompilerParams(vmem_limit_bytes=40 << 20),
        name="hand",
    )(tab, got)


def pack_whole_kernel(tab_ref, own_ref, out_ref):
    out_ref[...] = own_ref[...]


def pack_whole(tab, own):
    block = (GR,) + own.shape[1:]
    return pl.pallas_call(
        pack_whole_kernel,
        grid_spec=pltpu.PrefetchScalarGridSpec(
            num_scalar_prefetch=1,
            grid=(N,),
            in_specs=[pl.BlockSpec(block, lambda i, tab: (tab[R_SEND, i], 0, 0))],
            out_specs=pl.BlockSpec(block, lambda i, tab: (i, 0, 0)),
        ),
        out_shape=jax.ShapeDtypeStruct((N * GR,) + own.shape[1:], own.dtype),
        name="pack_whole",
    )(tab, own)


def place_kernel(c2, me_ref, tab_ref, loc_ref):
    me = me_ref[0]
    order, counts, late_of = N * GR, N * GR + N, N * GR + 2 * N

    def clear(s, _):
        loc_ref[late_of + s] = 0
        for g in range(GR):
            loc_ref[s * GR + g] = s * GR + g if c2 == 0 else 0
        return 0

    lax.fori_loop(0, N, clear, 0)

    def find(s, handed):
        w = tab_ref[R_F1COL, s]
        filled = C1 - (w & 3)
        for k in range(C1):
            code = w >> (2 + 12 * k)

            @pl.when((k < filled) & (((code >> 3) & 0xFF) == me) & (s != me))
            def _():
                loc_ref[(s ^ ((code >> 11) & 1)) * GR + (code & 7)] = s * C1 + k

        w = tab_ref[R_F1COLM, s]
        for k in range(C1):
            code = w >> (2 + 12 * k)
            handed_here = (code >> 10) & 1

            @pl.when(handed_here == 1)
            def _():
                loc_ref[s * GR + (code & 7)] = (C1 + c2) * N + handed
                loc_ref[late_of + s] = 1

            handed = handed + handed_here

        w = tab_ref[R_F2COL, s]
        filled = c2 - (w & 3)
        for k in range(c2):
            code = w >> (2 + 14 * k)
            kind = code & 3
            origin = jnp.where(kind >= 2, (code >> 6) & (N - 1), s ^ (kind & 1))

            @pl.when((k < filled) & (s != me))
            def _():
                loc_ref[origin * GR + ((code >> 2) & 7)] = C1 * N + s * c2 + k
                loc_ref[late_of + origin] = 1

        return handed

    if c2 > 0:
        lax.fori_loop(0, N, find, jnp.int32(0))

    def sort(s, c):
        early, late = c
        is_live = (tab_ref[R_GIN, s] > 0).astype(jnp.int32)
        is_late = loc_ref[late_of + s]

        @pl.when(is_live == 1)
        def _():
            loc_ref[order + jnp.where(is_late == 1, N - 1 - late, early)] = s

        return early + is_live * (1 - is_late), late + is_live * is_late

    early, late = lax.fori_loop(0, N, sort, (jnp.int32(0), jnp.int32(0)))
    loc_ref[counts] = early
    loc_ref[counts + 1] = late


def place(c2, me, tab):
    return pl.pallas_call(
        functools.partial(place_kernel, c2),
        out_shape=jax.ShapeDtypeStruct((N * GR + 3 * N,), jnp.int32),
        in_specs=[pl.BlockSpec(memory_space=pltpu.SMEM)] * 2,
        out_specs=pl.BlockSpec(memory_space=pltpu.SMEM),
        name="place",
    )(me, tab)


def best_of(row, col, len_in, len_own, incoming, own_t):
    scale = 1.0 / jnp.sqrt(jnp.float32(own_t.shape[0]))
    score = jnp.dot(incoming, own_t, preferred_element_type=jnp.float32) * scale
    in_count = len_in.astype(jnp.float32)
    real_in = row < len_in
    real_own = col < len_own
    over_own = jnp.sum(jnp.where(real_own, score, 0.0), 1, keepdims=True) / len_own.astype(jnp.float32)
    over_in = jnp.sum(jnp.where(real_in, score, 0.0), 0, keepdims=True) / in_count
    grand = jnp.sum(jnp.where(real_in[:, :1], over_own, 0.0), 0, keepdims=True) / in_count
    own_best = jnp.max(jnp.where(real_in, score - over_own, lowest), 0, keepdims=True) - over_in + grand
    in_best = jnp.max(jnp.where(real_own, score - over_in, lowest), 1, keepdims=True) - over_own + grand
    return own_best, in_best


def match_kernel(late, ends, tab_ref, loc_ref, lens_ref, own_t_ref, best0_ref, ret0_ref, *refs):
    gots, (best_ref, ret_ref, buf, sem) = refs[: len(ends)], refs[len(ends) :]
    width = own_t_ref.shape[1]
    best_ref[...] = best0_ref[...]
    ret_ref[...] = ret0_ref[...]
    count = loc_ref[N * GR + N + int(late)]

    def sender(i):
        return loc_ref[N * GR + (N - 1 - i if late else i)]

    def fetch(i):
        @pl.when(i < count)
        def _():
            s = sender(i)
            slot = i & (DEPTH - 1)
            granules = tab_ref[R_GIN, s]
            for g in range(GR):

                @pl.when(g < granules)
                def _():
                    at = loc_ref[s * GR + g]
                    start = 0
                    for got_ref, end in zip(gots, ends):

                        @pl.when((at >= start) & (at < end))
                        def _(got_ref=got_ref, start=start):
                            pltpu.make_async_copy(
                                got_ref.at[at - start], buf.at[slot, g], sem.at[slot, g]
                            ).start()

                        start = end

    def arrive(i):
        @pl.when(i < count)
        def _():
            s = sender(i)
            slot = i & (DEPTH - 1)
            granules = tab_ref[R_GIN, s]
            for g in range(GR):

                @pl.when(g < granules)
                def _():
                    pltpu.make_async_copy(gots[0].at[0], buf.at[slot, g], sem.at[slot, g]).wait()

    for i in range(DEPTH - GROUP):
        fetch(i)
    row = lax.broadcasted_iota(jnp.int32, (N, N), 0)
    col = lax.broadcasted_iota(jnp.int32, (N, N), 1)

    def body(j, _):
        first = j * GROUP
        for u in range(GROUP):
            fetch(first + u + DEPTH - GROUP)
        for u in range(GROUP):
            arrive(first + u)
        found = []
        for u in range(GROUP):
            i = jnp.minimum(first + u, count - 1)
            s = sender(i)
            p = tab_ref[R_OWN, s]
            incoming = buf[i & (DEPTH - 1)].reshape(N, width)
            found.append((s, p) + best_of(
                row, col, tab_ref[R_LIN, s], lens_ref[p], incoming, own_t_ref[p]
            ))
        ret = ret_ref[...]
        for s, p, own_best, in_best in found:
            best_ref[pl.ds(p, 1), :] = jnp.maximum(best_ref[pl.ds(p, 1), :], own_best)
            ret = jnp.where(col == s, in_best, ret)
        ret_ref[...] = ret
        return 0

    lax.fori_loop(0, (count + GROUP - 1) // GROUP, body, 0)
    if late:
        ret_ref[...] = ret_ref[...].T


def match(late, tab, loc, lens, own_t, best, ret, *gots):
    ends = []
    for got in gots:
        ends.append((ends[-1] if ends else 0) + got.shape[0])
    return pl.pallas_call(
        functools.partial(match_kernel, late, tuple(ends)),
        out_shape=[jax.ShapeDtypeStruct(x.shape, x.dtype) for x in (best, ret)],
        in_specs=[pl.BlockSpec(memory_space=pltpu.SMEM)] * 3
        + [pl.BlockSpec(memory_space=pltpu.VMEM)] * 3
        + [pl.BlockSpec(memory_space=pltpu.HBM)] * len(gots),
        out_specs=[pl.BlockSpec(memory_space=pltpu.VMEM)] * 2,
        scratch_shapes=[
            pltpu.VMEM((DEPTH, GR, 16, own_t.shape[1]), own_t.dtype),
            pltpu.SemaphoreType.DMA((DEPTH, GR)),
        ],
        compiler_params=pltpu.CompilerParams(vmem_limit_bytes=40 << 20),
        name="match_late" if late else "match_early",
    )(tab, loc, lens, own_t, best, ret, *gots)


def near_kernel(late, tab_ref, loc_ref, lens_ref, own_t_hbm, best0_ref, ret0_ref, *refs):
    gots, (best_ref, ret_ref, own_t_ref, all_ref, buf, sem, piece_sem) = refs[:-7], refs[-7:]
    copies = [pltpu.make_async_copy(own_t_hbm, own_t_ref, sem.at[0])]
    start = gots[0].shape[0]
    for i, got in enumerate(gots[1:]):
        end = start + got.shape[0]
        copies.append(pltpu.make_async_copy(got, all_ref.at[pl.ds(start, end - start)], sem.at[i + 1]))
        start = end
    senders = N // PIECES
    rows = senders * C1
    pieces = [
        pltpu.make_async_copy(
            gots[0].at[pl.ds(c * rows, rows)], all_ref.at[pl.ds(c * rows, rows)], piece_sem.at[c]
        )
        for c in range(PIECES)
    ]
    for copy in copies + pieces:
        copy.start()
    width = own_t_ref.shape[1]
    best_ref[...] = best0_ref[...]
    ret_ref[...] = ret0_ref[...]
    count = loc_ref[N * GR + N + int(late)]

    def sender(i):
        i = jnp.minimum(i, count - 1)
        return loc_ref[N * GR + (N - 1 - i if late else i)]

    def gather(i, u):
        s = sender(i)
        for g in range(GR):
            buf[u, g] = all_ref[loc_ref[s * GR + g]]

    for copy in copies:
        copy.wait()
    row = lax.broadcasted_iota(jnp.int32, (N, N), 0)
    col = lax.broadcasted_iota(jnp.int32, (N, N), 1)

    def body(j, here):
        first = j * GROUP
        need = sender(first + GROUP - 1) // senders + 1
        for c in range(PIECES):

            @pl.when((c >= here) & (c < need))
            def _(c=c):
                pieces[c].wait()

        for u in range(GROUP):
            gather(first + u, u)
        found = []
        for u in range(GROUP):
            s = sender(first + u)
            p = tab_ref[R_OWN, s]
            found.append((s, p) + best_of(
                row, col, tab_ref[R_LIN, s], lens_ref[p], buf[u].reshape(N, width), own_t_ref[p]
            ))
        ret = ret_ref[...]
        for s, p, own_best, in_best in found:
            best_ref[pl.ds(p, 1), :] = jnp.maximum(best_ref[pl.ds(p, 1), :], own_best)
            ret = jnp.where(col == s, in_best, ret)
        ret_ref[...] = ret
        return jnp.maximum(here, need)

    here = lax.fori_loop(0, (count + GROUP - 1) // GROUP, body, jnp.int32(0))
    for c in range(PIECES):

        @pl.when(c >= here)
        def _(c=c):
            pieces[c].wait()

    if late:
        ret_ref[...] = ret_ref[...].T


def near(late, tab, loc, lens, own_t, best, ret, *gots):
    total = sum(got.shape[0] for got in gots)
    far = [pltpu.with_memory_space_constraint(x, pltpu.HBM) for x in (own_t,) + gots]
    return pl.pallas_call(
        functools.partial(near_kernel, late),
        out_shape=[jax.ShapeDtypeStruct(x.shape, x.dtype) for x in (best, ret)],
        in_specs=[pl.BlockSpec(memory_space=pltpu.SMEM)] * 3
        + [pl.BlockSpec(memory_space=pltpu.HBM)]
        + [pl.BlockSpec(memory_space=pltpu.VMEM)] * 2
        + [pl.BlockSpec(memory_space=pltpu.HBM)] * len(gots),
        out_specs=[pl.BlockSpec(memory_space=pltpu.VMEM)] * 2,
        scratch_shapes=[
            pltpu.VMEM(own_t.shape, own_t.dtype),
            pltpu.VMEM((total,) + gots[0].shape[1:], own_t.dtype),
            pltpu.VMEM((GROUP, GR, 16, own_t.shape[1]), own_t.dtype),
            pltpu.SemaphoreType.DMA((len(gots),)),
            pltpu.SemaphoreType.DMA((PIECES,)),
        ],
        compiler_params=pltpu.CompilerParams(vmem_limit_bytes=44 << 20),
        name="near_late" if late else "near_early",
    )(tab, loc, lens, far[0], best, ret, *far[1:])


def centred(score_matrix, row_validity_mask, col_mask):
    row_count = jnp.sum(row_validity_mask, -1)
    col_count = jnp.sum(col_mask, -1)
    row_mean = jnp.sum(score_matrix * col_mask[..., None, :], -1) / col_count[..., None]
    col_mean = jnp.sum(score_matrix * row_validity_mask[..., :, None], -2) / row_count[..., None]
    grand_mean = jnp.sum(row_mean * row_validity_mask, -1) / row_count
    return (
        score_matrix - row_mean[..., :, None] - col_mean[..., None, :] + grand_mean[..., None, None]
    )


def within_cluster(embeddings, masks):
    proteins_here, slots, width = embeddings.shape
    inverse_square_root = 1.0 / jnp.sqrt(jnp.float32(width))
    block_size = 8
    block_count = proteins_here // block_size

    def one_block(block_start):
        block_rows = lax.dynamic_slice_in_dim(embeddings, block_start, block_size, 0)
        block_mask = lax.dynamic_slice_in_dim(masks, block_start, block_size, 0)
        score_matrix = (
            jnp.einsum("bie,qje->bqij", block_rows, embeddings, preferred_element_type=jnp.float32)
            * inverse_square_root
        )
        cent = centred(score_matrix, block_mask[:, None, :], masks[None, :, :])
        row_max = jnp.max(jnp.where(masks[None, :, None, :] > 0, cent, lowest), -1)
        self_pair = (block_start + jnp.arange(block_size))[:, None] == jnp.arange(proteins_here)[
            None, :
        ]
        row_max = jnp.where(self_pair[:, :, None], lowest, row_max)
        best_match = jnp.max(row_max, 1)
        return jnp.where(block_mask > 0, best_match, 0.0)

    start_offsets = jnp.arange(block_count) * block_size
    return lax.map(one_block, start_offsets).reshape(proteins_here, slots)


def exchange(x):
    return lax.all_to_all(x, "shard", split_axis=0, concat_axis=0, tiled=True)


def other_core(x):
    return lax.ppermute(x, "shard", [(d, d ^ 1) for d in range(N)])


def per_device(embeddings, lengths, requests, query_local):
    proteins_here, slots, width = embeddings.shape
    masks = (jnp.arange(slots)[None, :] < lengths[:, None]).astype(jnp.float32)
    me = lax.axis_index("shard").astype(jnp.int32)[None]
    plan = jnp.concatenate([requests, query_local, lengths[None, :]], 1)
    plan = jnp.pad(plan, ((0, 0), (0, 3 * N - plan.shape[1])))
    plan = exchange(jnp.broadcast_to(plan, (N, 3 * N)))
    own = embeddings.reshape(proteins_here * GR, 16, width)

    mate = other_core(own)
    none_own = jnp.full((proteins_here, slots), lowest, jnp.float32)
    none_in = jnp.full((N, slots), lowest, jnp.float32)

    def finish(tab, best, ret, local_best):
        returned = exchange(ret)
        mine = (tab[R_SEND][None, :] == jnp.arange(proteins_here)[:, None]) & (tab[R_GOUT] > 0)[None, :]
        from_ret = jnp.max(jnp.where(mine[:, :, None], returned[None, :, :], lowest), 1)
        best = jnp.maximum(from_ret, best)
        cross_best = jnp.where((masks > 0) & (best > -1e29), best, 0.0)
        return local_best, cross_best

    def packed(c2, tab):
        loc = place(c2, me, tab)
        got1 = exchange(pack1(tab, own, mate))
        local_best = within_cluster(embeddings, masks)
        rows, local_best = lax.optimization_barrier((embeddings, local_best))
        own_t = jnp.swapaxes(rows, 1, 2)
        got1, local_best, own_t = lax.optimization_barrier((got1, local_best, own_t))
        send2 = pack2(c2, tab, own, mate, got1)
        send2, got1 = lax.optimization_barrier((send2, got1))
        got2 = exchange(send2)
        handed = other_core(hand(tab, got1))
        best, ret = near(False, tab, loc, lengths, own_t, none_own, none_in, got1)
        best, ret, got2 = lax.optimization_barrier((best, ret, got2))
        best, ret = near(True, tab, loc, lengths, own_t, best, ret, got1, got2, handed)
        return finish(tab, best, ret, local_best)

    def whole(tab):
        loc = place(0, me, tab)
        got = exchange(pack_whole(tab, own))
        own_t = jnp.swapaxes(embeddings, 1, 2)
        local_best = within_cluster(embeddings, masks)
        best, ret = match(False, tab, loc, lengths, own_t, none_own, none_in, got)
        best, ret = match(True, tab, loc, lengths, own_t, best, ret, got)
        return finish(tab, best, ret, local_best)

    def second(_):
        tab, left = route(2, me, plan)
        return lax.cond(left[0] == 0, functools.partial(packed, 2), whole, tab)

    tab, left = route(1, me, plan)
    return lax.cond(left[0] == 0, functools.partial(packed, 1), second, tab)


def solution(mesh):
    placed = (P("shard", None, None), P("shard"), P("shard", None), P("shard", None))
    return jax.shard_map(
        per_device,
        mesh=mesh,
        in_specs=placed,
        out_specs=(P("shard", None), P("shard", None)),
        check_vma=False,
    )
```

```python
import functools

import jax
import jax.numpy as jnp
from jax import lax
from jax.experimental import pallas as pl
from jax.experimental.pallas import tpu as pltpu
from jax.sharding import PartitionSpec as P

lowest = -1e30
N = 128
GR = 8
C1 = 2
K = 64
DEPTH = 16
GROUP = 4
PIECES = 4
TRIES = 6
FEW = 32

R_F1ROW, R_F1COL, R_F1COLM, R_F2ROW, R_F2COL, R_SEND, R_SENDM, R_GIN, R_LIN, R_OWN, R_GOUT = range(11)


def swap_rows(x, s):
    return jnp.where((s & 1) == 0, pltpu.roll(x, N - 1, 0), pltpu.roll(x, 1, 0))


def swap_cols(x, r):
    return jnp.where((r & 1) == 0, pltpu.roll(x, N - 1, 1), pltpu.roll(x, 1, 1))


def skew(x, by, axis, sign):
    for b in range(7):
        shift = (1 << b) if sign > 0 else N - (1 << b)
        x = jnp.where(((by >> b) & 1) == 1, pltpu.roll(x, shift, axis), x)
    return x


def before(x, s):
    total = x
    for b in range(7):
        total = total + jnp.where(s >= (1 << b), pltpu.roll(total, 1 << b, 0), 0)
    return total - x


def route_kernel(c2, me_ref, plan_ref, tab_ref, left_ref, tmp_ref, first_ref):
    s = lax.broadcasted_iota(jnp.int32, (N, N), 0)
    r = lax.broadcasted_iota(jnp.int32, (N, N), 1)
    req = plan_ref[:, :N]
    q = plan_ref[:, N : 2 * N]
    lens = plan_ref[:, 2 * N :]
    lens_t = lens.T
    live = (req >= 0).astype(jnp.int32)
    req = jnp.maximum(req, 0)
    la = jnp.zeros((N, N), jnp.int32)
    lb = jnp.zeros((N, N), jnp.int32)
    for p in range(16):
        la = jnp.where(q == p, lens[:, p : p + 1], la)
        lb = jnp.where(req == p, lens_t[p : p + 1, :], lb)
    la = la * live
    lb = lb * live
    la_t = la.T
    lb_t = lb.T
    req_t = req.T
    ga = (la + 15) >> 4
    gb = (lb + 15) >> 4
    ga_t = (la_t + 15) >> 4
    gb_t = (lb_t + 15) >> 4
    anti = live - (lb_t > 0).astype(jnp.int32)
    base = 1000 * (gb + gb_t - ga - ga_t) + jnp.where(((s + r) & 1) == 0, 250, -250)
    score = base
    bias_col = jnp.zeros((N, 1), jnp.int32)
    bias_row = jnp.zeros((1, N), jnp.int32)
    for eta in (10, 6, 4):
        gets = score < 0
        net = jnp.where(gets, gb_t, ga) - jnp.where(gets, gb, ga_t)
        bias_row = bias_row + eta * jnp.sum(net, axis=0, keepdims=True)
        bias_col = bias_col - eta * jnp.sum(net, axis=1, keepdims=True)
        score = base + anti * (bias_col - bias_row)
    lister_gets = score < 0
    lin = jnp.where(lister_gets, lb_t, la)
    lin_t = jnp.where(lister_gets, lb, la_t)
    psend = jnp.where(lister_gets, req_t, q)
    pown_t = jnp.where(lister_gets, q, req_t)
    m_tot = (lin + 15) >> 4

    diag = s == r
    free1 = jnp.where(diag, 0, C1)
    n = jnp.minimum(m_tot, free1)
    rem = m_tot - n
    w1 = free1 - n
    for k in range(C1):
        w1 = w1 | jnp.where(k < n, ((r << 3) | k) << (2 + 12 * k), 0)
    m_swap = swap_rows(m_tot, s)
    rem_s = swap_rows(rem, s)
    used = C1 - (w1 & 3)
    n = jnp.where(diag, 0, jnp.minimum(rem_s, w1 & 3))
    w1 = w1 - n
    for k in range(C1):
        code = (1 << 11) | (r << 3) | (m_swap - rem_s + k - used)
        w1 = w1 | jnp.where((k >= used) & (k < used + n), code << (2 + 12 * k), 0)
    rem = swap_rows(rem_s - n, s)
    free2 = jnp.where(diag, 0, c2)
    g_from = m_tot - rem
    n = jnp.minimum(rem, free2)
    rem = rem - n
    w2 = free2 - n
    for k in range(c2):
        w2 = w2 | jnp.where(k < n, ((g_from + k) << 2) << (2 + 14 * k), 0)
    rem_s = swap_rows(rem, s)
    used = c2 - (w2 & 3)
    n = jnp.where(diag, 0, jnp.minimum(rem_s, w2 & 3))
    w2 = w2 - n
    for k in range(c2):
        code = 1 | ((m_swap - rem_s + k - used) << 2)
        w2 = w2 | jnp.where((k >= used) & (k < used + n), code << (2 + 14 * k), 0)
    rem = swap_rows(rem_s - n, s)
    rem_c = swap_cols(rem, r)
    g_from = swap_cols(m_tot, r) - rem_c
    used = C1 - (w1 & 3)
    n = jnp.where(diag, 0, jnp.minimum(rem_c, w1 & 3))
    n = jnp.maximum(jnp.minimum(n, K - before(n, s)), 0)
    w1 = w1 - n
    for k in range(C1):
        code = (1 << 10) | ((r ^ 1) << 3) | (g_from + k - used)
        w1 = w1 | jnp.where((k >= used) & (k < used + n), code << (2 + 12 * k), 0)
    rem = swap_cols(rem_c - n, r)

    w1 = skew(w1, s, 1, -1)
    w2 = skew(w2, r, 0, -1)

    last = m_tot - 1
    kept2 = ((s << 6) | 2) << 2

    def step(limit, w1, w2, g):
        f1 = w1 & 3
        f2 = w2 & 3
        ok = (jnp.minimum(f1, f2) > 0) & (g <= limit)
        first = f1 == C1
        at = g << 2
        code1 = (r << 5) | at
        w1_new = w1 + jnp.where(first, code1, code1 << 12) - 1
        code2 = kept2 + (at << 2) + jnp.where(first, 0, 1 << 7)
        if c2 > 1:
            code2 = jnp.where(f2 == c2, code2, code2 << 14)
        w2_new = w2 + code2 - 1
        w1 = jnp.where(ok, w1_new, w1)
        w2 = jnp.where(ok, w2_new, w2)
        g = jnp.where(ok, g + 1, g)
        return pltpu.roll(w1, N - 1, 1), pltpu.roll(w2, N - 1, 0), g

    first_ref[0] = w1
    first_ref[1] = w2
    first_ref[2] = m_tot - rem

    def sweep(limit, turns, w1, w2, g):
        def body(c):
            i, _, w1, w2, g = c
            for _ in range(8):
                w1, w2, g = step(limit, w1, w2, g)
            return i + 1, jnp.max(limit - g), w1, w2, g

        i, most, w1, w2, g = lax.while_loop(
            lambda c: (c[0] < N // 8) & (c[1] >= 0),
            body,
            (jnp.int32(0), jnp.max(limit - g), w1, w2, g),
        )
        return most, turns + 8 * i, w1, w2, g

    def attempt(c):
        tries, _, _, _, _, urgent = c
        limit = jnp.where(urgent > 0, last, -1)
        _, turns, w1, w2, g = sweep(limit, 0, first_ref[0], first_ref[1], first_ref[2])
        _, turns, w1, w2, g = sweep(last, turns, w1, w2, g)
        late = (g <= last).astype(jnp.int32)
        return tries + 1, jnp.sum(late), turns, w1, w2, jnp.maximum(late, urgent)

    _, left, turns, w1, w2, _ = lax.while_loop(
        lambda c: (c[0] < TRIES) & (c[1] > 0) & (c[1] <= FEW),
        attempt,
        (jnp.int32(0), jnp.int32(1), jnp.int32(0), w1, w2, jnp.zeros((N, N), jnp.int32)),
    )
    turns = turns & (N - 1)
    w1 = skew(pltpu.roll(w1, turns, 1), s, 1, 1)
    w2 = skew(pltpu.roll(w2, turns, 0), r, 0, 1)

    me = me_ref[0]
    mate = me ^ 1

    def put(x, *rows):
        tmp_ref[...] = x
        for row, at in rows:
            tab_ref[row : row + 1, :] = tmp_ref[pl.ds(at, 1), :]

    put(w1, (R_F1ROW, me))
    put(w1.T, (R_F1COL, me), (R_F1COLM, mate))
    put(w2, (R_F2ROW, me))
    put(w2.T, (R_F2COL, me))
    put(psend, (R_SEND, me), (R_SENDM, mate))
    put((lin_t + 15) >> 4, (R_GIN, me))
    put(lin_t, (R_LIN, me))
    put(pown_t, (R_OWN, me))
    left_ref[0] = left
    put(m_tot, (R_GOUT, me))
    tab_ref[R_GOUT + 1 :, :] = jnp.zeros((16 - R_GOUT - 1, N), jnp.int32)


def route(c2, me, plan):
    return pl.pallas_call(
        functools.partial(route_kernel, c2),
        out_shape=[jax.ShapeDtypeStruct((16, N), jnp.int32), jax.ShapeDtypeStruct((1,), jnp.int32)],
        in_specs=[pl.BlockSpec(memory_space=pltpu.SMEM), pl.BlockSpec(memory_space=pltpu.VMEM)],
        out_specs=[pl.BlockSpec(memory_space=pltpu.VMEM), pl.BlockSpec(memory_space=pltpu.SMEM)],
        scratch_shapes=[pltpu.VMEM((N, N), jnp.int32), pltpu.VMEM((3, N, N), jnp.int32)],
        compiler_params=pltpu.CompilerParams(vmem_limit_bytes=32 << 20),
        name=f"route{c2}",
    )(me, plan)


def pack1_kernel(tab_ref, own_ref, mate_ref, out_ref, both, buf, in_sem, out_sem):
    parts = out_sem.shape[0]
    each = N // parts
    held = own_ref.shape[0]

    def piece(ref, part):
        return ref.at[pl.ds(part * each * C1, each * C1)]

    copies = [
        pltpu.make_async_copy(ref, both.at[pl.ds(i * held, held)], in_sem.at[i])
        for i, ref in enumerate((own_ref, mate_ref))
    ]
    for copy in copies:
        copy.start()
    for copy in copies:
        copy.wait()
    for part in range(parts):

        def body(j, _):
            w = tab_ref[R_F1ROW, j]
            for k in range(C1):
                code = w >> (2 + 12 * k)
                core = (code >> 11) & 1
                protein = tab_ref[R_SEND + core, (code >> 3) & (N - 1)]
                buf[j * C1 + k] = both[core * held + protein * GR + (code & 7)]
            return 0

        lax.fori_loop(part * each, (part + 1) * each, body, 0, unroll=8)
        pltpu.make_async_copy(piece(buf, part), piece(out_ref, part), out_sem.at[part]).start()
    for part in range(parts):
        pltpu.make_async_copy(piece(buf, part), piece(out_ref, part), out_sem.at[part]).wait()


def pack1(tab, own, mate):
    parts = 8
    shape = (N * C1,) + own.shape[1:]
    return pl.pallas_call(
        pack1_kernel,
        out_shape=pltpu.HBM(shape, own.dtype),
        in_specs=[pl.BlockSpec(memory_space=pltpu.SMEM)] + [pl.BlockSpec(memory_space=pltpu.HBM)] * 2,
        out_specs=pl.BlockSpec(memory_space=pltpu.HBM),
        scratch_shapes=[
            pltpu.VMEM((2 * own.shape[0],) + own.shape[1:], own.dtype),
            pltpu.VMEM(shape, own.dtype),
            pltpu.SemaphoreType.DMA((2,)),
            pltpu.SemaphoreType.DMA((parts,)),
        ],
        compiler_params=pltpu.CompilerParams(vmem_limit_bytes=40 << 20),
        name="pack1",
    )(tab, *(pltpu.with_memory_space_constraint(x, pltpu.HBM) for x in (own, mate)))


def pack2_kernel(c2, tab_ref, own_ref, mate_ref, got_ref, out_ref, buf, in_sem, out_sem):
    parts = in_sem.shape[0]
    each = N // parts

    def fetch(part):
        def body(j, count):
            to = part * each + j
            w = tab_ref[R_F2ROW, to]
            filled = c2 - (w & 3)
            for k in range(c2):
                code = w >> (2 + 14 * k)
                kind = code & 3
                g = (code >> 2) & 7
                slot = ((code >> 6) & (N - 1)) * C1 + ((code >> 5) & 1)
                dst = buf.at[to * c2 + k]

                @pl.when((k < filled) & (kind == 0))
                def _():
                    src = own_ref.at[tab_ref[R_SEND, to] * GR + g]
                    pltpu.make_async_copy(src, dst, in_sem.at[part]).start()

                @pl.when((k < filled) & (kind == 1))
                def _():
                    src = mate_ref.at[tab_ref[R_SENDM, to] * GR + g]
                    pltpu.make_async_copy(src, dst, in_sem.at[part]).start()

                @pl.when((k < filled) & (kind >= 2))
                def _():
                    pltpu.make_async_copy(got_ref.at[slot], dst, in_sem.at[part]).start()

            return count + filled

        return lax.fori_loop(0, each, body, jnp.int32(0), unroll=4)

    def piece(ref, part):
        return ref.at[pl.ds(part * each * c2, each * c2)]

    counts = [fetch(part) for part in range(parts)]
    for part in range(parts):

        def arrive(i, _, part=part):
            pltpu.make_async_copy(own_ref.at[0], buf.at[0], in_sem.at[part]).wait()
            return 0

        lax.fori_loop(0, counts[part], arrive, 0)
        pltpu.make_async_copy(piece(buf, part), piece(out_ref, part), out_sem.at[part]).start()
    for part in range(parts):
        pltpu.make_async_copy(piece(buf, part), piece(out_ref, part), out_sem.at[part]).wait()


def pack2(c2, tab, own, mate, got):
    parts = 4
    shape = (N * c2,) + own.shape[1:]
    return pl.pallas_call(
        functools.partial(pack2_kernel, c2),
        out_shape=pltpu.HBM(shape, own.dtype),
        in_specs=[pl.BlockSpec(memory_space=pltpu.SMEM)] + [pl.BlockSpec(memory_space=pltpu.HBM)] * 3,
        out_specs=pl.BlockSpec(memory_space=pltpu.HBM),
        scratch_shapes=[
            pltpu.VMEM(shape, own.dtype),
            pltpu.SemaphoreType.DMA((parts,)),
            pltpu.SemaphoreType.DMA((parts,)),
        ],
        compiler_params=pltpu.CompilerParams(vmem_limit_bytes=40 << 20),
        name="pack2",
    )(tab, *(pltpu.with_memory_space_constraint(x, pltpu.HBM) for x in (own, mate, got)))


def hand_kernel(tab_ref, got_ref, out_ref, sem):
    def body(s, count):
        w = tab_ref[R_F1COL, s]
        for k in range(C1):
            mine = (w >> (2 + 12 * k + 10)) & 1

            @pl.when(mine == 1)
            def _():
                pltpu.make_async_copy(got_ref.at[s * C1 + k], out_ref.at[count], sem).start()

            count = count + mine
        return count

    count = lax.fori_loop(0, N, body, jnp.int32(0))

    def fill(j, _):
        pltpu.make_async_copy(got_ref.at[0], out_ref.at[j], sem).start()
        return 0

    lax.fori_loop(count, K, fill, 0)
    pltpu.make_async_copy(out_ref, out_ref, sem).wait()


def hand(tab, got):
    return pl.pallas_call(
        hand_kernel,
        out_shape=jax.ShapeDtypeStruct((K,) + got.shape[1:], got.dtype),
        in_specs=[pl.BlockSpec(memory_space=pltpu.SMEM), pl.BlockSpec(memory_space=pltpu.HBM)],
        out_specs=pl.BlockSpec(memory_space=pltpu.VMEM),
        scratch_shapes=[pltpu.SemaphoreType.DMA],
        compiler_params=pltpu.CompilerParams(vmem_limit_bytes=40 << 20),
        name="hand",
    )(tab, got)


def pack_whole_kernel(tab_ref, own_ref, out_ref):
    out_ref[...] = own_ref[...]


def pack_whole(tab, own):
    block = (GR,) + own.shape[1:]
    return pl.pallas_call(
        pack_whole_kernel,
        grid_spec=pltpu.PrefetchScalarGridSpec(
            num_scalar_prefetch=1,
            grid=(N,),
            in_specs=[pl.BlockSpec(block, lambda i, tab: (tab[R_SEND, i], 0, 0))],
            out_specs=pl.BlockSpec(block, lambda i, tab: (i, 0, 0)),
        ),
        out_shape=jax.ShapeDtypeStruct((N * GR,) + own.shape[1:], own.dtype),
        name="pack_whole",
    )(tab, own)


def place_kernel(c2, me_ref, tab_ref, loc_ref):
    me = me_ref[0]
    order, counts, late_of = N * GR, N * GR + N, N * GR + 2 * N

    def clear(s, _):
        loc_ref[late_of + s] = 0
        for g in range(GR):
            loc_ref[s * GR + g] = s * GR + g if c2 == 0 else 0
        return 0

    lax.fori_loop(0, N, clear, 0)

    def find(s, handed):
        w = tab_ref[R_F1COL, s]
        filled = C1 - (w & 3)
        for k in range(C1):
            code = w >> (2 + 12 * k)

            @pl.when((k < filled) & (((code >> 3) & 0xFF) == me) & (s != me))
            def _():
                loc_ref[(s ^ ((code >> 11) & 1)) * GR + (code & 7)] = s * C1 + k

        w = tab_ref[R_F1COLM, s]
        for k in range(C1):
            code = w >> (2 + 12 * k)
            handed_here = (code >> 10) & 1

            @pl.when(handed_here == 1)
            def _():
                loc_ref[s * GR + (code & 7)] = (C1 + c2) * N + handed
                loc_ref[late_of + s] = 1

            handed = handed + handed_here

        w = tab_ref[R_F2COL, s]
        filled = c2 - (w & 3)
        for k in range(c2):
            code = w >> (2 + 14 * k)
            kind = code & 3
            origin = jnp.where(kind >= 2, (code >> 6) & (N - 1), s ^ (kind & 1))

            @pl.when((k < filled) & (s != me))
            def _():
                loc_ref[origin * GR + ((code >> 2) & 7)] = C1 * N + s * c2 + k
                loc_ref[late_of + origin] = 1

        return handed

    if c2 > 0:
        lax.fori_loop(0, N, find, jnp.int32(0))

    def sort(s, c):
        early, late = c
        is_live = (tab_ref[R_GIN, s] > 0).astype(jnp.int32)
        is_late = loc_ref[late_of + s]

        @pl.when(is_live == 1)
        def _():
            loc_ref[order + jnp.where(is_late == 1, N - 1 - late, early)] = s

        return early + is_live * (1 - is_late), late + is_live * is_late

    early, late = lax.fori_loop(0, N, sort, (jnp.int32(0), jnp.int32(0)))
    loc_ref[counts] = early
    loc_ref[counts + 1] = late


def place(c2, me, tab):
    return pl.pallas_call(
        functools.partial(place_kernel, c2),
        out_shape=jax.ShapeDtypeStruct((N * GR + 3 * N,), jnp.int32),
        in_specs=[pl.BlockSpec(memory_space=pltpu.SMEM)] * 2,
        out_specs=pl.BlockSpec(memory_space=pltpu.SMEM),
        name="place",
    )(me, tab)


def best_of(row, col, len_in, len_own, incoming, own_t):
    scale = 1.0 / jnp.sqrt(jnp.float32(own_t.shape[0]))
    score = jnp.dot(incoming, own_t, preferred_element_type=jnp.float32) * scale
    in_count = len_in.astype(jnp.float32)
    real_in = row < len_in
    real_own = col < len_own
    over_own = jnp.sum(jnp.where(real_own, score, 0.0), 1, keepdims=True) / len_own.astype(jnp.float32)
    over_in = jnp.sum(jnp.where(real_in, score, 0.0), 0, keepdims=True) / in_count
    grand = jnp.sum(jnp.where(real_in[:, :1], over_own, 0.0), 0, keepdims=True) / in_count
    own_best = jnp.max(jnp.where(real_in, score - over_own, lowest), 0, keepdims=True) - over_in + grand
    in_best = jnp.max(jnp.where(real_own, score - over_in, lowest), 1, keepdims=True) - over_own + grand
    return own_best, in_best


def match_kernel(late, ends, tab_ref, loc_ref, lens_ref, own_t_ref, best0_ref, ret0_ref, *refs):
    gots, (best_ref, ret_ref, buf, sem) = refs[: len(ends)], refs[len(ends) :]
    width = own_t_ref.shape[1]
    best_ref[...] = best0_ref[...]
    ret_ref[...] = ret0_ref[...]
    count = loc_ref[N * GR + N + int(late)]

    def sender(i):
        return loc_ref[N * GR + (N - 1 - i if late else i)]

    def fetch(i):
        @pl.when(i < count)
        def _():
            s = sender(i)
            slot = i & (DEPTH - 1)
            granules = tab_ref[R_GIN, s]
            for g in range(GR):

                @pl.when(g < granules)
                def _():
                    at = loc_ref[s * GR + g]
                    start = 0
                    for got_ref, end in zip(gots, ends):

                        @pl.when((at >= start) & (at < end))
                        def _(got_ref=got_ref, start=start):
                            pltpu.make_async_copy(
                                got_ref.at[at - start], buf.at[slot, g], sem.at[slot, g]
                            ).start()

                        start = end

    def arrive(i):
        @pl.when(i < count)
        def _():
            s = sender(i)
            slot = i & (DEPTH - 1)
            granules = tab_ref[R_GIN, s]
            for g in range(GR):

                @pl.when(g < granules)
                def _():
                    pltpu.make_async_copy(gots[0].at[0], buf.at[slot, g], sem.at[slot, g]).wait()

    for i in range(DEPTH - GROUP):
        fetch(i)
    row = lax.broadcasted_iota(jnp.int32, (N, N), 0)
    col = lax.broadcasted_iota(jnp.int32, (N, N), 1)

    def body(j, _):
        first = j * GROUP
        for u in range(GROUP):
            fetch(first + u + DEPTH - GROUP)
        for u in range(GROUP):
            arrive(first + u)
        found = []
        for u in range(GROUP):
            i = jnp.minimum(first + u, count - 1)
            s = sender(i)
            p = tab_ref[R_OWN, s]
            incoming = buf[i & (DEPTH - 1)].reshape(N, width)
            found.append((s, p) + best_of(
                row, col, tab_ref[R_LIN, s], lens_ref[p], incoming, own_t_ref[p]
            ))
        ret = ret_ref[...]
        for s, p, own_best, in_best in found:
            best_ref[pl.ds(p, 1), :] = jnp.maximum(best_ref[pl.ds(p, 1), :], own_best)
            ret = jnp.where(col == s, in_best, ret)
        ret_ref[...] = ret
        return 0

    lax.fori_loop(0, (count + GROUP - 1) // GROUP, body, 0)
    if late:
        ret_ref[...] = ret_ref[...].T


def match(late, tab, loc, lens, own_t, best, ret, *gots):
    ends = []
    for got in gots:
        ends.append((ends[-1] if ends else 0) + got.shape[0])
    return pl.pallas_call(
        functools.partial(match_kernel, late, tuple(ends)),
        out_shape=[jax.ShapeDtypeStruct(x.shape, x.dtype) for x in (best, ret)],
        in_specs=[pl.BlockSpec(memory_space=pltpu.SMEM)] * 3
        + [pl.BlockSpec(memory_space=pltpu.VMEM)] * 3
        + [pl.BlockSpec(memory_space=pltpu.HBM)] * len(gots),
        out_specs=[pl.BlockSpec(memory_space=pltpu.VMEM)] * 2,
        scratch_shapes=[
            pltpu.VMEM((DEPTH, GR, 16, own_t.shape[1]), own_t.dtype),
            pltpu.SemaphoreType.DMA((DEPTH, GR)),
        ],
        compiler_params=pltpu.CompilerParams(vmem_limit_bytes=40 << 20),
        name="match_late" if late else "match_early",
    )(tab, loc, lens, own_t, best, ret, *gots)


def near_kernel(late, tab_ref, loc_ref, lens_ref, own_t_hbm, best0_ref, ret0_ref, *refs):
    gots, (best_ref, ret_ref, own_t_ref, all_ref, buf, sem, piece_sem) = refs[:-7], refs[-7:]
    copies = [pltpu.make_async_copy(own_t_hbm, own_t_ref, sem.at[0])]
    start = gots[0].shape[0]
    for i, got in enumerate(gots[1:]):
        end = start + got.shape[0]
        copies.append(pltpu.make_async_copy(got, all_ref.at[pl.ds(start, end - start)], sem.at[i + 1]))
        start = end
    senders = N // PIECES
    rows = senders * C1
    pieces = [
        pltpu.make_async_copy(
            gots[0].at[pl.ds(c * rows, rows)], all_ref.at[pl.ds(c * rows, rows)], piece_sem.at[c]
        )
        for c in range(PIECES)
    ]
    for copy in copies + pieces:
        copy.start()
    width = own_t_ref.shape[1]
    best_ref[...] = best0_ref[...]
    ret_ref[...] = ret0_ref[...]
    count = loc_ref[N * GR + N + int(late)]

    def sender(i):
        i = jnp.minimum(i, count - 1)
        return loc_ref[N * GR + (N - 1 - i if late else i)]

    def gather(i, u):
        s = sender(i)
        for g in range(GR):
            buf[u, g] = all_ref[loc_ref[s * GR + g]]

    for copy in copies:
        copy.wait()
    row = lax.broadcasted_iota(jnp.int32, (N, N), 0)
    col = lax.broadcasted_iota(jnp.int32, (N, N), 1)

    def body(j, here):
        first = j * GROUP
        need = sender(first + GROUP - 1) // senders + 1
        for c in range(PIECES):

            @pl.when((c >= here) & (c < need))
            def _(c=c):
                pieces[c].wait()

        for u in range(GROUP):
            gather(first + u, u)
        found = []
        for u in range(GROUP):
            s = sender(first + u)
            p = tab_ref[R_OWN, s]
            found.append((s, p) + best_of(
                row, col, tab_ref[R_LIN, s], lens_ref[p], buf[u].reshape(N, width), own_t_ref[p]
            ))
        ret = ret_ref[...]
        for s, p, own_best, in_best in found:
            best_ref[pl.ds(p, 1), :] = jnp.maximum(best_ref[pl.ds(p, 1), :], own_best)
            ret = jnp.where(col == s, in_best, ret)
        ret_ref[...] = ret
        return jnp.maximum(here, need)

    here = lax.fori_loop(0, (count + GROUP - 1) // GROUP, body, jnp.int32(0))
    for c in range(PIECES):

        @pl.when(c >= here)
        def _(c=c):
            pieces[c].wait()

    if late:
        ret_ref[...] = ret_ref[...].T


def near(late, tab, loc, lens, own_t, best, ret, *gots):
    total = sum(got.shape[0] for got in gots)
    far = [pltpu.with_memory_space_constraint(x, pltpu.HBM) for x in (own_t,) + gots]
    return pl.pallas_call(
        functools.partial(near_kernel, late),
        out_shape=[jax.ShapeDtypeStruct(x.shape, x.dtype) for x in (best, ret)],
        in_specs=[pl.BlockSpec(memory_space=pltpu.SMEM)] * 3
        + [pl.BlockSpec(memory_space=pltpu.HBM)]
        + [pl.BlockSpec(memory_space=pltpu.VMEM)] * 2
        + [pl.BlockSpec(memory_space=pltpu.HBM)] * len(gots),
        out_specs=[pl.BlockSpec(memory_space=pltpu.VMEM)] * 2,
        scratch_shapes=[
            pltpu.VMEM(own_t.shape, own_t.dtype),
            pltpu.VMEM((total,) + gots[0].shape[1:], own_t.dtype),
            pltpu.VMEM((GROUP, GR, 16, own_t.shape[1]), own_t.dtype),
            pltpu.SemaphoreType.DMA((len(gots),)),
            pltpu.SemaphoreType.DMA((PIECES,)),
        ],
        compiler_params=pltpu.CompilerParams(vmem_limit_bytes=44 << 20),
        name="near_late" if late else "near_early",
    )(tab, loc, lens, far[0], best, ret, *far[1:])


def centred(score_matrix, row_validity_mask, col_mask):
    row_count = jnp.sum(row_validity_mask, -1)
    col_count = jnp.sum(col_mask, -1)
    row_mean = jnp.sum(score_matrix * col_mask[..., None, :], -1) / col_count[..., None]
    col_mean = jnp.sum(score_matrix * row_validity_mask[..., :, None], -2) / row_count[..., None]
    grand_mean = jnp.sum(row_mean * row_validity_mask, -1) / row_count
    return (
        score_matrix - row_mean[..., :, None] - col_mean[..., None, :] + grand_mean[..., None, None]
    )


def within_cluster(embeddings, masks):
    proteins_here, slots, width = embeddings.shape
    inverse_square_root = 1.0 / jnp.sqrt(jnp.float32(width))
    block_size = 8
    block_count = proteins_here // block_size

    def one_block(block_start):
        block_rows = lax.dynamic_slice_in_dim(embeddings, block_start, block_size, 0)
        block_mask = lax.dynamic_slice_in_dim(masks, block_start, block_size, 0)
        score_matrix = (
            jnp.einsum("bie,qje->bqij", block_rows, embeddings, preferred_element_type=jnp.float32)
            * inverse_square_root
        )
        cent = centred(score_matrix, block_mask[:, None, :], masks[None, :, :])
        row_max = jnp.max(jnp.where(masks[None, :, None, :] > 0, cent, lowest), -1)
        self_pair = (block_start + jnp.arange(block_size))[:, None] == jnp.arange(proteins_here)[
            None, :
        ]
        row_max = jnp.where(self_pair[:, :, None], lowest, row_max)
        best_match = jnp.max(row_max, 1)
        return jnp.where(block_mask > 0, best_match, 0.0)

    start_offsets = jnp.arange(block_count) * block_size
    return lax.map(one_block, start_offsets).reshape(proteins_here, slots)


def exchange(x):
    return lax.all_to_all(x, "shard", split_axis=0, concat_axis=0, tiled=True)


def other_core(x):
    return lax.ppermute(x, "shard", [(d, d ^ 1) for d in range(N)])


def per_device(embeddings, lengths, requests, query_local):
    proteins_here, slots, width = embeddings.shape
    masks = (jnp.arange(slots)[None, :] < lengths[:, None]).astype(jnp.float32)
    me = lax.axis_index("shard").astype(jnp.int32)[None]
    plan = jnp.concatenate([requests, query_local, lengths[None, :]], 1)
    plan = jnp.pad(plan, ((0, 0), (0, 3 * N - plan.shape[1])))
    plan = exchange(jnp.broadcast_to(plan, (N, 3 * N)))
    own = embeddings.reshape(proteins_here * GR, 16, width)

    mate = other_core(own)
    none_own = jnp.full((proteins_here, slots), lowest, jnp.float32)
    none_in = jnp.full((N, slots), lowest, jnp.float32)

    def finish(tab, best, ret, local_best):
        returned = exchange(ret)
        mine = (tab[R_SEND][None, :] == jnp.arange(proteins_here)[:, None]) & (tab[R_GOUT] > 0)[None, :]
        from_ret = jnp.max(jnp.where(mine[:, :, None], returned[None, :, :], lowest), 1)
        best = jnp.maximum(from_ret, best)
        cross_best = jnp.where((masks > 0) & (best > -1e29), best, 0.0)
        return local_best, cross_best

    def packed(c2, tab):
        loc = place(c2, me, tab)
        got1 = exchange(pack1(tab, own, mate))
        local_best = within_cluster(embeddings, masks)
        rows, local_best = lax.optimization_barrier((embeddings, local_best))
        own_t = jnp.swapaxes(rows, 1, 2)
        got1, local_best, own_t = lax.optimization_barrier((got1, local_best, own_t))
        send2 = pack2(c2, tab, own, mate, got1)
        send2, got1 = lax.optimization_barrier((send2, got1))
        got2 = exchange(send2)
        handed = other_core(hand(tab, got1))
        best, ret = near(False, tab, loc, lengths, own_t, none_own, none_in, got1)
        best, ret, got2 = lax.optimization_barrier((best, ret, got2))
        best, ret = near(True, tab, loc, lengths, own_t, best, ret, got1, got2, handed)
        return finish(tab, best, ret, local_best)

    def whole(tab):
        loc = place(0, me, tab)
        got = exchange(pack_whole(tab, own))
        own_t = jnp.swapaxes(embeddings, 1, 2)
        local_best = within_cluster(embeddings, masks)
        best, ret = match(False, tab, loc, lengths, own_t, none_own, none_in, got)
        best, ret = match(True, tab, loc, lengths, own_t, best, ret, got)
        return finish(tab, best, ret, local_best)

    def second(_):
        tab, left = route(2, me, plan)
        return lax.cond(left[0] == 0, functools.partial(packed, 2), whole, tab)

    tab, left = route(1, me, plan)
    return lax.cond(left[0] == 0, functools.partial(packed, 1), second, tab)


def solution(mesh):
    placed = (P("shard", None, None), P("shard"), P("shard", None), P("shard", None))
    return jax.shard_map(
        per_device,
        mesh=mesh,
        in_specs=placed,
        out_specs=(P("shard", None), P("shard", None)),
        check_vma=False,
    )
```

```python
import functools

import jax
import jax.numpy as jnp
from jax import lax
from jax.experimental import pallas as pl
from jax.experimental.pallas import tpu as pltpu
from jax.sharding import PartitionSpec as P

lowest = -1e30
N = 128
GR = 8
C1 = 2
K = 64
DEPTH = 16
GROUP = 8
PIECES = 4
TRIES = 6
FEW = 32

R_F1ROW, R_F1COL, R_F1COLM, R_F2ROW, R_F2COL, R_SEND, R_SENDM, R_GIN, R_LIN, R_OWN, R_GOUT = range(11)


def swap_rows(x, s):
    return jnp.where((s & 1) == 0, pltpu.roll(x, N - 1, 0), pltpu.roll(x, 1, 0))


def swap_cols(x, r):
    return jnp.where((r & 1) == 0, pltpu.roll(x, N - 1, 1), pltpu.roll(x, 1, 1))


def skew(x, by, axis, sign):
    for b in range(7):
        shift = (1 << b) if sign > 0 else N - (1 << b)
        x = jnp.where(((by >> b) & 1) == 1, pltpu.roll(x, shift, axis), x)
    return x


def before(x, s):
    total = x
    for b in range(7):
        total = total + jnp.where(s >= (1 << b), pltpu.roll(total, 1 << b, 0), 0)
    return total - x


def route_kernel(c2, me_ref, plan_ref, tab_ref, left_ref, tmp_ref, first_ref):
    s = lax.broadcasted_iota(jnp.int32, (N, N), 0)
    r = lax.broadcasted_iota(jnp.int32, (N, N), 1)
    req = plan_ref[:, :N]
    q = plan_ref[:, N : 2 * N]
    lens = plan_ref[:, 2 * N :]
    lens_t = lens.T
    live = (req >= 0).astype(jnp.int32)
    req = jnp.maximum(req, 0)
    la = jnp.zeros((N, N), jnp.int32)
    lb = jnp.zeros((N, N), jnp.int32)
    for p in range(16):
        la = jnp.where(q == p, lens[:, p : p + 1], la)
        lb = jnp.where(req == p, lens_t[p : p + 1, :], lb)
    la = la * live
    lb = lb * live
    la_t = la.T
    lb_t = lb.T
    req_t = req.T
    ga = (la + 15) >> 4
    gb = (lb + 15) >> 4
    ga_t = (la_t + 15) >> 4
    gb_t = (lb_t + 15) >> 4
    anti = live - (lb_t > 0).astype(jnp.int32)
    base = 1000 * (gb + gb_t - ga - ga_t) + jnp.where(((s + r) & 1) == 0, 250, -250)
    score = base
    bias_col = jnp.zeros((N, 1), jnp.int32)
    bias_row = jnp.zeros((1, N), jnp.int32)
    for eta in (10, 6, 4):
        gets = score < 0
        net = jnp.where(gets, gb_t, ga) - jnp.where(gets, gb, ga_t)
        bias_row = bias_row + eta * jnp.sum(net, axis=0, keepdims=True)
        bias_col = bias_col - eta * jnp.sum(net, axis=1, keepdims=True)
        score = base + anti * (bias_col - bias_row)
    lister_gets = score < 0
    lin = jnp.where(lister_gets, lb_t, la)
    lin_t = jnp.where(lister_gets, lb, la_t)
    psend = jnp.where(lister_gets, req_t, q)
    pown_t = jnp.where(lister_gets, q, req_t)
    m_tot = (lin + 15) >> 4

    diag = s == r
    free1 = jnp.where(diag, 0, C1)
    n = jnp.minimum(m_tot, free1)
    rem = m_tot - n
    w1 = free1 - n
    for k in range(C1):
        w1 = w1 | jnp.where(k < n, ((r << 3) | k) << (2 + 12 * k), 0)
    m_swap = swap_rows(m_tot, s)
    rem_s = swap_rows(rem, s)
    used = C1 - (w1 & 3)
    n = jnp.where(diag, 0, jnp.minimum(rem_s, w1 & 3))
    w1 = w1 - n
    for k in range(C1):
        code = (1 << 11) | (r << 3) | (m_swap - rem_s + k - used)
        w1 = w1 | jnp.where((k >= used) & (k < used + n), code << (2 + 12 * k), 0)
    rem = swap_rows(rem_s - n, s)
    free2 = jnp.where(diag, 0, c2)
    g_from = m_tot - rem
    n = jnp.minimum(rem, free2)
    rem = rem - n
    w2 = free2 - n
    for k in range(c2):
        w2 = w2 | jnp.where(k < n, ((g_from + k) << 2) << (2 + 14 * k), 0)
    rem_s = swap_rows(rem, s)
    used = c2 - (w2 & 3)
    n = jnp.where(diag, 0, jnp.minimum(rem_s, w2 & 3))
    w2 = w2 - n
    for k in range(c2):
        code = 1 | ((m_swap - rem_s + k - used) << 2)
        w2 = w2 | jnp.where((k >= used) & (k < used + n), code << (2 + 14 * k), 0)
    rem = swap_rows(rem_s - n, s)
    rem_c = swap_cols(rem, r)
    g_from = swap_cols(m_tot, r) - rem_c
    used = C1 - (w1 & 3)
    n = jnp.where(diag, 0, jnp.minimum(rem_c, w1 & 3))
    n = jnp.maximum(jnp.minimum(n, K - before(n, s)), 0)
    w1 = w1 - n
    for k in range(C1):
        code = (1 << 10) | ((r ^ 1) << 3) | (g_from + k - used)
        w1 = w1 | jnp.where((k >= used) & (k < used + n), code << (2 + 12 * k), 0)
    rem = swap_cols(rem_c - n, r)

    w1 = skew(w1, s, 1, -1)
    w2 = skew(w2, r, 0, -1)

    last = m_tot - 1
    kept2 = ((s << 6) | 2) << 2

    def step(limit, w1, w2, g):
        f1 = w1 & 3
        f2 = w2 & 3
        ok = (jnp.minimum(f1, f2) > 0) & (g <= limit)
        first = f1 == C1
        at = g << 2
        code1 = (r << 5) | at
        w1_new = w1 + jnp.where(first, code1, code1 << 12) - 1
        code2 = kept2 + (at << 2) + jnp.where(first, 0, 1 << 7)
        if c2 > 1:
            code2 = jnp.where(f2 == c2, code2, code2 << 14)
        w2_new = w2 + code2 - 1
        w1 = jnp.where(ok, w1_new, w1)
        w2 = jnp.where(ok, w2_new, w2)
        g = jnp.where(ok, g + 1, g)
        return pltpu.roll(w1, N - 1, 1), pltpu.roll(w2, N - 1, 0), g

    first_ref[0] = w1
    first_ref[1] = w2
    first_ref[2] = m_tot - rem

    def sweep(limit, turns, w1, w2, g):
        def body(c):
            i, _, w1, w2, g = c
            for _ in range(8):
                w1, w2, g = step(limit, w1, w2, g)
            return i + 1, jnp.max(limit - g), w1, w2, g

        i, most, w1, w2, g = lax.while_loop(
            lambda c: (c[0] < N // 8) & (c[1] >= 0),
            body,
            (jnp.int32(0), jnp.max(limit - g), w1, w2, g),
        )
        return most, turns + 8 * i, w1, w2, g

    def attempt(c):
        tries, _, _, _, _, urgent = c
        limit = jnp.where(urgent > 0, last, -1)
        _, turns, w1, w2, g = sweep(limit, 0, first_ref[0], first_ref[1], first_ref[2])
        _, turns, w1, w2, g = sweep(last, turns, w1, w2, g)
        late = (g <= last).astype(jnp.int32)
        return tries + 1, jnp.sum(late), turns, w1, w2, jnp.maximum(late, urgent)

    _, left, turns, w1, w2, _ = lax.while_loop(
        lambda c: (c[0] < TRIES) & (c[1] > 0) & (c[1] <= FEW),
        attempt,
        (jnp.int32(0), jnp.int32(1), jnp.int32(0), w1, w2, jnp.zeros((N, N), jnp.int32)),
    )
    turns = turns & (N - 1)
    w1 = skew(pltpu.roll(w1, turns, 1), s, 1, 1)
    w2 = skew(pltpu.roll(w2, turns, 0), r, 0, 1)

    me = me_ref[0]
    mate = me ^ 1

    def put(x, *rows):
        tmp_ref[...] = x
        for row, at in rows:
            tab_ref[row : row + 1, :] = tmp_ref[pl.ds(at, 1), :]

    put(w1, (R_F1ROW, me))
    put(w1.T, (R_F1COL, me), (R_F1COLM, mate))
    put(w2, (R_F2ROW, me))
    put(w2.T, (R_F2COL, me))
    put(psend, (R_SEND, me), (R_SENDM, mate))
    put((lin_t + 15) >> 4, (R_GIN, me))
    put(lin_t, (R_LIN, me))
    put(pown_t, (R_OWN, me))
    left_ref[0] = left
    put(m_tot, (R_GOUT, me))
    tab_ref[R_GOUT + 1 :, :] = jnp.zeros((16 - R_GOUT - 1, N), jnp.int32)


def route(c2, me, plan):
    return pl.pallas_call(
        functools.partial(route_kernel, c2),
        out_shape=[jax.ShapeDtypeStruct((16, N), jnp.int32), jax.ShapeDtypeStruct((1,), jnp.int32)],
        in_specs=[pl.BlockSpec(memory_space=pltpu.SMEM), pl.BlockSpec(memory_space=pltpu.VMEM)],
        out_specs=[pl.BlockSpec(memory_space=pltpu.VMEM), pl.BlockSpec(memory_space=pltpu.SMEM)],
        scratch_shapes=[pltpu.VMEM((N, N), jnp.int32), pltpu.VMEM((3, N, N), jnp.int32)],
        compiler_params=pltpu.CompilerParams(vmem_limit_bytes=32 << 20),
        name=f"route{c2}",
    )(me, plan)


def pack1_kernel(tab_ref, own_ref, mate_ref, out_ref, both, buf, in_sem, out_sem):
    parts = out_sem.shape[0]
    each = N // parts
    held = own_ref.shape[0]

    def piece(ref, part):
        return ref.at[pl.ds(part * each * C1, each * C1)]

    copies = [
        pltpu.make_async_copy(ref, both.at[pl.ds(i * held, held)], in_sem.at[i])
        for i, ref in enumerate((own_ref, mate_ref))
    ]
    for copy in copies:
        copy.start()
    for copy in copies:
        copy.wait()
    for part in range(parts):

        def body(j, _):
            w = tab_ref[R_F1ROW, j]
            for k in range(C1):
                code = w >> (2 + 12 * k)
                core = (code >> 11) & 1
                protein = tab_ref[R_SEND + core, (code >> 3) & (N - 1)]
                buf[j * C1 + k] = both[core * held + protein * GR + (code & 7)]
            return 0

        lax.fori_loop(part * each, (part + 1) * each, body, 0, unroll=8)
        pltpu.make_async_copy(piece(buf, part), piece(out_ref, part), out_sem.at[part]).start()
    for part in range(parts):
        pltpu.make_async_copy(piece(buf, part), piece(out_ref, part), out_sem.at[part]).wait()


def pack1(tab, own, mate):
    parts = 8
    shape = (N * C1,) + own.shape[1:]
    return pl.pallas_call(
        pack1_kernel,
        out_shape=pltpu.HBM(shape, own.dtype),
        in_specs=[pl.BlockSpec(memory_space=pltpu.SMEM)] + [pl.BlockSpec(memory_space=pltpu.HBM)] * 2,
        out_specs=pl.BlockSpec(memory_space=pltpu.HBM),
        scratch_shapes=[
            pltpu.VMEM((2 * own.shape[0],) + own.shape[1:], own.dtype),
            pltpu.VMEM(shape, own.dtype),
            pltpu.SemaphoreType.DMA((2,)),
            pltpu.SemaphoreType.DMA((parts,)),
        ],
        compiler_params=pltpu.CompilerParams(vmem_limit_bytes=40 << 20),
        name="pack1",
    )(tab, *(pltpu.with_memory_space_constraint(x, pltpu.HBM) for x in (own, mate)))


def pack2_kernel(c2, tab_ref, own_ref, mate_ref, got_ref, out_ref, buf, in_sem, out_sem):
    parts = in_sem.shape[0]
    each = N // parts

    def fetch(part):
        def body(j, count):
            to = part * each + j
            w = tab_ref[R_F2ROW, to]
            filled = c2 - (w & 3)
            for k in range(c2):
                code = w >> (2 + 14 * k)
                kind = code & 3
                g = (code >> 2) & 7
                slot = ((code >> 6) & (N - 1)) * C1 + ((code >> 5) & 1)
                dst = buf.at[to * c2 + k]

                @pl.when((k < filled) & (kind == 0))
                def _():
                    src = own_ref.at[tab_ref[R_SEND, to] * GR + g]
                    pltpu.make_async_copy(src, dst, in_sem.at[part]).start()

                @pl.when((k < filled) & (kind == 1))
                def _():
                    src = mate_ref.at[tab_ref[R_SENDM, to] * GR + g]
                    pltpu.make_async_copy(src, dst, in_sem.at[part]).start()

                @pl.when((k < filled) & (kind >= 2))
                def _():
                    pltpu.make_async_copy(got_ref.at[slot], dst, in_sem.at[part]).start()

            return count + filled

        return lax.fori_loop(0, each, body, jnp.int32(0), unroll=4)

    def piece(ref, part):
        return ref.at[pl.ds(part * each * c2, each * c2)]

    counts = [fetch(part) for part in range(parts)]
    for part in range(parts):

        def arrive(i, _, part=part):
            pltpu.make_async_copy(own_ref.at[0], buf.at[0], in_sem.at[part]).wait()
            return 0

        lax.fori_loop(0, counts[part], arrive, 0)
        pltpu.make_async_copy(piece(buf, part), piece(out_ref, part), out_sem.at[part]).start()
    for part in range(parts):
        pltpu.make_async_copy(piece(buf, part), piece(out_ref, part), out_sem.at[part]).wait()


def pack2(c2, tab, own, mate, got):
    parts = 4
    shape = (N * c2,) + own.shape[1:]
    return pl.pallas_call(
        functools.partial(pack2_kernel, c2),
        out_shape=pltpu.HBM(shape, own.dtype),
        in_specs=[pl.BlockSpec(memory_space=pltpu.SMEM)] + [pl.BlockSpec(memory_space=pltpu.HBM)] * 3,
        out_specs=pl.BlockSpec(memory_space=pltpu.HBM),
        scratch_shapes=[
            pltpu.VMEM(shape, own.dtype),
            pltpu.SemaphoreType.DMA((parts,)),
            pltpu.SemaphoreType.DMA((parts,)),
        ],
        compiler_params=pltpu.CompilerParams(vmem_limit_bytes=40 << 20),
        name="pack2",
    )(tab, *(pltpu.with_memory_space_constraint(x, pltpu.HBM) for x in (own, mate, got)))


def hand_kernel(tab_ref, got_ref, out_ref, sem):
    def body(s, count):
        w = tab_ref[R_F1COL, s]
        for k in range(C1):
            mine = (w >> (2 + 12 * k + 10)) & 1

            @pl.when(mine == 1)
            def _():
                pltpu.make_async_copy(got_ref.at[s * C1 + k], out_ref.at[count], sem).start()

            count = count + mine
        return count

    count = lax.fori_loop(0, N, body, jnp.int32(0))

    def fill(j, _):
        pltpu.make_async_copy(got_ref.at[0], out_ref.at[j], sem).start()
        return 0

    lax.fori_loop(count, K, fill, 0)
    pltpu.make_async_copy(out_ref, out_ref, sem).wait()


def hand(tab, got):
    return pl.pallas_call(
        hand_kernel,
        out_shape=jax.ShapeDtypeStruct((K,) + got.shape[1:], got.dtype),
        in_specs=[pl.BlockSpec(memory_space=pltpu.SMEM), pl.BlockSpec(memory_space=pltpu.HBM)],
        out_specs=pl.BlockSpec(memory_space=pltpu.VMEM),
        scratch_shapes=[pltpu.SemaphoreType.DMA],
        compiler_params=pltpu.CompilerParams(vmem_limit_bytes=40 << 20),
        name="hand",
    )(tab, got)


def pack_whole_kernel(tab_ref, own_ref, out_ref):
    out_ref[...] = own_ref[...]


def pack_whole(tab, own):
    block = (GR,) + own.shape[1:]
    return pl.pallas_call(
        pack_whole_kernel,
        grid_spec=pltpu.PrefetchScalarGridSpec(
            num_scalar_prefetch=1,
            grid=(N,),
            in_specs=[pl.BlockSpec(block, lambda i, tab: (tab[R_SEND, i], 0, 0))],
            out_specs=pl.BlockSpec(block, lambda i, tab: (i, 0, 0)),
        ),
        out_shape=jax.ShapeDtypeStruct((N * GR,) + own.shape[1:], own.dtype),
        name="pack_whole",
    )(tab, own)


def place_kernel(c2, me_ref, tab_ref, loc_ref):
    me = me_ref[0]
    order, counts, late_of = N * GR, N * GR + N, N * GR + 2 * N

    def clear(s, _):
        loc_ref[late_of + s] = 0
        for g in range(GR):
            loc_ref[s * GR + g] = s * GR + g if c2 == 0 else 0
        return 0

    lax.fori_loop(0, N, clear, 0)

    def find(s, handed):
        w = tab_ref[R_F1COL, s]
        filled = C1 - (w & 3)
        for k in range(C1):
            code = w >> (2 + 12 * k)

            @pl.when((k < filled) & (((code >> 3) & 0xFF) == me) & (s != me))
            def _():
                loc_ref[(s ^ ((code >> 11) & 1)) * GR + (code & 7)] = s * C1 + k

        w = tab_ref[R_F1COLM, s]
        for k in range(C1):
            code = w >> (2 + 12 * k)
            handed_here = (code >> 10) & 1

            @pl.when(handed_here == 1)
            def _():
                loc_ref[s * GR + (code & 7)] = (C1 + c2) * N + handed
                loc_ref[late_of + s] = 1

            handed = handed + handed_here

        w = tab_ref[R_F2COL, s]
        filled = c2 - (w & 3)
        for k in range(c2):
            code = w >> (2 + 14 * k)
            kind = code & 3
            origin = jnp.where(kind >= 2, (code >> 6) & (N - 1), s ^ (kind & 1))

            @pl.when((k < filled) & (s != me))
            def _():
                loc_ref[origin * GR + ((code >> 2) & 7)] = C1 * N + s * c2 + k
                loc_ref[late_of + origin] = 1

        return handed

    if c2 > 0:
        lax.fori_loop(0, N, find, jnp.int32(0))

    def sort(s, c):
        early, late = c
        is_live = (tab_ref[R_GIN, s] > 0).astype(jnp.int32)
        is_late = loc_ref[late_of + s]

        @pl.when(is_live == 1)
        def _():
            loc_ref[order + jnp.where(is_late == 1, N - 1 - late, early)] = s

        return early + is_live * (1 - is_late), late + is_live * is_late

    early, late = lax.fori_loop(0, N, sort, (jnp.int32(0), jnp.int32(0)))
    loc_ref[counts] = early
    loc_ref[counts + 1] = late


def place(c2, me, tab):
    return pl.pallas_call(
        functools.partial(place_kernel, c2),
        out_shape=jax.ShapeDtypeStruct((N * GR + 3 * N,), jnp.int32),
        in_specs=[pl.BlockSpec(memory_space=pltpu.SMEM)] * 2,
        out_specs=pl.BlockSpec(memory_space=pltpu.SMEM),
        name="place",
    )(me, tab)


def best_of(row, col, len_in, len_own, incoming, own_t):
    scale = 1.0 / jnp.sqrt(jnp.float32(own_t.shape[0]))
    score = jnp.dot(incoming, own_t, preferred_element_type=jnp.float32) * scale
    in_count = len_in.astype(jnp.float32)
    real_in = row < len_in
    real_own = col < len_own
    over_own = jnp.sum(jnp.where(real_own, score, 0.0), 1, keepdims=True) / len_own.astype(jnp.float32)
    over_in = jnp.sum(jnp.where(real_in, score, 0.0), 0, keepdims=True) / in_count
    grand = jnp.sum(jnp.where(real_in[:, :1], over_own, 0.0), 0, keepdims=True) / in_count
    own_best = jnp.max(jnp.where(real_in, score - over_own, lowest), 0, keepdims=True) - over_in + grand
    in_best = jnp.max(jnp.where(real_own, score - over_in, lowest), 1, keepdims=True) - over_own + grand
    return own_best, in_best


def match_kernel(late, ends, tab_ref, loc_ref, lens_ref, own_t_ref, best0_ref, ret0_ref, *refs):
    gots, (best_ref, ret_ref, buf, sem) = refs[: len(ends)], refs[len(ends) :]
    width = own_t_ref.shape[1]
    best_ref[...] = best0_ref[...]
    ret_ref[...] = ret0_ref[...]
    count = loc_ref[N * GR + N + int(late)]

    def sender(i):
        return loc_ref[N * GR + (N - 1 - i if late else i)]

    def fetch(i):
        @pl.when(i < count)
        def _():
            s = sender(i)
            slot = i & (DEPTH - 1)
            granules = tab_ref[R_GIN, s]
            for g in range(GR):

                @pl.when(g < granules)
                def _():
                    at = loc_ref[s * GR + g]
                    start = 0
                    for got_ref, end in zip(gots, ends):

                        @pl.when((at >= start) & (at < end))
                        def _(got_ref=got_ref, start=start):
                            pltpu.make_async_copy(
                                got_ref.at[at - start], buf.at[slot, g], sem.at[slot, g]
                            ).start()

                        start = end

    def arrive(i):
        @pl.when(i < count)
        def _():
            s = sender(i)
            slot = i & (DEPTH - 1)
            granules = tab_ref[R_GIN, s]
            for g in range(GR):

                @pl.when(g < granules)
                def _():
                    pltpu.make_async_copy(gots[0].at[0], buf.at[slot, g], sem.at[slot, g]).wait()

    for i in range(DEPTH - GROUP):
        fetch(i)
    row = lax.broadcasted_iota(jnp.int32, (N, N), 0)
    col = lax.broadcasted_iota(jnp.int32, (N, N), 1)

    def body(j, _):
        first = j * GROUP
        for u in range(GROUP):
            fetch(first + u + DEPTH - GROUP)
        for u in range(GROUP):
            arrive(first + u)
        found = []
        for u in range(GROUP):
            i = jnp.minimum(first + u, count - 1)
            s = sender(i)
            p = tab_ref[R_OWN, s]
            incoming = buf[i & (DEPTH - 1)].reshape(N, width)
            found.append((s, p) + best_of(
                row, col, tab_ref[R_LIN, s], lens_ref[p], incoming, own_t_ref[p]
            ))
        ret = ret_ref[...]
        for s, p, own_best, in_best in found:
            best_ref[pl.ds(p, 1), :] = jnp.maximum(best_ref[pl.ds(p, 1), :], own_best)
            ret = jnp.where(col == s, in_best, ret)
        ret_ref[...] = ret
        return 0

    lax.fori_loop(0, (count + GROUP - 1) // GROUP, body, 0)
    if late:
        ret_ref[...] = ret_ref[...].T


def match(late, tab, loc, lens, own_t, best, ret, *gots):
    ends = []
    for got in gots:
        ends.append((ends[-1] if ends else 0) + got.shape[0])
    return pl.pallas_call(
        functools.partial(match_kernel, late, tuple(ends)),
        out_shape=[jax.ShapeDtypeStruct(x.shape, x.dtype) for x in (best, ret)],
        in_specs=[pl.BlockSpec(memory_space=pltpu.SMEM)] * 3
        + [pl.BlockSpec(memory_space=pltpu.VMEM)] * 3
        + [pl.BlockSpec(memory_space=pltpu.HBM)] * len(gots),
        out_specs=[pl.BlockSpec(memory_space=pltpu.VMEM)] * 2,
        scratch_shapes=[
            pltpu.VMEM((DEPTH, GR, 16, own_t.shape[1]), own_t.dtype),
            pltpu.SemaphoreType.DMA((DEPTH, GR)),
        ],
        compiler_params=pltpu.CompilerParams(vmem_limit_bytes=40 << 20),
        name="match_late" if late else "match_early",
    )(tab, loc, lens, own_t, best, ret, *gots)


def near_kernel(late, tab_ref, loc_ref, lens_ref, own_t_hbm, best0_ref, ret0_ref, *refs):
    gots, (best_ref, ret_ref, own_t_ref, all_ref, buf, sem, piece_sem) = refs[:-7], refs[-7:]
    copies = [pltpu.make_async_copy(own_t_hbm, own_t_ref, sem.at[0])]
    start = gots[0].shape[0]
    for i, got in enumerate(gots[1:]):
        end = start + got.shape[0]
        copies.append(pltpu.make_async_copy(got, all_ref.at[pl.ds(start, end - start)], sem.at[i + 1]))
        start = end
    senders = N // PIECES
    rows = senders * C1
    pieces = [
        pltpu.make_async_copy(
            gots[0].at[pl.ds(c * rows, rows)], all_ref.at[pl.ds(c * rows, rows)], piece_sem.at[c]
        )
        for c in range(PIECES)
    ]
    for copy in copies + pieces:
        copy.start()
    width = own_t_ref.shape[1]
    best_ref[...] = best0_ref[...]
    ret_ref[...] = ret0_ref[...]
    count = loc_ref[N * GR + N + int(late)]

    def sender(i):
        i = jnp.minimum(i, count - 1)
        return loc_ref[N * GR + (N - 1 - i if late else i)]

    def gather(i, u):
        s = sender(i)
        for g in range(GR):
            buf[u, g] = all_ref[loc_ref[s * GR + g]]

    for copy in copies:
        copy.wait()
    row = lax.broadcasted_iota(jnp.int32, (N, N), 0)
    col = lax.broadcasted_iota(jnp.int32, (N, N), 1)

    def body(j, here):
        first = j * GROUP
        need = sender(first + GROUP - 1) // senders + 1
        for c in range(PIECES):

            @pl.when((c >= here) & (c < need))
            def _(c=c):
                pieces[c].wait()

        for u in range(GROUP):
            gather(first + u, u)
        found = []
        for u in range(GROUP):
            s = sender(first + u)
            p = tab_ref[R_OWN, s]
            found.append((s, p) + best_of(
                row, col, tab_ref[R_LIN, s], lens_ref[p], buf[u].reshape(N, width), own_t_ref[p]
            ))
        ret = ret_ref[...]
        for s, p, own_best, in_best in found:
            best_ref[pl.ds(p, 1), :] = jnp.maximum(best_ref[pl.ds(p, 1), :], own_best)
            ret = jnp.where(col == s, in_best, ret)
        ret_ref[...] = ret
        return jnp.maximum(here, need)

    here = lax.fori_loop(0, (count + GROUP - 1) // GROUP, body, jnp.int32(0))
    for c in range(PIECES):

        @pl.when(c >= here)
        def _(c=c):
            pieces[c].wait()

    if late:
        ret_ref[...] = ret_ref[...].T


def near(late, tab, loc, lens, own_t, best, ret, *gots):
    total = sum(got.shape[0] for got in gots)
    far = [pltpu.with_memory_space_constraint(x, pltpu.HBM) for x in (own_t,) + gots]
    return pl.pallas_call(
        functools.partial(near_kernel, late),
        out_shape=[jax.ShapeDtypeStruct(x.shape, x.dtype) for x in (best, ret)],
        in_specs=[pl.BlockSpec(memory_space=pltpu.SMEM)] * 3
        + [pl.BlockSpec(memory_space=pltpu.HBM)]
        + [pl.BlockSpec(memory_space=pltpu.VMEM)] * 2
        + [pl.BlockSpec(memory_space=pltpu.HBM)] * len(gots),
        out_specs=[pl.BlockSpec(memory_space=pltpu.VMEM)] * 2,
        scratch_shapes=[
            pltpu.VMEM(own_t.shape, own_t.dtype),
            pltpu.VMEM((total,) + gots[0].shape[1:], own_t.dtype),
            pltpu.VMEM((GROUP, GR, 16, own_t.shape[1]), own_t.dtype),
            pltpu.SemaphoreType.DMA((len(gots),)),
            pltpu.SemaphoreType.DMA((PIECES,)),
        ],
        compiler_params=pltpu.CompilerParams(vmem_limit_bytes=44 << 20),
        name="near_late" if late else "near_early",
    )(tab, loc, lens, far[0], best, ret, *far[1:])


def centred(score_matrix, row_validity_mask, col_mask):
    row_count = jnp.sum(row_validity_mask, -1)
    col_count = jnp.sum(col_mask, -1)
    row_mean = jnp.sum(score_matrix * col_mask[..., None, :], -1) / col_count[..., None]
    col_mean = jnp.sum(score_matrix * row_validity_mask[..., :, None], -2) / row_count[..., None]
    grand_mean = jnp.sum(row_mean * row_validity_mask, -1) / row_count
    return (
        score_matrix - row_mean[..., :, None] - col_mean[..., None, :] + grand_mean[..., None, None]
    )


def within_cluster(embeddings, masks):
    proteins_here, slots, width = embeddings.shape
    inverse_square_root = 1.0 / jnp.sqrt(jnp.float32(width))
    block_size = 8
    block_count = proteins_here // block_size

    def one_block(block_start):
        block_rows = lax.dynamic_slice_in_dim(embeddings, block_start, block_size, 0)
        block_mask = lax.dynamic_slice_in_dim(masks, block_start, block_size, 0)
        score_matrix = (
            jnp.einsum("bie,qje->bqij", block_rows, embeddings, preferred_element_type=jnp.float32)
            * inverse_square_root
        )
        cent = centred(score_matrix, block_mask[:, None, :], masks[None, :, :])
        row_max = jnp.max(jnp.where(masks[None, :, None, :] > 0, cent, lowest), -1)
        self_pair = (block_start + jnp.arange(block_size))[:, None] == jnp.arange(proteins_here)[
            None, :
        ]
        row_max = jnp.where(self_pair[:, :, None], lowest, row_max)
        best_match = jnp.max(row_max, 1)
        return jnp.where(block_mask > 0, best_match, 0.0)

    start_offsets = jnp.arange(block_count) * block_size
    return lax.map(one_block, start_offsets).reshape(proteins_here, slots)


def exchange(x):
    return lax.all_to_all(x, "shard", split_axis=0, concat_axis=0, tiled=True)


def other_core(x):
    return lax.ppermute(x, "shard", [(d, d ^ 1) for d in range(N)])


def per_device(embeddings, lengths, requests, query_local):
    proteins_here, slots, width = embeddings.shape
    masks = (jnp.arange(slots)[None, :] < lengths[:, None]).astype(jnp.float32)
    me = lax.axis_index("shard").astype(jnp.int32)[None]
    plan = jnp.concatenate([requests, query_local, lengths[None, :]], 1)
    plan = jnp.pad(plan, ((0, 0), (0, 3 * N - plan.shape[1])))
    plan = exchange(jnp.broadcast_to(plan, (N, 3 * N)))
    own = embeddings.reshape(proteins_here * GR, 16, width)

    mate = other_core(own)
    none_own = jnp.full((proteins_here, slots), lowest, jnp.float32)
    none_in = jnp.full((N, slots), lowest, jnp.float32)

    def finish(tab, best, ret, local_best):
        returned = exchange(ret)
        mine = (tab[R_SEND][None, :] == jnp.arange(proteins_here)[:, None]) & (tab[R_GOUT] > 0)[None, :]
        from_ret = jnp.max(jnp.where(mine[:, :, None], returned[None, :, :], lowest), 1)
        best = jnp.maximum(from_ret, best)
        cross_best = jnp.where((masks > 0) & (best > -1e29), best, 0.0)
        return local_best, cross_best

    def packed(c2, tab):
        loc = place(c2, me, tab)
        got1 = exchange(pack1(tab, own, mate))
        local_best = within_cluster(embeddings, masks)
        rows, local_best = lax.optimization_barrier((embeddings, local_best))
        own_t = jnp.swapaxes(rows, 1, 2)
        got1, local_best, own_t = lax.optimization_barrier((got1, local_best, own_t))
        send2 = pack2(c2, tab, own, mate, got1)
        send2, got1 = lax.optimization_barrier((send2, got1))
        got2 = exchange(send2)
        handed = other_core(hand(tab, got1))
        best, ret = near(False, tab, loc, lengths, own_t, none_own, none_in, got1)
        best, ret, got2 = lax.optimization_barrier((best, ret, got2))
        best, ret = near(True, tab, loc, lengths, own_t, best, ret, got1, got2, handed)
        return finish(tab, best, ret, local_best)

    def whole(tab):
        loc = place(0, me, tab)
        got = exchange(pack_whole(tab, own))
        own_t = jnp.swapaxes(embeddings, 1, 2)
        local_best = within_cluster(embeddings, masks)
        best, ret = match(False, tab, loc, lengths, own_t, none_own, none_in, got)
        best, ret = match(True, tab, loc, lengths, own_t, best, ret, got)
        return finish(tab, best, ret, local_best)

    def second(_):
        tab, left = route(2, me, plan)
        return lax.cond(left[0] == 0, functools.partial(packed, 2), whole, tab)

    tab, left = route(1, me, plan)
    return lax.cond(left[0] == 0, functools.partial(packed, 1), second, tab)


def solution(mesh):
    placed = (P("shard", None, None), P("shard"), P("shard", None), P("shard", None))
    return jax.shard_map(
        per_device,
        mesh=mesh,
        in_specs=placed,
        out_specs=(P("shard", None), P("shard", None)),
        check_vma=False,
    )
```
